256 devices in a mesh: space: 16 (over y, z_lo, core), tm: 16 (over x, z_hi).
Axes of the slice: x: 4, y: 4, z: 8 (z_hi: 4, z_lo: 2; z = z_hi * 2 + z_lo), core: 2. Of those that a mesh axis runs over, the one named last changes fastest.
Arguments:
- probe_field: bfloat16 [16384, 4096], P('space', 'tm'), may hold values from -5 to 5
- kappa: float32 [16384], P('space'), may hold values from 0.1 to 1
- theta_space: float32 [64], P('tm'), may hold values from 0.3 to 1
- theta_time: float32 [64], P('tm'), may hold values from 0.2 to 0.8
- diag_blocks: bfloat16 [128, 128, 128], P('space'), may hold values from -0.05 to 1.05
- off_blocks: bfloat16 [128, 8, 128, 128], P('space'), may hold values from -0.375 to 0.375
- block_cols: int32 [128, 8], P('space'), may hold values from 0 to 11
- halo_needs: int32 [64], P('space'), may hold values from 0 to 7
- covariates: bfloat16 [524288, 256], P(('space', 'tm')), may hold values from -4 to 4
- obs_owner: int32 [524288, 1], P(('space', 'tm')), may hold values from 0 to 15; in each aligned block of 2048 rows (0 to 2047, 2048 to 4095, ...) at most 256 rows name the same one
- obs_cell: int32 [524288], P(('space', 'tm')), may hold values from 0 to 4095
- svc_coef: bfloat16 [16384, 256], P('space'), may hold values from -0.375 to 0.375
Outputs:
- solution: float32 [16384, 4096], P('space', 'tm')
- grads: float32 [2, 4096], P(None, 'tm')
The draws below stay inside these ranges and needn't reach their ends.
Inputs may be any that keep to these rules, and one draw needn't show every extreme that they name: `obs_owner`: in each aligned block of 2048 rows (the rows of one device) no owner is named by more than 256 rows, a bound that some block reaches.
All inputs are finite; a program needn't handle non-finite values.
Results may differ from the reference program's by a relative error of at most 0.0021.
Values may be sent and summed in bfloat16 or wider, within the bound.
A program may use at most 64 MiB of HBM per device.

```python
import math
import jax
import jax.numpy as jnp
import numpy as np
from jax import lax

NB_DEV = 8
BLOCK = 128
NNZ_OFF = 8
HALO_B = 2
T_DEV = 4
PROBES = 64
NCOV = 256
OBS_DEV = 2048
ITERS = 4
CAP = 256
NODES_DEV = 1024
NB = 128
NODES = 16384
NT = 64
OBS = 524288
NEEDS = 64
N_SPACE = 16
N_TM = 16


def draw_diag_blocks(key, part):
    shape = (NB, BLOCK, BLOCK)
    noise = jax.random.uniform(key, shape, jnp.float32, -0.04, 0.04)
    identity = jnp.eye(BLOCK, dtype=jnp.float32)[None, :, :]
    return (identity + noise).astype(jnp.bfloat16)


def plant(drawn, rng, smallest, top_value):
    place = [jax.random.randint(jax.random.fold_in(rng, axis), (), 0, length) for axis, length in enumerate(drawn.shape)]
    longest = drawn.shape.index(max(drawn.shape))
    beside = place[:longest] + [(place[longest] + 1) % drawn.shape[longest]] + place[longest + 1:]
    return drawn.at[tuple(place)].set(smallest).at[tuple(beside)].set(top_value)


def block_scale(rng, dims, cuts, smallest, high):
    factor_of = 1.0
    for dim, parts in cuts:
        steps = jax.random.uniform(jax.random.fold_in(jax.random.fold_in(rng, 6), dim), (parts,), jnp.float32, smallest / len(cuts), high / len(cuts))
        factor_of = factor_of * jnp.repeat(jnp.exp(steps), dims[dim] // parts).reshape((-1,) + (1,) * (len(dims) - 1 - dim))
    return factor_of


def routed_block(rng, own, number, rows, number_of, top, most, slope):
    ranking = jax.random.permutation(rng, number_of)
    crowded, common = shares(number_of, rows * top, most, slope, True), shares(number_of, rows * top, most, slope, False)
    places = jnp.arange(number_of)

    def named(lengths, offset_by):
        used = int((lengths > 0).sum())
        fixed = max(1, used // 4)
        shifted = fixed + (places - fixed + offset_by * (used - fixed)) % max(1, number_of - fixed)
        return jnp.zeros((number_of,), jnp.int32).at[ranking[jnp.where(places < fixed, places, shifted)]].set(jnp.asarray(lengths, jnp.int32))

    lengths = jnp.where(number % 4 == 0, named(crowded, number // 4), named(common, number - number // 4 - 1))
    mixed = jax.random.permutation(jax.random.fold_in(own, 3), number_of)
    giver, sink = mixed[0:number_of // 2 * 2:2], mixed[1:number_of // 2 * 2:2]
    slack = jnp.minimum(lengths[giver] - 1, most - lengths[sink]) // 2
    slack = jnp.where((giver == ranking[0]) | (sink == ranking[0]) | (lengths[sink] == 0), 0, jnp.maximum(slack, 0))
    shifted = jax.random.randint(jax.random.fold_in(own, 4), (number_of // 2,), 0, 1 << 20) % (slack + 1)
    lengths = lengths.at[giver].add(-shifted).at[sink].add(shifted)
    members = jnp.searchsorted(jnp.cumsum(lengths), jnp.arange(rows * top), side="right").astype(jnp.int32)
    grid = members.reshape(top, rows).T
    grid = grid[jax.random.permutation(jax.random.fold_in(own, 1), rows)]
    offset_by = jax.random.randint(jax.random.fold_in(own, 2), (rows, 1), 0, top)
    return jnp.take_along_axis(grid, (jnp.arange(top)[None, :] + offset_by) % top, axis=1)


def shares(amount, total, limit, lean, full):
    weights = [(1 << 20) // math.isqrt(grade ** lean) + 1 for grade in range(1, amount + 1)]
    largest = limit if full else min(limit, max(-(-total // amount), total * weights[0] // sum(weights)))
    least = 1 if total - largest >= amount - 1 else 0
    counts, spare = [largest] + [least] * (amount - 1), total - largest - least * (amount - 1)
    while spare > 0:
        movable = [i for i in range(1, amount) if counts[i] < largest] or [i for i in range(1, amount) if counts[i] < limit]
        whole, left = sum([weights[i] for i in movable]), spare
        for i in movable:
            more = min(limit - counts[i], max(1, left * weights[i] // whole), spare)
            counts[i] = counts[i] + more
            spare = spare - more
    return np.array(counts)


def centred(key, dims, width, reach, split=(), kind=jnp.bfloat16):
    array = jax.random.normal(key, dims, jnp.float32) * width
    if len(split) > 0:
        array = block_scale(key, dims, split, -0.22, 0.18) * array
    return jnp.clip(array, min=-reach, max=reach).astype(kind)


def setup_inputs(seed: int = 0) -> dict:
    splits = jax.random.split(jax.random.key(seed), 13)
    probe_field = centred(splits[0], (NODES, NT * PROBES), 1.0, 5.0, ((0, 16), (1, 16)))
    kappa = jnp.clip(jnp.exp(math.log(1.0) - 2.3025851 * jax.random.uniform(splits[1], (NODES,), jnp.float32) ** block_scale(splits[1], (NODES,), ((0, 16),), -0.2, 0.2)), 0.1, 1.0)
    theta_space = jnp.clip(jnp.exp(math.log(1.0) - 1.2039728 * jax.random.uniform(splits[2], (NT,), jnp.float32) ** block_scale(splits[2], (NT,), ((0, 16),), -0.2, 0.2)), 0.3, 1.0)
    theta_time = jnp.clip(jnp.exp(math.log(0.8) - 1.3862944 * jax.random.uniform(splits[3], (NT,), jnp.float32) ** block_scale(splits[3], (NT,), ((0, 16),), -0.2, 0.2)), 0.2, 0.8)
    diag_blocks = draw_diag_blocks(jax.random.fold_in(splits[12], 71), 0)
    off_blocks = centred(splits[5], (NB, NNZ_OFF, BLOCK, BLOCK), (0.8 / (BLOCK * NNZ_OFF) ** 0.5), 0.375, ((0, 16),))
    block_cols = plant(jax.random.randint(splits[6], (NB, NNZ_OFF), 0, NB_DEV + 2 * HALO_B), jax.random.fold_in(splits[6], 1), 0, (NB_DEV + 2 * HALO_B) - 1).astype(jnp.int32)
    halo_needs = plant(jax.random.randint(splits[7], (NEEDS,), 0, NB_DEV), jax.random.fold_in(splits[7], 1), 0, NB_DEV - 1).astype(jnp.int32)
    covariates = centred(splits[8], (OBS, NCOV), 0.7, 4.0, ((0, 256),))
    obs_owner_keys = jax.random.split(jax.random.fold_in(splits[9], 1), OBS // OBS_DEV)
    obs_owner_turns = jax.random.permutation(jax.random.fold_in(splits[9], 3), OBS // OBS_DEV)
    obs_owner = jax.vmap(lambda own, number: routed_block(jax.random.fold_in(splits[9], 2), own, number, OBS_DEV, N_SPACE, 1, CAP, 1))(obs_owner_keys, obs_owner_turns).reshape((OBS, 1))
    obs_cell = plant(jax.random.randint(splits[10], (OBS,), 0, NODES_DEV * T_DEV), jax.random.fold_in(splits[10], 1), 0, (NODES_DEV * T_DEV) - 1).astype(jnp.int32)
    svc_coef = centred(splits[11], (NODES, NCOV), NCOV ** -0.5, 0.375, ((0, 16),))
    return {"probe_field": probe_field, "kappa": kappa, "theta_space": theta_space, "theta_time": theta_time, "diag_blocks": diag_blocks, "off_blocks": off_blocks, "block_cols": block_cols, "halo_needs": halo_needs, "covariates": covariates, "obs_owner": obs_owner, "obs_cell": obs_cell, "svc_coef": svc_coef}


relaxation = 0.6


def reference(probe_field, kappa, theta_space, theta_time, diag_blocks, off_blocks, block_cols, halo_needs, covariates, obs_owner, obs_cell, svc_coef):
    columns = NT * PROBES
    width_local = NB_DEV + 2 * HALO_B
    probe_vals = probe_field.astype(jnp.float32)
    sdiag = jnp.diagonal(diag_blocks.astype(jnp.float32), axis1=1, axis2=2).reshape(NODES)
    scale_space = jnp.repeat(theta_space, PROBES)[None, :]
    scale_time = jnp.repeat(theta_time, PROBES)[None, :]
    base_diag = scale_space * sdiag[:, None] + 2.0 * scale_time + kappa[:, None]

    row_ids = jnp.arange(OBS, dtype=jnp.int32)
    slab = (row_ids // OBS_DEV) % N_TM
    owner = obs_owner[:, 0]
    node_ids = owner * NODES_DEV + obs_cell // T_DEV
    time_ids = slab * T_DEV + obs_cell % T_DEV
    eta = jnp.sum(covariates.astype(jnp.float32) * svc_coef[node_ids].astype(jnp.float32), axis=1)
    obs_weight = jnp.exp(eta)
    counted = jax.ops.segment_sum(obs_weight, node_ids * NT + time_ids, num_segments=NODES * NT)
    obs_diag = jnp.repeat(counted.reshape(NODES, NT), PROBES, axis=1)
    full_diag = base_diag + obs_diag

    block_ids = jnp.arange(NB, dtype=jnp.int32)
    space_of = block_ids // NB_DEV
    needs = halo_needs.reshape(N_SPACE, 2, HALO_B)

    def global_column(local):
        own = space_of * NB_DEV + local
        low_slot = jnp.clip(local - NB_DEV, 0, HALO_B - 1)
        low_block = needs[space_of, 0, low_slot]
        low_global = jnp.where(space_of > 0, (space_of - 1) * NB_DEV + low_block, NB)
        high_slot = jnp.clip(local - NB_DEV - HALO_B, 0, HALO_B - 1)
        high_block = needs[space_of, 1, high_slot]
        high_global = jnp.where(space_of < N_SPACE - 1, (space_of + 1) * NB_DEV + high_block, NB)
        return jnp.where(local < NB_DEV, own, jnp.where(local < NB_DEV + HALO_B, low_global, high_global)).astype(jnp.int32)

    local_ids = jnp.arange(width_local, dtype=jnp.int32)
    picks = (block_cols[:, :, None] == local_ids[None, None, :]).astype(jnp.float32)
    own_pick = ((block_ids - space_of * NB_DEV)[:, None] == local_ids[None, :]).astype(jnp.float32)
    combined = jnp.einsum('bkm,bkij->bmij', picks, off_blocks.astype(jnp.float32))
    combined = combined + own_pick[:, :, None, None] * diag_blocks.astype(jnp.float32)[:, None, :, :]
    combined = lax.optimization_barrier(combined.astype(jnp.bfloat16)).astype(jnp.float32)
    global_cols = [global_column(jnp.full((NB,), index, jnp.int32)) for index in range(width_local)]

    def spatial(field):
        blocks = field.reshape(NB, BLOCK, columns)
        padded = jnp.concatenate([blocks, jnp.zeros((1, BLOCK, columns), field.dtype)], axis=0)
        total = jnp.zeros((NB, BLOCK, columns), jnp.float32)
        for index in range(width_local):
            picked = padded[global_cols[index]]
            total = total + jnp.einsum('bij,bjc->bic', combined[:, index], picked.astype(jnp.float32))
        return total.reshape(NODES, columns)

    def temporal(field):
        values = field.astype(jnp.float32).reshape(NODES, NT, PROBES)
        padded = jnp.pad(values, ((0, 0), (1, 1), (0, 0)))
        return (2.0 * values - padded[:, :-2] - padded[:, 2:]).reshape(NODES, columns)

    solution = relaxation * probe_vals / base_diag
    for sweep in range(ITERS):
        rounded = lax.optimization_barrier(solution.astype(jnp.bfloat16))
        applied = scale_space * spatial(rounded) + scale_time * temporal(rounded) + (kappa[:, None] + obs_diag) * rounded.astype(jnp.float32)
        solution = solution + relaxation * (probe_vals - applied) / full_diag
    rounded = solution.astype(jnp.bfloat16)
    grad_space = jnp.sum(probe_vals * spatial(rounded), axis=0) / NODES
    grad_time = jnp.sum(probe_vals * temporal(rounded), axis=0) / NODES
    return solution, jnp.stack([grad_space, grad_time])
```

```python
import functools

import jax
import jax.numpy as jnp
from jax import lax
from jax.experimental import pallas as pl
from jax.experimental.pallas import tpu as pltpu
from jax.sharding import PartitionSpec as P

NB_DEV = 8
BLOCK = 128
HALO_B = 2
T_DEV = 4
PROBES = 64
NCOV = 256
OBS_DEV = 2048
ITERS = 4
NODES_DEV = 1024
COLS = T_DEV * PROBES
WIDTH = (NB_DEV + 2 * HALO_B) * BLOCK
HALO_ROWS = HALO_B * BLOCK
PACKED = NODES_DEV // 2
ROWS = NCOV + 16
EXCHANGES = ITERS + 1
CHUNK = 256

RELAX = 0.6
MESH = pl.DeviceIdType.MESH
F32 = jnp.float32
BF16 = jnp.bfloat16
NT_DIMS = (((1,), (1,)), ((), ()))


def dot(a, b):
    return jnp.dot(a, b, preferred_element_type=F32)


def iota(shape, dim):
    return lax.broadcasted_iota(jnp.int32, shape, dim)


def mark(condition):
    return jnp.where(condition, 1.0, 0.0).astype(BF16)


def split3(values):
    first = jnp.clip(values, -3.38e38, 3.38e38).astype(BF16)
    rest = values - first.astype(F32)
    second = rest.astype(BF16)
    third = (rest - second.astype(F32)).astype(BF16)
    return first, second, third


def kernel(
    peers,
    slabs,
    cap,
    probe_hbm,
    kappa_ref,
    theta_space_ref,
    theta_time_ref,
    diag_hbm,
    off_hbm,
    cols_ref,
    needs_ref,
    cov_hbm,
    owner_ref,
    cell_ref,
    coef_hbm,
    sol_ref,
    grads_ref,
    probe,
    diag,
    off,
    cov,
    coef,
    slots,
    covt,
    onehot,
    send_obs,
    recv_obs,
    masks,
    counted,
    comb,
    field,
    time_low,
    time_high,
    send_up,
    send_down,
    send_left,
    send_right,
    product,
    local_diag,
    step,
    needs_out,
    needs_in,
    picks,
    grads_out,
    grads_in,
    load_sem,
    obs_send_sem,
    obs_recv_sem,
    needs_send_sem,
    needs_recv_sem,
    halo_send_sem,
    halo_recv_sem,
    grads_send_sem,
    grads_recv_sem,
):
    me = lax.axis_index("space")
    slab = lax.axis_index("tm")
    left = lax.rem(slab + slabs - 1, slabs)
    right = lax.rem(slab + 1, slabs)
    down = lax.rem(me + peers - 1, peers)
    up = lax.rem(me + 1, peers)
    has_down, has_up = me > 0, me < peers - 1
    has_left, has_right = slab > 0, slab < slabs - 1

    loads = [
        pltpu.make_async_copy(src, dst, load_sem.at[i])
        for i, (src, dst) in enumerate(
            ((cov_hbm, cov), (probe_hbm, probe), (diag_hbm, diag), (off_hbm, off), (coef_hbm, coef))
        )
    ]
    for load in loads:
        load.start()

    barrier = pltpu.get_barrier_semaphore()

    def greet(k, carry):
        pl.semaphore_signal(
            barrier, inc=1, device_id=(lax.rem(me + k, peers), slab), device_id_type=MESH
        )
        return carry

    lax.fori_loop(1, peers, greet, 0)
    for other in (left, right):
        pl.semaphore_signal(barrier, inc=1, device_id=(me, other), device_id_type=MESH)

    owner_cols = jnp.transpose(owner_ref[...].astype(F32))
    lanes = iota((BLOCK, BLOCK), 1)
    below = mark(iota((BLOCK, BLOCK), 1) < iota((BLOCK, BLOCK), 0))
    seen = jnp.zeros((1, BLOCK), F32)
    for c in range(OBS_DEV // BLOCK):
        owner_col = owner_cols[:, c : c + 1].astype(jnp.int32)
        hit = owner_col == lanes
        hits = mark(hit)
        before = dot(below, hits) + seen
        rank = jnp.sum(jnp.where(hit, before, 0.0), axis=1, keepdims=True)
        seen = seen + jnp.sum(hits.astype(F32), axis=0, keepdims=True)
        slot = owner_col * cap + rank.astype(jnp.int32)
        slots[c * BLOCK : (c + 1) * BLOCK, :] = jnp.broadcast_to(slot, (BLOCK, BLOCK))

    loads[0].wait()
    sub = iota((16, BLOCK), 0)
    for c in range(OBS_DEV // BLOCK):
        part = slice(c * BLOCK, (c + 1) * BLOCK)
        covt[:NCOV, part] = jnp.transpose(cov[part, :])
        cell = jnp.broadcast_to(cell_ref[c : c + 1, :], (16, BLOCK))
        extra = jnp.where(
            sub == 0, cell // 64, jnp.where(sub == 1, cell % 64, jnp.where(sub == 2, 1, 0))
        )
        covt[NCOV:, part] = extra.astype(F32).astype(BF16)

    def compact(target):
        for c in range(OBS_DEV // BLOCK):
            part = slice(c * BLOCK, (c + 1) * BLOCK)
            place = slots[part, :] - target * cap
            for h in range(0, cap, BLOCK):
                onehot[part, h : h + BLOCK] = mark(place == lanes + h)
        return dot(covt[...], onehot[...]).astype(BF16)

    pl.semaphore_wait(barrier, peers + 1)

    sub8 = iota((8, COLS), 0)
    listed = jnp.zeros((8, COLS), jnp.int32)
    for i in range(2 * HALO_B):
        listed = jnp.where(sub8 == i, needs_ref[i], listed)
    needs_out[...] = listed

    def needs_copy(side, target):
        return pltpu.make_async_remote_copy(
            src_ref=needs_out,
            dst_ref=needs_in.at[side],
            send_sem=needs_send_sem.at[side],
            recv_sem=needs_recv_sem.at[side],
            device_id=(target, slab),
            device_id_type=MESH,
        )

    needs_copies = (needs_copy(0, up), needs_copy(1, down))
    for copy in needs_copies:
        copy.start()

    def obs_copy(k, target):
        return pltpu.make_async_remote_copy(
            src_ref=send_obs.at[k],
            dst_ref=recv_obs.at[k],
            send_sem=obs_send_sem.at[k],
            recv_sem=obs_recv_sem.at[k],
            device_id=(target, slab),
            device_id_type=MESH,
        )

    def send(k, carry):
        target = lax.rem(me + k, peers)
        send_obs[k] = compact(target)
        obs_copy(k, target).start()
        return carry

    lax.fori_loop(1, peers, send, 0)
    recv_obs[0] = compact(me)

    col_time = iota((1, COLS), 1) // PROBES
    scale_space = jnp.zeros((1, COLS), F32)
    scale_time = jnp.zeros((1, COLS), F32)
    for t in range(T_DEV):
        scale_space = jnp.where(col_time == t, theta_space_ref[t], scale_space)
        scale_time = jnp.where(col_time == t, theta_time_ref[t], scale_time)
    kappa_cols = jnp.transpose(kappa_ref[...])
    eye = iota((BLOCK, BLOCK), 0) == iota((BLOCK, BLOCK), 1)
    loads[1].wait()
    loads[2].wait()
    for b in range(NB_DEV):
        part = slice(b * BLOCK, (b + 1) * BLOCK)
        sdiag = jnp.sum(jnp.where(eye, diag[b].astype(F32), 0.0), axis=1, keepdims=True)
        kappa_col = kappa_cols[:, b : b + 1]
        base = scale_space * sdiag + 2.0 * scale_time + kappa_col
        step[part, :] = base
        local_diag[part, :] = jnp.broadcast_to(kappa_col, (BLOCK, COLS))
        start = RELAX * probe[part, :].astype(F32) / base
        sol_ref[part, :] = start
        field[0, part, :] = start.astype(BF16)

    for e in range(EXCHANGES):

        @pl.when(jnp.logical_not(has_down))
        def _():
            field[e, NODES_DEV : NODES_DEV + HALO_ROWS, :] = jnp.zeros((HALO_ROWS, COLS), BF16)

        @pl.when(jnp.logical_not(has_up))
        def _():
            field[e, NODES_DEV + HALO_ROWS :, :] = jnp.zeros((HALO_ROWS, COLS), BF16)

        @pl.when(jnp.logical_not(has_left))
        def _():
            time_low[e] = jnp.zeros((PACKED, BLOCK), BF16)

        @pl.when(jnp.logical_not(has_right))
        def _():
            time_high[e] = jnp.zeros((PACKED, BLOCK), BF16)

    for copy in needs_copies:
        copy.wait()
    for i in range(HALO_B):
        for b in range(NB_DEV):
            for side, row in ((1, i), (0, HALO_B + i)):
                picks[side, i, b] = mark(needs_in[side, row : row + 1, :] == b)

    row128 = iota((BLOCK, BLOCK), 0)
    shift_low = mark(row128 == lanes + PROBES)
    keep_high = mark((row128 == lanes) & (lanes >= PROBES))
    keep_low = mark((row128 == lanes) & (lanes < PROBES))
    shift_high = mark(row128 + PROBES == lanes)

    def halo_copy(e, which, src, dst, target):
        return pltpu.make_async_remote_copy(
            src_ref=src,
            dst_ref=dst,
            send_sem=halo_send_sem.at[e, which],
            recv_sem=halo_recv_sem.at[e, which],
            device_id=target,
            device_id_type=MESH,
        )

    def halo_copies(e):
        low = field.at[e, pl.ds(NODES_DEV, HALO_ROWS)]
        high = field.at[e, pl.ds(NODES_DEV + HALO_ROWS, HALO_ROWS)]
        return (
            (has_right, has_left, halo_copy(e, 0, send_right.at[e], time_low.at[e], (me, right))),
            (has_left, has_right, halo_copy(e, 1, send_left.at[e], time_high.at[e], (me, left))),
            (has_up, has_down, halo_copy(e, 2, send_up.at[e], low, (up, slab))),
            (has_down, has_up, halo_copy(e, 3, send_down.at[e], high, (down, slab))),
        )

    def start_halo(e):
        send_right[e] = (
            dot(field[e, :PACKED, BLOCK:], shift_low) + dot(field[e, PACKED:NODES_DEV, BLOCK:], keep_high)
        ).astype(BF16)
        send_left[e] = (
            dot(field[e, :PACKED, :BLOCK], keep_low) + dot(field[e, PACKED:NODES_DEV, :BLOCK], shift_high)
        ).astype(BF16)
        for i in range(HALO_B):
            part = slice(i * BLOCK, (i + 1) * BLOCK)
            for side, staged in ((1, send_up), (0, send_down)):
                chosen = picks[side, i, 0] * field[e, :BLOCK, :]
                for b in range(1, NB_DEV):
                    chosen = chosen + picks[side, i, b] * field[e, b * BLOCK : (b + 1) * BLOCK, :]
                staged[e, part, :] = chosen
        for sends, _, copy in halo_copies(e):
            pl.when(sends)(copy.start)

    def wait_halo(e):
        for _, receives, copy in halo_copies(e):
            pl.when(receives)(copy.wait_recv)

    start_halo(0)

    loads[3].wait()

    def combine(i, carry):
        b = i // NB_DEV
        rows = pl.ds(pl.multiple_of((i % NB_DEV) * 16, 16), 16)
        parts = [off[b, k, rows, :].astype(F32) for k in range(NB_DEV)]
        own = diag[b, rows, :].astype(F32)
        columns = [cols_ref[b, k] for k in range(NB_DEV)]
        place = pl.ds(pl.multiple_of(i * 16, 16), 16)
        for m in range(WIDTH // BLOCK):
            total = jnp.zeros((16, BLOCK), F32)
            for k in range(NB_DEV):
                total = total + jnp.where(columns[k] == m, 1.0, 0.0) * parts[k]
            if m < NB_DEV:
                total = total + jnp.where(b == m, 1.0, 0.0) * own
            comb[place, m * BLOCK : (m + 1) * BLOCK] = total.astype(BF16)
        return carry

    lax.fori_loop(0, NODES_DEV // 16, combine, 0)

    row_t, lane_t = iota((COLS, COLS), 0), iota((COLS, COLS), 1)
    inner = jnp.where(
        row_t == lane_t, 2.0, jnp.where(jnp.abs(row_t - lane_t) == PROBES, -1.0, 0.0)
    ).astype(BF16)
    row_h, lane_h = iota((BLOCK, COLS), 0), iota((BLOCK, COLS), 1)
    low_edge, high_edge = [], []
    for half in range(2):
        chosen = (row_h // PROBES) == half
        shift = half * PROBES
        low_edge.append(jnp.where(chosen & (lane_h == row_h - shift), -1.0, 0.0).astype(BF16))
        high_edge.append(
            jnp.where(chosen & (lane_h == row_h - shift + COLS - PROBES), -1.0, 0.0).astype(BF16)
        )

    def own_product(e):
        product[...] = dot(comb[:, :NODES_DEV], field[e, :NODES_DEV, :])

    def both(e, c):
        part = slice(c * CHUNK, (c + 1) * CHUNK)
        half, rest = divmod(c * CHUNK, PACKED)
        packed = slice(rest, rest + CHUNK)
        space = product[part, :] + dot(comb[part, NODES_DEV:], field[e, NODES_DEV:, :])
        time = (
            dot(field[e, part, :], inner)
            + dot(time_low[e, packed, :], low_edge[half])
            + dot(time_high[e, packed, :], high_edge[half])
        )
        return part, space, time

    own_product(0)

    loads[4].wait()
    counted[...] = jnp.zeros((NODES_DEV, BLOCK), F32)
    row_w = iota((BLOCK, cap), 0)

    def weigh(k):
        digits = recv_obs[k, NCOV:, :].astype(F32)
        live = digits[2:3, :] > 0.5
        cell = (digits[0:1, :] * 64.0 + digits[1:2, :]).astype(jnp.int32)
        node = jnp.where(live, cell // T_DEV, -1)
        time = cell % T_DEV
        rows = recv_obs[k, :NCOV, :]
        eta = jnp.zeros((1, cap), F32)
        for c in range(NODES_DEV // CHUNK):
            part = slice(c * CHUNK, (c + 1) * CHUNK)
            scores = dot(coef[part, :], rows)
            found = iota((CHUNK, cap), 0) + c * CHUNK == node
            eta = eta + jnp.sum(jnp.where(found, scores, 0.0), axis=0, keepdims=True)
            masks[part, :] = mark(found)
        weight = jnp.where(live, jnp.exp(eta), 0.0)
        pieces = [piece.astype(F32) for piece in split3(weight)]
        spread = jnp.zeros((BLOCK, cap), F32)
        for i, piece in enumerate(pieces):
            spread = jnp.where(row_w == time + i * T_DEV, piece, spread)
        counted[...] += lax.dot_general(
            masks[...], spread.astype(BF16), NT_DIMS, preferred_element_type=F32
        )

    weigh(0)

    def receive(k, carry):
        obs_copy(k, lax.rem(me + k, peers)).wait_recv()
        weigh(k)
        return carry

    lax.fori_loop(1, peers, receive, 0)

    spread_row, spread_col = iota((BLOCK, COLS), 0), iota((BLOCK, COLS), 1) // PROBES
    repeat = mark((spread_row < 3 * T_DEV) & (spread_row % T_DEV == spread_col))
    wait_halo(0)
    for c in range(NODES_DEV // CHUNK):
        part, space, time = both(0, c)
        pieces = split3(counted[part, :])
        obs_diag = dot(pieces[0], repeat) + dot(pieces[1], repeat) + dot(pieces[2], repeat)
        mine = local_diag[part, :] + obs_diag
        local_diag[part, :] = mine
        rate = RELAX / (step[part, :] + obs_diag)
        step[part, :] = rate
        applied = scale_space * space + scale_time * time + mine * field[0, part, :].astype(F32)
        solved = sol_ref[part, :] + rate * (probe[part, :].astype(F32) - applied)
        sol_ref[part, :] = solved
        field[1, part, :] = solved.astype(BF16)

    for e in range(1, ITERS):
        start_halo(e)
        own_product(e)
        wait_halo(e)
        for c in range(NODES_DEV // CHUNK):
            part, space, time = both(e, c)
            applied = (
                scale_space * space
                + scale_time * time
                + local_diag[part, :] * field[e, part, :].astype(F32)
            )
            solved = sol_ref[part, :] + step[part, :] * (probe[part, :].astype(F32) - applied)
            sol_ref[part, :] = solved
            field[e + 1, part, :] = solved.astype(BF16)

    start_halo(ITERS)
    own_product(ITERS)
    wait_halo(ITERS)
    sums = [jnp.zeros((1, COLS), F32), jnp.zeros((1, COLS), F32)]
    for c in range(NODES_DEV // CHUNK):
        part, space, time = both(ITERS, c)
        values = probe[part, :].astype(F32)
        sums[0] = sums[0] + jnp.sum(values * space, axis=0, keepdims=True)
        sums[1] = sums[1] + jnp.sum(values * time, axis=0, keepdims=True)
    grads_out[...] = jnp.where(sub8 == 0, sums[0], jnp.where(sub8 == 1, sums[1], 0.0))
    grads_in[me] = grads_out[...]

    def grads_copy(k):
        target = lax.rem(me + k, peers)
        return pltpu.make_async_remote_copy(
            src_ref=grads_out,
            dst_ref=grads_in.at[me],
            send_sem=grads_send_sem.at[k],
            recv_sem=grads_recv_sem.at[k],
            device_id=(target, slab),
            device_id_type=MESH,
        )

    def grads_send(k, carry):
        grads_copy(k).start()
        return carry

    lax.fori_loop(1, peers, grads_send, 0)

    def finish(k, carry):
        grads_copy(k).wait()
        obs_copy(k, lax.rem(me + k, peers)).wait_send()
        return carry

    lax.fori_loop(1, peers, finish, 0)
    for e in range(EXCHANGES):
        for sends, _, copy in halo_copies(e):
            pl.when(sends)(copy.wait_send)
    total = grads_in[0]
    for s in range(1, peers):
        total = total + grads_in[s]
    grads_ref[...] = total[0:2, :] / (NODES_DEV * peers)


def shards(
    probe_field,
    kappa,
    theta_space,
    theta_time,
    diag_blocks,
    off_blocks,
    block_cols,
    halo_needs,
    covariates,
    obs_owner,
    obs_cell,
    svc_coef,
):
    peers = lax.axis_size("space")
    slabs = lax.axis_size("tm")
    cap = 2 * OBS_DEV // peers
    vmem = pl.BlockSpec(memory_space=pltpu.VMEM)
    smem = pl.BlockSpec(memory_space=pltpu.SMEM)
    anywhere = pl.BlockSpec(memory_space=pl.ANY)
    dma = pltpu.SemaphoreType.DMA
    return pl.pallas_call(
        functools.partial(kernel, peers, slabs, cap),
        out_shape=(
            jax.ShapeDtypeStruct((NODES_DEV, COLS), F32),
            jax.ShapeDtypeStruct((2, COLS), F32),
        ),
        in_specs=[
            anywhere,
            vmem,
            smem,
            smem,
            anywhere,
            anywhere,
            smem,
            smem,
            anywhere,
            vmem,
            vmem,
            anywhere,
        ],
        out_specs=(vmem, vmem),
        scratch_shapes=[
            pltpu.VMEM((NODES_DEV, COLS), BF16),
            pltpu.VMEM((NB_DEV, BLOCK, BLOCK), BF16),
            pltpu.VMEM((NB_DEV, NB_DEV, BLOCK, BLOCK), BF16),
            pltpu.VMEM((OBS_DEV, NCOV), BF16),
            pltpu.VMEM((NODES_DEV, NCOV), BF16),
            pltpu.VMEM((OBS_DEV, BLOCK), jnp.int32),
            pltpu.VMEM((ROWS, OBS_DEV), BF16),
            pltpu.VMEM((OBS_DEV, cap), BF16),
            pltpu.VMEM((peers, ROWS, cap), BF16),
            pltpu.VMEM((peers, ROWS, cap), BF16),
            pltpu.VMEM((NODES_DEV, cap), BF16),
            pltpu.VMEM((NODES_DEV, BLOCK), F32),
            pltpu.VMEM((NODES_DEV, WIDTH), BF16),
            pltpu.VMEM((EXCHANGES, WIDTH, COLS), BF16),
            pltpu.VMEM((EXCHANGES, PACKED, BLOCK), BF16),
            pltpu.VMEM((EXCHANGES, PACKED, BLOCK), BF16),
            pltpu.VMEM((EXCHANGES, HALO_ROWS, COLS), BF16),
            pltpu.VMEM((EXCHANGES, HALO_ROWS, COLS), BF16),
            pltpu.VMEM((EXCHANGES, PACKED, BLOCK), BF16),
            pltpu.VMEM((EXCHANGES, PACKED, BLOCK), BF16),
            pltpu.VMEM((NODES_DEV, COLS), F32),
            pltpu.VMEM((NODES_DEV, COLS), F32),
            pltpu.VMEM((NODES_DEV, COLS), F32),
            pltpu.VMEM((8, COLS), jnp.int32),
            pltpu.VMEM((2, 8, COLS), jnp.int32),
            pltpu.VMEM((2, HALO_B, NB_DEV, 1, COLS), BF16),
            pltpu.VMEM((8, COLS), F32),
            pltpu.VMEM((peers, 8, COLS), F32),
            dma((5,)),
            dma((peers,)),
            dma((peers,)),
            dma((2,)),
            dma((2,)),
            dma((EXCHANGES, 4)),
            dma((EXCHANGES, 4)),
            dma((peers,)),
            dma((peers,)),
        ],
        compiler_params=pltpu.CompilerParams(
            collective_id=0,
            has_side_effects=True,
            vmem_limit_bytes=48 * 1024 * 1024,
        ),
    )(
        probe_field,
        kappa.reshape(NB_DEV, BLOCK),
        theta_space,
        theta_time,
        diag_blocks,
        off_blocks,
        block_cols,
        halo_needs,
        covariates,
        obs_owner.reshape(OBS_DEV // BLOCK, BLOCK),
        obs_cell.reshape(OBS_DEV // BLOCK, BLOCK),
        svc_coef,
    )


def solution(mesh):
    return jax.shard_map(
        shards,
        mesh=mesh,
        in_specs=(
            P("space", "tm"),
            P("space"),
            P("tm"),
            P("tm"),
            P("space", None, None),
            P("space", None, None, None),
            P("space", None),
            P("space"),
            P(("space", "tm"), None),
            P(("space", "tm"), None),
            P(("space", "tm")),
            P("space", None),
        ),
        out_specs=(P("space", "tm"), P(None, "tm")),
        check_vma=False,
    )
```

```python
import functools

import jax
import jax.numpy as jnp
from jax import lax
from jax.experimental import pallas as pl
from jax.experimental.pallas import tpu as pltpu
from jax.sharding import PartitionSpec as P

NB_DEV = 8
BLOCK = 128
HALO_B = 2
T_DEV = 4
PROBES = 64
NCOV = 256
OBS_DEV = 2048
ITERS = 4
NODES_DEV = 1024
COLS = T_DEV * PROBES
WIDTH = (NB_DEV + 2 * HALO_B) * BLOCK
HALO_ROWS = HALO_B * BLOCK
ROWS = NCOV + 16
EXCHANGES = ITERS + 1
CHUNK = 256
CHUNKS = NODES_DEV // CHUNK

RELAX = 0.6
MESH = pl.DeviceIdType.MESH
F32 = jnp.float32
BF16 = jnp.bfloat16
NT_DIMS = (((1,), (1,)), ((), ()))


def dot(a, b):
    return jnp.dot(a, b, preferred_element_type=F32)


def iota(shape, dim):
    return lax.broadcasted_iota(jnp.int32, shape, dim)


def mark(condition):
    return jnp.where(condition, 1.0, 0.0).astype(BF16)


def split3(values):
    first = jnp.clip(values, -3.38e38, 3.38e38).astype(BF16)
    rest = values - first.astype(F32)
    second = rest.astype(BF16)
    third = (rest - second.astype(F32)).astype(BF16)
    return first, second, third


def kernel(
    peers,
    slabs,
    cap,
    probe_hbm,
    kappa_hbm,
    theta_space_hbm,
    theta_time_hbm,
    diag_hbm,
    off_hbm,
    cols_hbm,
    needs_hbm,
    cov_hbm,
    owner_hbm,
    cell_hbm,
    coef_hbm,
    sol_ref,
    grads_ref,
    probe,
    kappa,
    theta_space,
    theta_time,
    diag,
    off,
    cols,
    needs,
    cov,
    owner,
    cell,
    coef,
    slots,
    covt,
    onehot,
    send_obs,
    recv_obs,
    masks,
    counted,
    comb,
    field,
    first_low,
    first_high,
    time_low,
    time_high,
    send_up,
    send_down,
    send_left,
    send_right,
    product,
    residual,
    edges_out,
    edges_in,
    cross_out,
    cross_in,
    local_diag,
    step,
    needs_out,
    needs_in,
    picks,
    grads_out,
    grads_in,
    load_sem,
    obs_send_sem,
    obs_recv_sem,
    needs_send_sem,
    needs_recv_sem,
    space_send_sem,
    space_recv_sem,
    time_send_sem,
    time_recv_sem,
    edges_send_sem,
    edges_recv_sem,
    cross_send_sem,
    cross_recv_sem,
    grads_send_sem,
    grads_recv_sem,
):
    me = lax.axis_index("space")
    slab = lax.axis_index("tm")
    left = lax.rem(slab + slabs - 1, slabs)
    right = lax.rem(slab + 1, slabs)
    down = lax.rem(me + peers - 1, peers)
    up = lax.rem(me + 1, peers)
    has_down, has_up = me > 0, me < peers - 1
    has_left, has_right = slab > 0, slab < slabs - 1

    pairs = (
        (owner_hbm, owner),
        (cov_hbm, cov),
        (cell_hbm, cell),
        (needs_hbm, needs),
        (probe_hbm, probe),
        (kappa_hbm, kappa),
        (theta_space_hbm, theta_space),
        (theta_time_hbm, theta_time),
        (diag_hbm, diag),
        (off_hbm, off),
        (cols_hbm, cols),
        (coef_hbm, coef),
    )
    loads = [
        pltpu.make_async_copy(src, dst, load_sem.at[i]) for i, (src, dst) in enumerate(pairs)
    ]
    for load in loads:
        load.start()

    barrier = pltpu.get_barrier_semaphore()

    def greet(k, carry):
        pl.semaphore_signal(
            barrier, inc=1, device_id=(lax.rem(me + k, peers), slab), device_id_type=MESH
        )
        return carry

    lax.fori_loop(1, peers, greet, 0)
    for other in (left, right):
        pl.semaphore_signal(barrier, inc=1, device_id=(me, other), device_id_type=MESH)

    loads[0].wait()
    owner_cols = jnp.transpose(owner[...].astype(F32))
    lanes = iota((BLOCK, BLOCK), 1)
    below = mark(iota((BLOCK, BLOCK), 1) < iota((BLOCK, BLOCK), 0))
    seen = jnp.zeros((1, BLOCK), F32)
    for c in range(OBS_DEV // BLOCK):
        owner_col = owner_cols[:, c : c + 1].astype(jnp.int32)
        hit = owner_col == lanes
        hits = mark(hit)
        before = dot(below, hits) + seen
        rank = jnp.sum(jnp.where(hit, before, 0.0), axis=1, keepdims=True)
        seen = seen + jnp.sum(hits.astype(F32), axis=0, keepdims=True)
        slot = owner_col * cap + rank.astype(jnp.int32)
        slots[c * BLOCK : (c + 1) * BLOCK, :] = jnp.broadcast_to(slot, (BLOCK, BLOCK))

    loads[1].wait()
    loads[2].wait()
    sub = iota((16, BLOCK), 0)
    for c in range(OBS_DEV // BLOCK):
        part = slice(c * BLOCK, (c + 1) * BLOCK)
        covt[:NCOV, part] = jnp.transpose(cov[part, :])
        row = jnp.broadcast_to(cell[c : c + 1, :], (16, BLOCK))
        extra = jnp.where(
            sub == 0, row // 64, jnp.where(sub == 1, row % 64, jnp.where(sub == 2, 1, 0))
        )
        covt[NCOV:, part] = extra.astype(F32).astype(BF16)

    def compact(target):
        for c in range(OBS_DEV // BLOCK):
            part = slice(c * BLOCK, (c + 1) * BLOCK)
            place = slots[part, :] - target * cap
            for h in range(0, cap, BLOCK):
                onehot[part, h : h + BLOCK] = mark(place == lanes + h)
        return dot(covt[...], onehot[...]).astype(BF16)

    pl.semaphore_wait(barrier, peers + 1)

    loads[3].wait()
    sub8 = iota((8, COLS), 0)
    listed = jnp.zeros((8, COLS), jnp.int32)
    for i in range(2 * HALO_B):
        listed = jnp.where(sub8 == i, needs[i], listed)
    needs_out[...] = listed

    def needs_copy(side, target):
        return pltpu.make_async_remote_copy(
            src_ref=needs_out,
            dst_ref=needs_in.at[side],
            send_sem=needs_send_sem.at[side],
            recv_sem=needs_recv_sem.at[side],
            device_id=(target, slab),
            device_id_type=MESH,
        )

    needs_copies = (needs_copy(0, up), needs_copy(1, down))
    for copy in needs_copies:
        copy.start()

    for i in range(4, 9):
        loads[i].wait()
    sub_e = iota((8, BLOCK), 0)
    ends = (theta_space[T_DEV - 1], theta_time[T_DEV - 1], theta_space[0], theta_time[0])
    scales = jnp.ones((8, BLOCK), F32)
    for i, value in enumerate(ends):
        scales = jnp.where(sub_e == i, value, scales)
    edges_out[...] = scales

    def beside(sends, receives, src, dst, send_sem, recv_sem, target):
        copy = pltpu.make_async_remote_copy(
            src_ref=src,
            dst_ref=dst,
            send_sem=send_sem,
            recv_sem=recv_sem,
            device_id=(me, target),
            device_id_type=MESH,
        )
        return sends, receives, copy

    def both_ways(src_right, src_left, dst_low, dst_high, send_sems, recv_sems):
        return (
            beside(has_right, has_left, src_right, dst_low, send_sems[0], recv_sems[0], right),
            beside(has_left, has_right, src_left, dst_high, send_sems[1], recv_sems[1], left),
        )

    def pair(sems, *index):
        return [sems.at[*index, which] for which in range(2)]

    edge_copies = both_ways(
        edges_out, edges_out, edges_in.at[0], edges_in.at[1], pair(edges_send_sem), pair(edges_recv_sem)
    )

    def start_copies(copies):
        for sends, _, copy in copies:
            pl.when(sends)(copy.start)

    def wait_arrivals(copies):
        for _, receives, copy in copies:
            pl.when(receives)(copy.wait_recv)

    def wait_departures(copies):
        for sends, _, copy in copies:
            pl.when(sends)(copy.wait_send)

    start_copies(edge_copies)

    def obs_copy(k, target):
        return pltpu.make_async_remote_copy(
            src_ref=send_obs.at[k],
            dst_ref=recv_obs.at[k],
            send_sem=obs_send_sem.at[k],
            recv_sem=obs_recv_sem.at[k],
            device_id=(target, slab),
            device_id_type=MESH,
        )

    def send(k, carry):
        target = lax.rem(me + k, peers)
        send_obs[k] = compact(target)
        obs_copy(k, target).start()
        return carry

    lax.fori_loop(1, peers, send, 0)
    recv_obs[0] = compact(me)

    col_time = iota((1, COLS), 1) // PROBES
    scale_space = jnp.zeros((1, COLS), F32)
    scale_time = jnp.zeros((1, COLS), F32)
    for t in range(T_DEV):
        scale_space = jnp.where(col_time == t, theta_space[t], scale_space)
        scale_time = jnp.where(col_time == t, theta_time[t], scale_time)
    kappa_cols = jnp.transpose(kappa[...])
    eye = iota((BLOCK, BLOCK), 0) == iota((BLOCK, BLOCK), 1)
    sdiag_cols = []
    for b in range(NB_DEV):
        part = slice(b * BLOCK, (b + 1) * BLOCK)
        sdiag = jnp.sum(jnp.where(eye, diag[b].astype(F32), 0.0), axis=1, keepdims=True)
        sdiag_cols.append(sdiag)
        kappa_col = kappa_cols[:, b : b + 1]
        base = scale_space * sdiag + 2.0 * scale_time + kappa_col
        step[part, :] = base
        local_diag[part, :] = jnp.broadcast_to(kappa_col, (BLOCK, COLS))
        start = RELAX * probe[part, :].astype(F32) / base
        sol_ref[part, :] = start
        field[0, part, :] = start.astype(BF16)

    for e in range(EXCHANGES):

        @pl.when(jnp.logical_not(has_down))
        def _():
            field[e, NODES_DEV : NODES_DEV + HALO_ROWS, :] = jnp.zeros((HALO_ROWS, COLS), BF16)

        @pl.when(jnp.logical_not(has_up))
        def _():
            field[e, NODES_DEV + HALO_ROWS :, :] = jnp.zeros((HALO_ROWS, COLS), BF16)

    for there, side, first, later in ((has_left, 0, first_low, time_low), (has_right, 1, first_high, time_high)):

        @pl.when(jnp.logical_not(there))
        def _():
            first[...] = jnp.zeros_like(first)
            later[...] = jnp.zeros_like(later)
            edges_in[side] = jnp.ones((8, BLOCK), F32)
            cross_in[side] = jnp.zeros((8, BLOCK), F32)

    for copy in needs_copies:
        copy.wait()
    for i in range(HALO_B):
        for b in range(NB_DEV):
            for side, row in ((1, i), (0, HALO_B + i)):
                picks[side, i, b] = mark(needs_in[side, row : row + 1, :] == b)

    lower_half = lanes < PROBES

    def pack_last(values):
        return jnp.where(
            lower_half, pltpu.roll(values[:BLOCK, BLOCK:], PROBES, 1), values[BLOCK:, BLOCK:]
        )

    def pack_first(values):
        return jnp.where(
            lower_half, values[:BLOCK, :BLOCK], pltpu.roll(values[BLOCK:, :BLOCK], PROBES, 1)
        )

    def time_copies(e, c):
        lows, highs = (first_low, first_high) if e == 0 else (time_low.at[e], time_high.at[e])
        return both_ways(
            send_right.at[e, c],
            send_left.at[e, c],
            lows.at[c],
            highs.at[c],
            pair(time_send_sem, e, c),
            pair(time_recv_sem, e, c),
        )

    def start_time(e, c, values):
        send_right[e, c] = pack_last(values).astype(BF16)
        send_left[e, c] = pack_first(values).astype(BF16)
        start_copies(time_copies(e, c))

    def space_copies(e):
        copies = []
        for which, sends, receives, src, offset, target in (
            (0, has_up, has_down, send_up, 0, up),
            (1, has_down, has_up, send_down, HALO_ROWS, down),
        ):
            copy = pltpu.make_async_remote_copy(
                src_ref=src.at[e],
                dst_ref=field.at[e, pl.ds(NODES_DEV + offset, HALO_ROWS)],
                send_sem=space_send_sem.at[e, which],
                recv_sem=space_recv_sem.at[e, which],
                device_id=(target, slab),
                device_id_type=MESH,
            )
            copies.append((sends, receives, copy))
        return copies

    def start_space(e):
        for i in range(HALO_B):
            part = slice(i * BLOCK, (i + 1) * BLOCK)
            for side, staged in ((1, send_up), (0, send_down)):
                chosen = picks[side, i, 0] * field[e, :BLOCK, :]
                for b in range(1, NB_DEV):
                    chosen = chosen + picks[side, i, b] * field[e, b * BLOCK : (b + 1) * BLOCK, :]
                staged[e, part, :] = chosen
        start_copies(space_copies(e))

    start_space(0)
    for c in range(CHUNKS):
        start_time(0, c, probe[c * CHUNK : (c + 1) * CHUNK, :].astype(F32))

    loads[9].wait()
    loads[10].wait()

    def combine(i, carry):
        b = i // NB_DEV
        rows = pl.ds(pl.multiple_of((i % NB_DEV) * 16, 16), 16)
        parts = [off[b, k, rows, :].astype(F32) for k in range(NB_DEV)]
        own = diag[b, rows, :].astype(F32)
        columns = [cols[b, k] for k in range(NB_DEV)]
        place = pl.ds(pl.multiple_of(i * 16, 16), 16)
        for m in range(WIDTH // BLOCK):
            total = jnp.zeros((16, BLOCK), F32)
            for k in range(NB_DEV):
                total = total + jnp.where(columns[k] == m, 1.0, 0.0) * parts[k]
            if m < NB_DEV:
                total = total + jnp.where(b == m, 1.0, 0.0) * own
            comb[place, m * BLOCK : (m + 1) * BLOCK] = total.astype(BF16)
        return carry

    lax.fori_loop(0, NODES_DEV // 16, combine, 0)

    row_t, lane_t = iota((COLS, COLS), 0), iota((COLS, COLS), 1)
    inner = jnp.where(
        row_t == lane_t, 2.0, jnp.where(jnp.abs(row_t - lane_t) == PROBES, -1.0, 0.0)
    ).astype(BF16)
    def own_product(e):
        product[...] = dot(comb[:, :NODES_DEV], field[e, :NODES_DEV, :])

    def both(e, part):
        space = product[part, :] + dot(comb[part, NODES_DEV:], field[e, NODES_DEV:, :])
        return space, dot(field[e, part, :], inner)

    def parts():
        for c in range(CHUNKS):
            yield c, slice(c * CHUNK, (c + 1) * CHUNK)

    def inner_residual(e):
        for _, part in parts():
            space, time = both(e, part)
            applied = (
                scale_space * space
                + scale_time * time
                + local_diag[part, :] * field[e, part, :].astype(F32)
            )
            residual[part, :] = probe[part, :].astype(F32) - applied

    def update(e, c, part):
        low, high = time_low[e, c].astype(F32), time_high[e, c].astype(F32)
        first = scale_time[:, :BLOCK] * jnp.concatenate(
            [jnp.where(lower_half, low, 0.0), jnp.where(lower_half, pltpu.roll(low, PROBES, 1), 0.0)], axis=0
        )
        last = scale_time[:, BLOCK:] * jnp.concatenate(
            [jnp.where(lower_half, 0.0, pltpu.roll(high, PROBES, 1)), jnp.where(lower_half, 0.0, high)], axis=0
        )
        left_over = residual[part, :] + jnp.concatenate([first, last], axis=1)
        solved = sol_ref[part, :] + step[part, :] * left_over
        sol_ref[part, :] = solved
        field[e + 1, part, :] = solved.astype(BF16)
        return solved

    own_product(0)

    loads[11].wait()
    counted[...] = jnp.zeros((NODES_DEV, BLOCK), F32)
    row_w = iota((BLOCK, cap), 0)

    def weigh(k):
        digits = recv_obs[k, NCOV:, :].astype(F32)
        live = digits[2:3, :] > 0.5
        number = (digits[0:1, :] * 64.0 + digits[1:2, :]).astype(jnp.int32)
        node = jnp.where(live, number // T_DEV, -1)
        time = number % T_DEV
        rows = recv_obs[k, :NCOV, :]
        eta = jnp.zeros((1, cap), F32)
        for c in range(NODES_DEV // CHUNK):
            part = slice(c * CHUNK, (c + 1) * CHUNK)
            scores = dot(coef[part, :], rows)
            found = iota((CHUNK, cap), 0) + c * CHUNK == node
            eta = eta + jnp.sum(jnp.where(found, scores, 0.0), axis=0, keepdims=True)
            masks[part, :] = mark(found)
        weight = jnp.where(live, jnp.exp(eta), 0.0)
        pieces = [piece.astype(F32) for piece in split3(weight)]
        spread = jnp.zeros((BLOCK, cap), F32)
        for i, piece in enumerate(pieces):
            spread = jnp.where(row_w == time + i * T_DEV, piece, spread)
        counted[...] += lax.dot_general(
            masks[...], spread.astype(BF16), NT_DIMS, preferred_element_type=F32
        )

    weigh(0)

    def receive(k, carry):
        obs_copy(k, lax.rem(me + k, peers)).wait_recv()
        weigh(k)
        return carry

    lax.fori_loop(1, peers, receive, 0)

    spread_row, spread_col = iota((BLOCK, COLS), 0), iota((BLOCK, COLS), 1) // PROBES
    repeat = mark((spread_row < 3 * T_DEV) & (spread_row % T_DEV == spread_col))
    for _, part in parts():
        pieces = split3(counted[part, :])
        obs_diag = dot(pieces[0], repeat) + dot(pieces[1], repeat) + dot(pieces[2], repeat)
        local_diag[part, :] = local_diag[part, :] + obs_diag
        step[part, :] = RELAX / (step[part, :] + obs_diag)

    wait_arrivals(edge_copies)
    for c in range(CHUNKS):
        wait_arrivals(time_copies(0, c))
        lo, hi = 2 * c, 2 * c + 1
        sdiag = jnp.where(lower_half, sdiag_cols[lo], sdiag_cols[hi])
        nugget = jnp.where(lower_half, kappa_cols[:, lo : lo + 1], kappa_cols[:, hi : hi + 1])
        for side, row, first, later in ((0, 0, first_low, time_low), (1, 2, first_high, time_high)):
            base = edges_in[side, row : row + 1, :] * sdiag + 2.0 * edges_in[side, row + 1 : row + 2, :] + nugget
            later[0, c] = (RELAX * first[c].astype(F32) / base).astype(BF16)

    crossed = [jnp.zeros((1, BLOCK), F32), jnp.zeros((1, BLOCK), F32)]
    for e in range(ITERS):
        wait_arrivals(space_copies(e))
        inner_residual(e)
        for c, part in parts():
            if e > 0:
                wait_arrivals(time_copies(e, c))
            solved = update(e, c, part)
            if e < ITERS - 1:
                start_time(e + 1, c, solved)
            else:
                rounded = solved.astype(BF16).astype(F32)
                for i, packed, there in ((0, pack_last(rounded), first_high), (1, pack_first(rounded), first_low)):
                    terms = packed * there[c].astype(F32)
                    crossed[i] = crossed[i] + jnp.sum(terms, axis=0, keepdims=True)
        start_space(e + 1)
        if e < ITERS - 1:
            own_product(e + 1)

    for i in range(2):
        cross_out[i] = jnp.broadcast_to(crossed[i], (8, BLOCK))
    cross_copies = both_ways(
        cross_out.at[0],
        cross_out.at[1],
        cross_in.at[0],
        cross_in.at[1],
        pair(cross_send_sem),
        pair(cross_recv_sem),
    )
    start_copies(cross_copies)
    own_product(ITERS)
    wait_arrivals(space_copies(ITERS))
    sums = [jnp.zeros((1, COLS), F32), jnp.zeros((1, COLS), F32)]
    for _, part in parts():
        values = probe[part, :].astype(F32)
        for i, term in enumerate(both(ITERS, part)):
            sums[i] = sums[i] + jnp.sum(values * term, axis=0, keepdims=True)
    wait_arrivals(cross_copies)
    folded = [cross_in[i] + pltpu.roll(cross_in[i], PROBES, 1) for i in range(2)]
    low8 = iota((8, BLOCK), 1) < PROBES
    owed = jnp.concatenate([jnp.where(low8, folded[0], 0.0), jnp.where(low8, 0.0, folded[1])], axis=1)
    sums[1] = sums[1] - owed[0:1, :]
    grads_out[...] = jnp.where(sub8 == 0, sums[0], jnp.where(sub8 == 1, sums[1], 0.0))
    grads_in[me] = grads_out[...]

    def grads_copy(k):
        target = lax.rem(me + k, peers)
        return pltpu.make_async_remote_copy(
            src_ref=grads_out,
            dst_ref=grads_in.at[me],
            send_sem=grads_send_sem.at[k],
            recv_sem=grads_recv_sem.at[k],
            device_id=(target, slab),
            device_id_type=MESH,
        )

    def grads_send(k, carry):
        grads_copy(k).start()
        return carry

    lax.fori_loop(1, peers, grads_send, 0)

    def finish(k, carry):
        grads_copy(k).wait()
        obs_copy(k, lax.rem(me + k, peers)).wait_send()
        return carry

    lax.fori_loop(1, peers, finish, 0)
    wait_departures(edge_copies)
    wait_departures(cross_copies)
    for e in range(EXCHANGES):
        wait_departures(space_copies(e))
        if e < ITERS:
            for c in range(CHUNKS):
                wait_departures(time_copies(e, c))
    total = grads_in[0]
    for s in range(1, peers):
        total = total + grads_in[s]
    grads_ref[...] = total[0:2, :] / (NODES_DEV * peers)


def shards(
    probe_field,
    kappa,
    theta_space,
    theta_time,
    diag_blocks,
    off_blocks,
    block_cols,
    halo_needs,
    covariates,
    obs_owner,
    obs_cell,
    svc_coef,
):
    peers = lax.axis_size("space")
    slabs = lax.axis_size("tm")
    cap = 2 * OBS_DEV // peers
    vmem = pl.BlockSpec(memory_space=pltpu.VMEM)
    dma = pltpu.SemaphoreType.DMA
    return pl.pallas_call(
        functools.partial(kernel, peers, slabs, cap),
        out_shape=(
            jax.ShapeDtypeStruct((NODES_DEV, COLS), F32),
            jax.ShapeDtypeStruct((2, COLS), F32),
        ),
        in_specs=[pl.BlockSpec(memory_space=pltpu.HBM)] * 12,
        out_specs=(vmem, vmem),
        scratch_shapes=[
            pltpu.VMEM((NODES_DEV, COLS), BF16),
            pltpu.VMEM((NB_DEV, BLOCK), F32),
            pltpu.SMEM((T_DEV,), F32),
            pltpu.SMEM((T_DEV,), F32),
            pltpu.VMEM((NB_DEV, BLOCK, BLOCK), BF16),
            pltpu.VMEM((NB_DEV, NB_DEV, BLOCK, BLOCK), BF16),
            pltpu.SMEM((NB_DEV, NB_DEV), jnp.int32),
            pltpu.SMEM((2 * HALO_B,), jnp.int32),
            pltpu.VMEM((OBS_DEV, NCOV), BF16),
            pltpu.VMEM((OBS_DEV // BLOCK, BLOCK), jnp.int32),
            pltpu.VMEM((OBS_DEV // BLOCK, BLOCK), jnp.int32),
            pltpu.VMEM((NODES_DEV, NCOV), BF16),
            pltpu.VMEM((OBS_DEV, BLOCK), jnp.int32),
            pltpu.VMEM((ROWS, OBS_DEV), BF16),
            pltpu.VMEM((OBS_DEV, cap), BF16),
            pltpu.VMEM((peers, ROWS, cap), BF16),
            pltpu.VMEM((peers, ROWS, cap), BF16),
            pltpu.VMEM((NODES_DEV, cap), BF16),
            pltpu.VMEM((NODES_DEV, BLOCK), F32),
            pltpu.VMEM((NODES_DEV, WIDTH), BF16),
            pltpu.VMEM((EXCHANGES, WIDTH, COLS), BF16),
            pltpu.VMEM((CHUNKS, BLOCK, BLOCK), BF16),
            pltpu.VMEM((CHUNKS, BLOCK, BLOCK), BF16),
            pltpu.VMEM((ITERS, CHUNKS, BLOCK, BLOCK), BF16),
            pltpu.VMEM((ITERS, CHUNKS, BLOCK, BLOCK), BF16),
            pltpu.VMEM((EXCHANGES, HALO_ROWS, COLS), BF16),
            pltpu.VMEM((EXCHANGES, HALO_ROWS, COLS), BF16),
            pltpu.VMEM((ITERS, CHUNKS, BLOCK, BLOCK), BF16),
            pltpu.VMEM((ITERS, CHUNKS, BLOCK, BLOCK), BF16),
            pltpu.VMEM((NODES_DEV, COLS), F32),
            pltpu.VMEM((NODES_DEV, COLS), F32),
            pltpu.VMEM((8, BLOCK), F32),
            pltpu.VMEM((2, 8, BLOCK), F32),
            pltpu.VMEM((2, 8, BLOCK), F32),
            pltpu.VMEM((2, 8, BLOCK), F32),
            pltpu.VMEM((NODES_DEV, COLS), F32),
            pltpu.VMEM((NODES_DEV, COLS), F32),
            pltpu.VMEM((8, COLS), jnp.int32),
            pltpu.VMEM((2, 8, COLS), jnp.int32),
            pltpu.VMEM((2, HALO_B, NB_DEV, 1, COLS), BF16),
            pltpu.VMEM((8, COLS), F32),
            pltpu.VMEM((peers, 8, COLS), F32),
            dma((12,)),
            dma((peers,)),
            dma((peers,)),
            dma((2,)),
            dma((2,)),
            dma((EXCHANGES, 2)),
            dma((EXCHANGES, 2)),
            dma((ITERS, CHUNKS, 2)),
            dma((ITERS, CHUNKS, 2)),
            dma((2,)),
            dma((2,)),
            dma((2,)),
            dma((2,)),
            dma((peers,)),
            dma((peers,)),
        ],
        compiler_params=pltpu.CompilerParams(
            collective_id=0,
            has_side_effects=True,
            vmem_limit_bytes=60 * 1024 * 1024,
        ),
    )(
        probe_field,
        kappa.reshape(NB_DEV, BLOCK),
        theta_space,
        theta_time,
        diag_blocks,
        off_blocks,
        block_cols,
        halo_needs,
        covariates,
        obs_owner.reshape(OBS_DEV // BLOCK, BLOCK),
        obs_cell.reshape(OBS_DEV // BLOCK, BLOCK),
        svc_coef,
    )


def solution(mesh):
    return jax.shard_map(
        shards,
        mesh=mesh,
        in_specs=(
            P("space", "tm"),
            P("space"),
            P("tm"),
            P("tm"),
            P("space", None, None),
            P("space", None, None, None),
            P("space", None),
            P("space"),
            P(("space", "tm"), None),
            P(("space", "tm"), None),
            P(("space", "tm")),
            P("space", None),
        ),
        out_specs=(P("space", "tm"), P(None, "tm")),
        check_vma=False,
    )
```

```python
import functools

import jax
import jax.numpy as jnp
from jax import lax
from jax.experimental import pallas as pl
from jax.experimental.pallas import tpu as pltpu
from jax.sharding import PartitionSpec as P

NB_DEV = 8
BLOCK = 128
HALO_B = 2
T_DEV = 4
PROBES = 64
NCOV = 256
OBS_DEV = 2048
ITERS = 4
NODES_DEV = 1024
COLS = T_DEV * PROBES
WIDTH = (NB_DEV + 2 * HALO_B) * BLOCK
HALO_ROWS = HALO_B * BLOCK
ROWS = NCOV + 16
EXCHANGES = ITERS + 1
CHUNK = 256
CHUNKS = NODES_DEV // CHUNK
GROUP = 4
THIN = PROBES // GROUP
HALF = NODES_DEV // 2
CELLS = NB_DEV * T_DEV

RELAX = 0.6
MESH = pl.DeviceIdType.MESH
F32 = jnp.float32
BF16 = jnp.bfloat16
NT_DIMS = (((1,), (1,)), ((), ()))


def dot(a, b):
    return jnp.dot(a, b, preferred_element_type=F32)


def iota(shape, dim):
    return lax.broadcasted_iota(jnp.int32, shape, dim)


def mark(condition):
    return jnp.where(condition, 1.0, 0.0).astype(BF16)


def split3(values):
    first = jnp.clip(values, -3.38e38, 3.38e38).astype(BF16)
    rest = values - first.astype(F32)
    second = rest.astype(BF16)
    third = (rest - second.astype(F32)).astype(BF16)
    return first, second, third


def kernel(
    peers,
    slabs,
    cap,
    probe_hbm,
    kappa_hbm,
    theta_space_hbm,
    theta_time_hbm,
    diag_hbm,
    off_hbm,
    cols_hbm,
    needs_hbm,
    cov_hbm,
    owner_hbm,
    cell_hbm,
    coef_hbm,
    sol_ref,
    grads_ref,
    probe,
    kappa,
    theta_space,
    theta_time,
    diag,
    off,
    cols,
    needs,
    cov,
    owner,
    cell,
    coef,
    slots,
    covt,
    onehot,
    send_obs,
    recv_obs,
    masks,
    counted,
    comb,
    field,
    time_low,
    time_high,
    send_up,
    send_down,
    send_left,
    send_right,
    product,
    residual,
    fine,
    turned,
    swap_out,
    swap_in,
    back_out,
    back_in,
    scales_out,
    scales_in,
    sums_out,
    sums_in,
    needs_out,
    needs_in,
    picks,
    local_diag,
    step,
    run_out,
    run_in,
    grads_out,
    grads_in,
    load_sem,
    obs_send_sem,
    obs_recv_sem,
    needs_send_sem,
    needs_recv_sem,
    space_send_sem,
    space_recv_sem,
    time_send_sem,
    time_recv_sem,
    swap_send_sem,
    swap_recv_sem,
    back_send_sem,
    back_recv_sem,
    scales_send_sem,
    scales_recv_sem,
    sums_send_sem,
    sums_recv_sem,
    run_send_sem,
    run_recv_sem,
    grads_send_sem,
    grads_recv_sem,
):
    me = lax.axis_index("space")
    slab = lax.axis_index("tm")
    turn = lax.rem(slab, GROUP)
    run = slab - turn
    left = lax.rem(slab + slabs - GROUP, slabs)
    right = lax.rem(slab + GROUP, slabs)
    down = lax.rem(me + peers - 1, peers)
    up = lax.rem(me + 1, peers)
    has_down, has_up = me > 0, me < peers - 1
    has_left, has_right = run > 0, run < slabs - GROUP

    pairs = (
        (owner_hbm, owner),
        (cov_hbm, cov),
        (cell_hbm, cell),
        (needs_hbm, needs),
        (probe_hbm, probe),
        (kappa_hbm, kappa),
        (theta_space_hbm, theta_space),
        (theta_time_hbm, theta_time),
        (diag_hbm, diag),
        (off_hbm, off),
        (cols_hbm, cols),
        (coef_hbm, coef),
    )
    loads = [
        pltpu.make_async_copy(src, dst, load_sem.at[i]) for i, (src, dst) in enumerate(pairs)
    ]
    for load in loads:
        load.start()

    barrier = pltpu.get_barrier_semaphore()

    def greet(k, carry):
        pl.semaphore_signal(
            barrier, inc=1, device_id=(lax.rem(me + k, peers), slab), device_id_type=MESH
        )
        return carry

    lax.fori_loop(1, peers, greet, 0)
    ahead = [run + lax.rem(turn + k, GROUP) for k in range(GROUP)]
    behind = [lax.rem(turn + GROUP - k, GROUP) for k in range(GROUP)]
    for other in (left, right, *ahead[1:]):
        pl.semaphore_signal(barrier, inc=1, device_id=(me, other), device_id_type=MESH)

    loads[0].wait()
    owner_cols = jnp.transpose(owner[...].astype(F32))
    lanes = iota((BLOCK, BLOCK), 1)
    below = mark(iota((BLOCK, BLOCK), 1) < iota((BLOCK, BLOCK), 0))
    seen = jnp.zeros((1, BLOCK), F32)
    for c in range(OBS_DEV // BLOCK):
        owner_col = owner_cols[:, c : c + 1].astype(jnp.int32)
        hit = owner_col == lanes
        hits = mark(hit)
        before = dot(below, hits) + seen
        rank = jnp.sum(jnp.where(hit, before, 0.0), axis=1, keepdims=True)
        seen = seen + jnp.sum(hits.astype(F32), axis=0, keepdims=True)
        slot = owner_col * cap + rank.astype(jnp.int32)
        slots[c * BLOCK : (c + 1) * BLOCK, :] = jnp.broadcast_to(slot, (BLOCK, BLOCK))

    loads[1].wait()
    loads[2].wait()
    sub = iota((16, BLOCK), 0)
    for c in range(OBS_DEV // BLOCK):
        part = slice(c * BLOCK, (c + 1) * BLOCK)
        covt[:NCOV, part] = jnp.transpose(cov[part, :])
        row = jnp.broadcast_to(cell[c : c + 1, :], (16, BLOCK))
        extra = jnp.where(
            sub == 0, row // 64, jnp.where(sub == 1, row % 64, jnp.where(sub == 2, 1, 0))
        )
        covt[NCOV:, part] = extra.astype(F32).astype(BF16)

    def compact(target):
        for c in range(OBS_DEV // BLOCK):
            part = slice(c * BLOCK, (c + 1) * BLOCK)
            place = slots[part, :] - target * cap
            for h in range(0, cap, BLOCK):
                onehot[part, h : h + BLOCK] = mark(place == lanes + h)
        return dot(covt[...], onehot[...]).astype(BF16)

    pl.semaphore_wait(barrier, peers + GROUP)

    loads[3].wait()
    sub8 = iota((8, COLS), 0)
    listed = jnp.zeros((8, COLS), jnp.int32)
    for i in range(2 * HALO_B):
        listed = jnp.where(sub8 == i, needs[i], listed)
    needs_out[...] = listed

    def needs_copy(side, target):
        return pltpu.make_async_remote_copy(
            src_ref=needs_out,
            dst_ref=needs_in.at[side],
            send_sem=needs_send_sem.at[side],
            recv_sem=needs_recv_sem.at[side],
            device_id=(target, slab),
            device_id_type=MESH,
        )

    needs_copies = (needs_copy(0, up), needs_copy(1, down))
    for copy in needs_copies:
        copy.start()

    for i in range(4, 9):
        loads[i].wait()
    col = iota((8, COLS), 1)
    sub8 = iota((8, COLS), 0)
    mine = jnp.zeros((8, COLS), F32)
    for t in range(T_DEV):
        here = (col // PROBES == turn) & ((col // THIN) % T_DEV == t)
        mine = jnp.where(here & (sub8 == 0), theta_space[t], mine)
        mine = jnp.where(here & (sub8 == 1), theta_time[t], mine)
    scales_out[...] = mine

    def group_copy(k, src, dst, send_sem, recv_sem):
        return pltpu.make_async_remote_copy(
            src_ref=src,
            dst_ref=dst,
            send_sem=send_sem.at[k],
            recv_sem=recv_sem.at[k],
            device_id=(me, ahead[k]),
            device_id_type=MESH,
        )

    scales_copies = [
        group_copy(k, scales_out, scales_in.at[k], scales_send_sem, scales_recv_sem) for k in range(1, GROUP)
    ]
    swap_copies = [
        group_copy(k, swap_out.at[k], swap_in.at[k], swap_send_sem, swap_recv_sem) for k in range(1, GROUP)
    ]
    back_copies = [
        group_copy(k, back_out.at[k], back_in.at[k], back_send_sem, back_recv_sem) for k in range(1, GROUP)
    ]
    place = pl.ds(pl.multiple_of(turn * CELLS, CELLS), CELLS)
    sums_copies = [
        group_copy(k, sums_out, sums_in.at[place], sums_send_sem, sums_recv_sem) for k in range(1, GROUP)
    ]

    tall, wide = (iota((COLS, BLOCK), i) for i in range(2))
    low_tall, high_wide = (iota((BLOCK, COLS), i) for i in range(2))

    def by_probe(lane, which):
        return (lane // THIN) * PROBES + which * THIN + lane % THIN

    def by_time(lane, which):
        return which * PROBES + lane

    def take(source, order, which):
        left_half = mark((wide < PROBES) & (tall == order(wide, which)))
        right_half = mark((wide >= PROBES) & (tall == order(wide - PROBES, which)))
        return (dot(source[:HALF, :], left_half) + dot(source[HALF:, :], right_half)).astype(BF16)

    def put(terms, order):
        halves = [jnp.zeros((HALF, COLS), F32), jnp.zeros((HALF, COLS), F32)]
        for value, which in terms:
            for half in range(2):
                lane = low_tall - half * PROBES
                keep = (low_tall // PROBES == half) & (high_wide == order(lane, which))
                halves[half] = halves[half] + dot(value, mark(keep))
        return halves

    swap_in[0] = take(probe, by_probe, turn)
    for k in range(1, GROUP):
        swap_out[k] = take(probe, by_probe, lax.rem(turn + k, GROUP))
    for copy in scales_copies + swap_copies:
        copy.start()

    def beside(sends, receives, src, dst, send_sem, recv_sem, target):
        copy = pltpu.make_async_remote_copy(
            src_ref=src,
            dst_ref=dst,
            send_sem=send_sem,
            recv_sem=recv_sem,
            device_id=(me, target),
            device_id_type=MESH,
        )
        return sends, receives, copy

    def both_ways(src_right, src_left, dst_low, dst_high, send_sems, recv_sems):
        return (
            beside(has_right, has_left, src_right, dst_low, send_sems[0], recv_sems[0], right),
            beside(has_left, has_right, src_left, dst_high, send_sems[1], recv_sems[1], left),
        )

    def pair(sems, *index):
        return [sems.at[*index, which] for which in range(2)]

    def start_copies(copies):
        for sends, _, copy in copies:
            pl.when(sends)(copy.start)

    def wait_arrivals(copies):
        for _, receives, copy in copies:
            pl.when(receives)(copy.wait_recv)

    def wait_departures(copies):
        for sends, _, copy in copies:
            pl.when(sends)(copy.wait_send)


    def obs_copy(k, target):
        return pltpu.make_async_remote_copy(
            src_ref=send_obs.at[k],
            dst_ref=recv_obs.at[k],
            send_sem=obs_send_sem.at[k],
            recv_sem=obs_recv_sem.at[k],
            device_id=(target, slab),
            device_id_type=MESH,
        )

    def send(k, carry):
        target = lax.rem(me + k, peers)
        send_obs[k] = compact(target)
        obs_copy(k, target).start()
        return carry

    lax.fori_loop(1, peers, send, 0)
    recv_obs[0] = compact(me)

    total = mine
    for k in range(1, GROUP):
        scales_copies[k - 1].wait_recv()
        total = total + scales_in[k]
    scale_space, scale_time = total[0:1, :], total[1:2, :]
    for copy in swap_copies:
        copy.wait_recv()
    for half, values in enumerate(put([(swap_in[k], behind[k]) for k in range(GROUP)], by_time)):
        turned[half * HALF : (half + 1) * HALF, :] = values.astype(BF16)
    kappa_cols = jnp.transpose(kappa[...])
    eye = iota((BLOCK, BLOCK), 0) == iota((BLOCK, BLOCK), 1)
    for b in range(NB_DEV):
        part = slice(b * BLOCK, (b + 1) * BLOCK)
        sdiag = jnp.sum(jnp.where(eye, diag[b].astype(F32), 0.0), axis=1, keepdims=True)
        kappa_col = kappa_cols[:, b : b + 1]
        base = scale_space * sdiag + 2.0 * scale_time + kappa_col
        step[part, :] = base
        local_diag[part, :] = jnp.broadcast_to(kappa_col, (BLOCK, COLS))
        start = RELAX * turned[part, :].astype(F32) / base
        fine[part, :] = start
        field[0, part, :] = start.astype(BF16)

    for e in range(EXCHANGES):

        @pl.when(jnp.logical_not(has_down))
        def _():
            field[e, NODES_DEV : NODES_DEV + HALO_ROWS, :] = jnp.zeros((HALO_ROWS, COLS), BF16)

        @pl.when(jnp.logical_not(has_up))
        def _():
            field[e, NODES_DEV + HALO_ROWS :, :] = jnp.zeros((HALO_ROWS, COLS), BF16)

    for there, later in ((has_left, time_low), (has_right, time_high)):

        @pl.when(jnp.logical_not(there))
        def _():
            later[...] = jnp.zeros_like(later)

    for copy in needs_copies:
        copy.wait()
    for i in range(HALO_B):
        for b in range(NB_DEV):
            for side, row in ((1, i), (0, HALO_B + i)):
                picks[side, i, b] = mark(needs_in[side, row : row + 1, :] == b)

    def pack(e, first, shift):
        packed = jnp.zeros((BLOCK, BLOCK), F32)
        for b in range(NB_DEV):
            edge = field[e, b * BLOCK : (b + 1) * BLOCK, first : first + BLOCK].astype(F32)
            moved = pltpu.roll(edge, (shift + b * THIN) % BLOCK, 1)
            packed = jnp.where(lanes // THIN == b, moved, packed)
        return packed.astype(BF16)

    def time_copies(e):
        return both_ways(
            send_right.at[e],
            send_left.at[e],
            time_low.at[e],
            time_high.at[e],
            pair(time_send_sem, e),
            pair(time_recv_sem, e),
        )

    def start_time(e):
        send_right[e] = pack(e, COLS - BLOCK, THIN)
        send_left[e] = pack(e, 0, 0)
        start_copies(time_copies(e))

    def space_copies(e):
        copies = []
        for which, sends, receives, src, offset, target in (
            (0, has_up, has_down, send_up, 0, up),
            (1, has_down, has_up, send_down, HALO_ROWS, down),
        ):
            copy = pltpu.make_async_remote_copy(
                src_ref=src.at[e],
                dst_ref=field.at[e, pl.ds(NODES_DEV + offset, HALO_ROWS)],
                send_sem=space_send_sem.at[e, which],
                recv_sem=space_recv_sem.at[e, which],
                device_id=(target, slab),
                device_id_type=MESH,
            )
            copies.append((sends, receives, copy))
        return copies

    def start_space(e):
        for i in range(HALO_B):
            part = slice(i * BLOCK, (i + 1) * BLOCK)
            for side, staged in ((1, send_up), (0, send_down)):
                chosen = picks[side, i, 0] * field[e, :BLOCK, :]
                for b in range(1, NB_DEV):
                    chosen = chosen + picks[side, i, b] * field[e, b * BLOCK : (b + 1) * BLOCK, :]
                staged[e, part, :] = chosen
        start_copies(space_copies(e))

    start_space(0)
    start_time(0)

    loads[9].wait()
    loads[10].wait()

    def combine(i, carry):
        b = i // NB_DEV
        rows = pl.ds(pl.multiple_of((i % NB_DEV) * 16, 16), 16)
        parts = [off[b, k, rows, :].astype(F32) for k in range(NB_DEV)]
        own = diag[b, rows, :].astype(F32)
        columns = [cols[b, k] for k in range(NB_DEV)]
        place = pl.ds(pl.multiple_of(i * 16, 16), 16)
        for m in range(WIDTH // BLOCK):
            total = jnp.zeros((16, BLOCK), F32)
            for k in range(NB_DEV):
                total = total + jnp.where(columns[k] == m, 1.0, 0.0) * parts[k]
            if m < NB_DEV:
                total = total + jnp.where(b == m, 1.0, 0.0) * own
            comb[place, m * BLOCK : (m + 1) * BLOCK] = total.astype(BF16)
        return carry

    lax.fori_loop(0, NODES_DEV // 16, combine, 0)

    row_t, lane_t = iota((COLS, COLS), 0), iota((COLS, COLS), 1)
    inner = jnp.where(
        row_t == lane_t, 2.0, jnp.where(jnp.abs(row_t - lane_t) == THIN, -1.0, 0.0)
    ).astype(BF16)
    def own_product(e):
        product[...] = dot(comb[:, :NODES_DEV], field[e, :NODES_DEV, :])

    def both(e, part):
        space = product[part, :] + dot(comb[part, NODES_DEV:], field[e, NODES_DEV:, :])
        return space, dot(field[e, part, :], inner)

    def parts():
        for c in range(CHUNKS):
            yield c, slice(c * CHUNK, (c + 1) * CHUNK)

    def beside_term(e, b):
        low, high = time_low[e].astype(F32), time_high[e].astype(F32)
        first = pltpu.roll(low, (BLOCK - b * THIN) % BLOCK, 1)
        last = pltpu.roll(high, (BLOCK - THIN - b * THIN) % BLOCK, 1)
        return jnp.concatenate(
            [jnp.where(lanes < THIN, first, 0.0), jnp.where(lanes >= BLOCK - THIN, last, 0.0)], axis=1
        )

    def beside_terms(e, c):
        return jnp.concatenate([beside_term(e, c * 2), beside_term(e, c * 2 + 1)], axis=0)

    def sweep(e):
        for c, part in parts():
            space, time = both(e, part)
            applied = (
                scale_space * space
                + scale_time * (time - beside_terms(e, c))
                + local_diag[part, :] * field[e, part, :].astype(F32)
            )
            solved = fine[part, :] + step[part, :] * (turned[part, :].astype(F32) - applied)
            fine[part, :] = solved
            field[e + 1, part, :] = solved.astype(BF16)

    own_product(0)

    loads[11].wait()
    counted[...] = jnp.zeros((NODES_DEV, BLOCK), F32)
    row_w = iota((BLOCK, cap), 0)

    def weigh(k):
        digits = recv_obs[k, NCOV:, :].astype(F32)
        live = digits[2:3, :] > 0.5
        number = (digits[0:1, :] * 64.0 + digits[1:2, :]).astype(jnp.int32)
        node = jnp.where(live, number // T_DEV, -1)
        time = number % T_DEV
        rows = recv_obs[k, :NCOV, :]
        eta = jnp.zeros((1, cap), F32)
        for c in range(NODES_DEV // CHUNK):
            part = slice(c * CHUNK, (c + 1) * CHUNK)
            scores = dot(coef[part, :], rows)
            found = iota((CHUNK, cap), 0) + c * CHUNK == node
            eta = eta + jnp.sum(jnp.where(found, scores, 0.0), axis=0, keepdims=True)
            masks[part, :] = mark(found)
        weight = jnp.where(live, jnp.exp(eta), 0.0)
        pieces = [piece.astype(F32) for piece in split3(weight)]
        spread = jnp.zeros((BLOCK, cap), F32)
        for i, piece in enumerate(pieces):
            spread = jnp.where(row_w == time + i * T_DEV, piece, spread)
        counted[...] += lax.dot_general(
            masks[...], spread.astype(BF16), NT_DIMS, preferred_element_type=F32
        )

    weigh(0)

    def receive(k, carry):
        obs_copy(k, lax.rem(me + k, peers)).wait_recv()
        weigh(k)
        return carry

    lax.fori_loop(1, peers, receive, 0)

    packed = jnp.zeros((BLOCK, BLOCK), F32)
    for b in range(NB_DEV):
        held = counted[b * BLOCK : (b + 1) * BLOCK, :]
        held = held + pltpu.roll(held, BLOCK - T_DEV, 1) + pltpu.roll(held, BLOCK - 2 * T_DEV, 1)
        packed = jnp.where(lanes // T_DEV == b, pltpu.roll(held, b * T_DEV, 1), packed)
    sums_out[...] = jnp.transpose(packed)[:CELLS, :]
    sums_in[place, :] = sums_out[...]
    for copy in sums_copies:
        copy.start()
    for copy in sums_copies:
        copy.wait_recv()
    pieces = split3(jnp.transpose(sums_in[...]))
    for b in range(NB_DEV):
        part = slice(b * BLOCK, (b + 1) * BLOCK)
        cell_of = (high_wide // PROBES) * CELLS + b * T_DEV + (high_wide // THIN) % T_DEV
        repeat = mark(low_tall == cell_of)
        obs_diag = dot(pieces[0], repeat) + dot(pieces[1], repeat) + dot(pieces[2], repeat)
        local_diag[part, :] = local_diag[part, :] + obs_diag
        step[part, :] = RELAX / (step[part, :] + obs_diag)

    for e in range(ITERS):
        wait_arrivals(space_copies(e))
        wait_arrivals(time_copies(e))
        sweep(e)
        start_space(e + 1)
        start_time(e + 1)
        if e < ITERS - 1:
            own_product(e + 1)

    for k in range(1, GROUP):
        back_out[k] = take(field.at[ITERS, pl.ds(0, NODES_DEV)], by_time, lax.rem(turn + k, GROUP))
        back_copies[k - 1].start()
    own_product(ITERS)
    kept = take(field.at[ITERS, pl.ds(0, NODES_DEV)], by_time, turn)
    for _, part in parts():
        rest = fine[part, :] - field[ITERS, part, :].astype(F32)
        residual[part, :] = rest.astype(BF16)
    small = take(residual, by_time, turn)
    wait_arrivals(space_copies(ITERS))
    wait_arrivals(time_copies(ITERS))
    sums = [jnp.zeros((1, COLS), F32), jnp.zeros((1, COLS), F32)]
    for c, part in parts():
        values = turned[part, :].astype(F32)
        space, time = both(ITERS, part)
        for i, term in enumerate((space, time - beside_terms(ITERS, c))):
            sums[i] = sums[i] + jnp.sum(values * term, axis=0, keepdims=True)
    run_out[...] = jnp.where(sub8 == 0, sums[0], jnp.where(sub8 == 1, sums[1], 0.0))
    run_in[0] = run_out[...]
    run_copies = [
        group_copy(k, run_out, run_in.at[k], run_send_sem, run_recv_sem) for k in range(1, GROUP)
    ]
    for copy in run_copies:
        copy.start()
    for copy in run_copies:
        copy.wait_recv()
    total = jnp.zeros((8, COLS), F32)
    for k in range(GROUP):
        chosen = (lane_t // THIN) % GROUP == behind[k]
        moved = mark(chosen & (row_t == turn * PROBES + (lane_t // PROBES) * THIN + lane_t % THIN))
        for piece in split3(run_in[k]):
            total = total + dot(piece, moved)
    grads_out[...] = total
    grads_in[me] = grads_out[...]

    def grads_copy(k):
        target = lax.rem(me + k, peers)
        return pltpu.make_async_remote_copy(
            src_ref=grads_out,
            dst_ref=grads_in.at[me],
            send_sem=grads_send_sem.at[k],
            recv_sem=grads_recv_sem.at[k],
            device_id=(target, slab),
            device_id_type=MESH,
        )

    def grads_send(k, carry):
        grads_copy(k).start()
        return carry

    lax.fori_loop(1, peers, grads_send, 0)

    def finish(k, carry):
        grads_copy(k).wait()
        obs_copy(k, lax.rem(me + k, peers)).wait_send()
        return carry

    lax.fori_loop(1, peers, finish, 0)
    for e in range(EXCHANGES):
        wait_departures(space_copies(e))
        wait_departures(time_copies(e))
    for copy in scales_copies + swap_copies + sums_copies + run_copies + back_copies:
        copy.wait_send()
    for copy in back_copies:
        copy.wait_recv()
    parted = [(kept, turn), (small, turn)] + [(back_in[k], behind[k]) for k in range(1, GROUP)]
    for half, values in enumerate(put(parted, by_probe)):
        sol_ref[half * HALF : (half + 1) * HALF, :] = values
    total = grads_in[0]
    for s in range(1, peers):
        total = total + grads_in[s]
    grads_ref[...] = total[0:2, :] / (NODES_DEV * peers)


def shards(
    probe_field,
    kappa,
    theta_space,
    theta_time,
    diag_blocks,
    off_blocks,
    block_cols,
    halo_needs,
    covariates,
    obs_owner,
    obs_cell,
    svc_coef,
):
    peers = lax.axis_size("space")
    slabs = lax.axis_size("tm")
    cap = 2 * OBS_DEV // peers
    vmem = pl.BlockSpec(memory_space=pltpu.VMEM)
    dma = pltpu.SemaphoreType.DMA
    return pl.pallas_call(
        functools.partial(kernel, peers, slabs, cap),
        out_shape=(
            jax.ShapeDtypeStruct((NODES_DEV, COLS), F32),
            jax.ShapeDtypeStruct((2, COLS), F32),
        ),
        in_specs=[pl.BlockSpec(memory_space=pltpu.HBM)] * 12,
        out_specs=(vmem, vmem),
        scratch_shapes=[
            pltpu.VMEM((NODES_DEV, COLS), BF16),
            pltpu.VMEM((NB_DEV, BLOCK), F32),
            pltpu.SMEM((T_DEV,), F32),
            pltpu.SMEM((T_DEV,), F32),
            pltpu.VMEM((NB_DEV, BLOCK, BLOCK), BF16),
            pltpu.VMEM((NB_DEV, NB_DEV, BLOCK, BLOCK), BF16),
            pltpu.SMEM((NB_DEV, NB_DEV), jnp.int32),
            pltpu.SMEM((2 * HALO_B,), jnp.int32),
            pltpu.VMEM((OBS_DEV, NCOV), BF16),
            pltpu.VMEM((OBS_DEV // BLOCK, BLOCK), jnp.int32),
            pltpu.VMEM((OBS_DEV // BLOCK, BLOCK), jnp.int32),
            pltpu.VMEM((NODES_DEV, NCOV), BF16),
            pltpu.VMEM((OBS_DEV, BLOCK), jnp.int32),
            pltpu.VMEM((ROWS, OBS_DEV), BF16),
            pltpu.VMEM((OBS_DEV, cap), BF16),
            pltpu.VMEM((peers, ROWS, cap), BF16),
            pltpu.VMEM((peers, ROWS, cap), BF16),
            pltpu.VMEM((NODES_DEV, cap), BF16),
            pltpu.VMEM((NODES_DEV, BLOCK), F32),
            pltpu.VMEM((NODES_DEV, WIDTH), BF16),
            pltpu.VMEM((EXCHANGES, WIDTH, COLS), BF16),
            pltpu.VMEM((EXCHANGES, BLOCK, BLOCK), BF16),
            pltpu.VMEM((EXCHANGES, BLOCK, BLOCK), BF16),
            pltpu.VMEM((EXCHANGES, HALO_ROWS, COLS), BF16),
            pltpu.VMEM((EXCHANGES, HALO_ROWS, COLS), BF16),
            pltpu.VMEM((EXCHANGES, BLOCK, BLOCK), BF16),
            pltpu.VMEM((EXCHANGES, BLOCK, BLOCK), BF16),
            pltpu.VMEM((NODES_DEV, COLS), F32),
            pltpu.VMEM((NODES_DEV, COLS), BF16),
            pltpu.VMEM((NODES_DEV, COLS), F32),
            pltpu.VMEM((NODES_DEV, COLS), BF16),
            pltpu.VMEM((GROUP, HALF, BLOCK), BF16),
            pltpu.VMEM((GROUP, HALF, BLOCK), BF16),
            pltpu.VMEM((GROUP, HALF, BLOCK), BF16),
            pltpu.VMEM((GROUP, HALF, BLOCK), BF16),
            pltpu.VMEM((8, COLS), F32),
            pltpu.VMEM((GROUP, 8, COLS), F32),
            pltpu.VMEM((CELLS, BLOCK), F32),
            pltpu.VMEM((GROUP * CELLS, BLOCK), F32),
            pltpu.VMEM((8, COLS), jnp.int32),
            pltpu.VMEM((2, 8, COLS), jnp.int32),
            pltpu.VMEM((2, HALO_B, NB_DEV, 1, COLS), BF16),
            pltpu.VMEM((NODES_DEV, COLS), F32),
            pltpu.VMEM((NODES_DEV, COLS), F32),
            pltpu.VMEM((8, COLS), F32),
            pltpu.VMEM((GROUP, 8, COLS), F32),
            pltpu.VMEM((8, COLS), F32),
            pltpu.VMEM((peers, 8, COLS), F32),
            dma((12,)),
            dma((peers,)),
            dma((peers,)),
            dma((2,)),
            dma((2,)),
            dma((EXCHANGES, 2)),
            dma((EXCHANGES, 2)),
            dma((EXCHANGES, 2)),
            dma((EXCHANGES, 2)),
            dma((GROUP,)),
            dma((GROUP,)),
            dma((GROUP,)),
            dma((GROUP,)),
            dma((GROUP,)),
            dma((GROUP,)),
            dma((GROUP,)),
            dma((GROUP,)),
            dma((GROUP,)),
            dma((GROUP,)),
            dma((peers,)),
            dma((peers,)),
        ],
        compiler_params=pltpu.CompilerParams(
            collective_id=0,
            has_side_effects=True,
            vmem_limit_bytes=60 * 1024 * 1024,
        ),
    )(
        probe_field,
        kappa.reshape(NB_DEV, BLOCK),
        theta_space,
        theta_time,
        diag_blocks,
        off_blocks,
        block_cols,
        halo_needs,
        covariates,
        obs_owner.reshape(OBS_DEV // BLOCK, BLOCK),
        obs_cell.reshape(OBS_DEV // BLOCK, BLOCK),
        svc_coef,
    )


def solution(mesh):
    return jax.shard_map(
        shards,
        mesh=mesh,
        in_specs=(
            P("space", "tm"),
            P("space"),
            P("tm"),
            P("tm"),
            P("space", None, None),
            P("space", None, None, None),
            P("space", None),
            P("space"),
            P(("space", "tm"), None),
            P(("space", "tm"), None),
            P(("space", "tm")),
            P("space", None),
        ),
        out_specs=(P("space", "tm"), P(None, "tm")),
        check_vma=False,
    )
```

```python
import functools

import jax
import jax.numpy as jnp
from jax import lax
from jax.experimental import pallas as pl
from jax.experimental.pallas import tpu as pltpu
from jax.sharding import PartitionSpec as P

NB_DEV = 8
BLOCK = 128
HALO_B = 2
T_DEV = 4
PROBES = 64
NCOV = 256
OBS_DEV = 2048
ITERS = 4
NODES_DEV = 1024
COLS = T_DEV * PROBES
WIDTH = (NB_DEV + 2 * HALO_B) * BLOCK
HALO_ROWS = HALO_B * BLOCK
ROWS = NCOV + 16
EXCHANGES = ITERS + 1
CHUNK = 256
CHUNKS = NODES_DEV // CHUNK
GROUP = 4
THIN = PROBES // GROUP
HALF = NODES_DEV // 2
CELLS = NB_DEV * T_DEV

RELAX = 0.6
MESH = pl.DeviceIdType.MESH
F32 = jnp.float32
BF16 = jnp.bfloat16
NT_DIMS = (((1,), (1,)), ((), ()))


def dot(a, b):
    return jnp.dot(a, b, preferred_element_type=F32)


def iota(shape, dim):
    return lax.broadcasted_iota(jnp.int32, shape, dim)


def mark(condition):
    return jnp.where(condition, 1.0, 0.0).astype(BF16)


def split3(values):
    first = jnp.clip(values, -3.38e38, 3.38e38).astype(BF16)
    rest = values - first.astype(F32)
    second = rest.astype(BF16)
    third = (rest - second.astype(F32)).astype(BF16)
    return first, second, third


def kernel(
    peers,
    slabs,
    cap,
    probe_hbm,
    kappa_hbm,
    theta_space_hbm,
    theta_time_hbm,
    diag_hbm,
    off_hbm,
    cols_hbm,
    needs_hbm,
    cov_hbm,
    owner_hbm,
    cell_hbm,
    coef_hbm,
    sol_ref,
    grads_ref,
    probe,
    kappa,
    theta_space,
    theta_time,
    diag,
    off,
    cols,
    needs,
    cov,
    owner,
    cell,
    coef,
    slots,
    covt,
    onehot,
    send_obs,
    recv_obs,
    masks,
    counted,
    comb,
    field,
    time_low,
    time_high,
    send_up,
    send_down,
    send_left,
    send_right,
    product,
    residual,
    fine,
    turned,
    swap_out,
    swap_in,
    back_out,
    back_in,
    scales_out,
    scales_in,
    sums_out,
    sums_in,
    needs_out,
    needs_in,
    picks,
    local_diag,
    step,
    run_out,
    run_in,
    grads_out,
    grads_in,
    load_sem,
    obs_send_sem,
    obs_recv_sem,
    needs_send_sem,
    needs_recv_sem,
    space_send_sem,
    space_recv_sem,
    time_send_sem,
    time_recv_sem,
    swap_send_sem,
    swap_recv_sem,
    back_send_sem,
    back_recv_sem,
    scales_send_sem,
    scales_recv_sem,
    sums_send_sem,
    sums_recv_sem,
    run_send_sem,
    run_recv_sem,
    coef_send_sem,
    coef_recv_sem,
    grads_send_sem,
    grads_recv_sem,
):
    me = lax.axis_index("space")
    slab = lax.axis_index("tm")
    turn = lax.rem(slab, GROUP)
    run = slab - turn
    left = lax.rem(slab + slabs - GROUP, slabs)
    right = lax.rem(slab + GROUP, slabs)
    down = lax.rem(me + peers - 1, peers)
    up = lax.rem(me + 1, peers)
    depth = lax.rem(me // 2, 2)
    spot = (me // 4) * 2 + lax.rem(me, 2)
    spots = peers // 2
    partner = me + 2 - 4 * depth
    has_down, has_up = me > 0, me < peers - 1
    has_left, has_right = run > 0, run < slabs - GROUP

    pairs = (
        (owner_hbm, owner),
        (cov_hbm, cov),
        (cell_hbm, cell),
        (needs_hbm, needs),
        (probe_hbm, probe),
        (kappa_hbm, kappa),
        (theta_space_hbm, theta_space),
        (theta_time_hbm, theta_time),
        (diag_hbm, diag),
        (off_hbm, off),
        (cols_hbm, cols),
        (coef_hbm, coef.at[0]),
    )
    loads = [
        pltpu.make_async_copy(src, dst, load_sem.at[i]) for i, (src, dst) in enumerate(pairs)
    ]
    for load in loads:
        load.start()

    barrier = pltpu.get_barrier_semaphore()

    def greet(k, carry):
        pl.semaphore_signal(
            barrier, inc=1, device_id=(lax.rem(me + k, peers), slab), device_id_type=MESH
        )
        return carry

    lax.fori_loop(1, peers, greet, 0)
    ahead = [run + lax.rem(turn + k, GROUP) for k in range(GROUP)]
    behind = [lax.rem(turn + GROUP - k, GROUP) for k in range(GROUP)]
    across = run + lax.rem(turn + GROUP - 1 + 2 * depth, GROUP)
    for other in (left, right, *ahead[1:]):
        pl.semaphore_signal(barrier, inc=1, device_id=(me, other), device_id_type=MESH)
    for other in ahead[1:]:
        pl.semaphore_signal(barrier, inc=1, device_id=(partner, other), device_id_type=MESH)

    loads[0].wait()
    owner_cols = jnp.transpose(owner[...].astype(F32))
    lanes = iota((BLOCK, BLOCK), 1)
    below = mark(iota((BLOCK, BLOCK), 1) < iota((BLOCK, BLOCK), 0))
    seen = jnp.zeros((1, BLOCK), F32)
    for c in range(OBS_DEV // BLOCK):
        owner_col = owner_cols[:, c : c + 1].astype(jnp.int32)
        hit = owner_col == lanes
        hits = mark(hit)
        before = dot(below, hits) + seen
        rank = jnp.sum(jnp.where(hit, before, 0.0), axis=1, keepdims=True)
        seen = seen + jnp.sum(hits.astype(F32), axis=0, keepdims=True)
        slot = owner_col * cap + rank.astype(jnp.int32)
        slots[c * BLOCK : (c + 1) * BLOCK, :] = jnp.broadcast_to(slot, (BLOCK, BLOCK))

    loads[1].wait()
    loads[2].wait()
    sub = iota((16, BLOCK), 0)
    for c in range(OBS_DEV // BLOCK):
        part = slice(c * BLOCK, (c + 1) * BLOCK)
        covt[:NCOV, part] = jnp.transpose(cov[part, :])
        row = jnp.broadcast_to(cell[c : c + 1, :], (16, BLOCK))
        extra = jnp.where(
            sub == 0, row // 64, jnp.where(sub == 1, row % 64, jnp.where(sub == 2, 1, 0))
        )
        covt[NCOV:, part] = extra.astype(F32).astype(BF16)

    def compact(target):
        for c in range(OBS_DEV // BLOCK):
            part = slice(c * BLOCK, (c + 1) * BLOCK)
            place = slots[part, :] - target * cap
            for h in range(0, cap, BLOCK):
                onehot[part, h : h + BLOCK] = mark(place == lanes + h)
        return dot(covt[...], onehot[...]).astype(BF16)

    for i in (8, 9, 10):
        loads[i].wait()

    def combine(i, carry):
        b = i // NB_DEV
        rows = pl.ds(pl.multiple_of((i % NB_DEV) * 16, 16), 16)
        parts = [off[b, k, rows, :].astype(F32) for k in range(NB_DEV)]
        own = diag[b, rows, :].astype(F32)
        columns = [cols[b, k] for k in range(NB_DEV)]
        place = pl.ds(pl.multiple_of(i * 16, 16), 16)
        for m in range(WIDTH // BLOCK):
            total = jnp.zeros((16, BLOCK), F32)
            for k in range(NB_DEV):
                total = total + jnp.where(columns[k] == m, 1.0, 0.0) * parts[k]
            if m < NB_DEV:
                total = total + jnp.where(b == m, 1.0, 0.0) * own
            comb[place, m * BLOCK : (m + 1) * BLOCK] = total.astype(BF16)
        return carry

    lax.fori_loop(0, NODES_DEV // 16, combine, 0)

    pl.semaphore_wait(barrier, peers + 2 * GROUP - 1)

    loads[3].wait()
    sub8 = iota((8, COLS), 0)
    listed = jnp.zeros((8, COLS), jnp.int32)
    for i in range(2 * HALO_B):
        listed = jnp.where(sub8 == i, needs[i], listed)
    needs_out[...] = listed

    def needs_copy(side, target):
        return pltpu.make_async_remote_copy(
            src_ref=needs_out,
            dst_ref=needs_in.at[side],
            send_sem=needs_send_sem.at[side],
            recv_sem=needs_recv_sem.at[side],
            device_id=(target, slab),
            device_id_type=MESH,
        )

    needs_copies = (needs_copy(0, up), needs_copy(1, down))
    for copy in needs_copies:
        copy.start()

    for i in range(4, 8):
        loads[i].wait()
    col = iota((8, COLS), 1)
    sub8 = iota((8, COLS), 0)
    mine = jnp.zeros((8, COLS), F32)
    for t in range(T_DEV):
        here = (col // PROBES == turn) & ((col // THIN) % T_DEV == t)
        mine = jnp.where(here & (sub8 == 0), theta_space[t], mine)
        mine = jnp.where(here & (sub8 == 1), theta_time[t], mine)
    scales_out[...] = mine

    def group_copy(k, src, dst, send_sem, recv_sem):
        return pltpu.make_async_remote_copy(
            src_ref=src,
            dst_ref=dst,
            send_sem=send_sem.at[k],
            recv_sem=recv_sem.at[k],
            device_id=(me, ahead[k]),
            device_id_type=MESH,
        )

    scales_copies = [
        group_copy(k, scales_out, scales_in.at[k], scales_send_sem, scales_recv_sem) for k in range(1, GROUP)
    ]
    swap_copies = [
        group_copy(k, swap_out.at[k], swap_in.at[k], swap_send_sem, swap_recv_sem) for k in range(1, GROUP)
    ]
    back_copies = [
        group_copy(k, back_out.at[k], back_in.at[k], back_send_sem, back_recv_sem) for k in range(1, GROUP)
    ]
    place = pl.ds(pl.multiple_of(turn * CELLS, CELLS), CELLS)
    sums_copies = [
        group_copy(k, sums_out.at[0], sums_in.at[0, place], sums_send_sem, sums_recv_sem)
        for k in range(1, GROUP)
    ]
    for k in range(GROUP):
        sums_copies.append(
            pltpu.make_async_remote_copy(
                src_ref=sums_out.at[1],
                dst_ref=sums_in.at[1, place],
                send_sem=sums_send_sem.at[GROUP + k],
                recv_sem=sums_recv_sem.at[GROUP + k],
                device_id=(partner, ahead[k]),
                device_id_type=MESH,
            )
        )

    tall, wide = (iota((COLS, BLOCK), i) for i in range(2))
    low_tall, high_wide = (iota((BLOCK, COLS), i) for i in range(2))

    def by_probe(lane, which):
        return (lane // THIN) * PROBES + which * THIN + lane % THIN

    def by_time(lane, which):
        return which * PROBES + lane

    def take(source, order, which):
        left_half = mark((wide < PROBES) & (tall == order(wide, which)))
        right_half = mark((wide >= PROBES) & (tall == order(wide - PROBES, which)))
        return (dot(source[:HALF, :], left_half) + dot(source[HALF:, :], right_half)).astype(BF16)

    def put(terms, order):
        halves = [jnp.zeros((HALF, COLS), F32), jnp.zeros((HALF, COLS), F32)]
        for value, which in terms:
            for half in range(2):
                lane = low_tall - half * PROBES
                keep = (low_tall // PROBES == half) & (high_wide == order(lane, which))
                halves[half] = halves[half] + dot(value, mark(keep))
        return halves

    swap_in[0] = take(probe, by_probe, turn)
    for k in range(1, GROUP):
        swap_out[k] = take(probe, by_probe, lax.rem(turn + k, GROUP))
    for copy in scales_copies + swap_copies:
        copy.start()

    loads[11].wait()
    coef_copies = []
    for i, target in enumerate((slab, across)):
        rows = pl.ds(i * HALF, HALF)
        coef_copies.append(
            pltpu.make_async_remote_copy(
                src_ref=coef.at[0, rows],
                dst_ref=coef.at[1, rows],
                send_sem=coef_send_sem.at[i],
                recv_sem=coef_recv_sem.at[i],
                device_id=(partner, target),
                device_id_type=MESH,
            )
        )
    for copy in coef_copies:
        copy.start()

    def beside(sends, receives, src, dst, send_sem, recv_sem, target):
        copy = pltpu.make_async_remote_copy(
            src_ref=src,
            dst_ref=dst,
            send_sem=send_sem,
            recv_sem=recv_sem,
            device_id=(me, target),
            device_id_type=MESH,
        )
        return sends, receives, copy

    def both_ways(src_right, src_left, dst_low, dst_high, send_sems, recv_sems):
        return (
            beside(has_right, has_left, src_right, dst_low, send_sems[0], recv_sems[0], right),
            beside(has_left, has_right, src_left, dst_high, send_sems[1], recv_sems[1], left),
        )

    def pair(sems, *index):
        return [sems.at[*index, which] for which in range(2)]

    def start_copies(copies):
        for sends, _, copy in copies:
            pl.when(sends)(copy.start)

    def wait_arrivals(copies):
        for _, receives, copy in copies:
            pl.when(receives)(copy.wait_recv)

    def wait_departures(copies):
        for sends, _, copy in copies:
            pl.when(sends)(copy.wait_send)


    def obs_copy(k, target):
        return pltpu.make_async_remote_copy(
            src_ref=send_obs.at[k],
            dst_ref=recv_obs.at[k],
            send_sem=obs_send_sem.at[k],
            recv_sem=obs_recv_sem.at[k],
            device_id=(target, slab),
            device_id_type=MESH,
        )

    def place_of(i):
        other = lax.rem(spot + i // 2, spots)
        return (other // 2) * 4 + lax.rem(other, 2)

    def owner_of(i):
        return place_of(i) + 2 * lax.rem(depth + i, 2)

    def target_of(i):
        return place_of(i) + 2 * depth

    def send(i, carry):
        send_obs[i] = compact(owner_of(i))
        obs_copy(i, target_of(i)).start()
        return carry

    lax.fori_loop(2, peers, send, 0)
    for i in range(2):
        recv_obs[i] = compact(owner_of(i))

    total = mine
    for k in range(1, GROUP):
        scales_copies[k - 1].wait_recv()
        total = total + scales_in[k]
    scale_space, scale_time = total[0:1, :], total[1:2, :]
    for copy in swap_copies:
        copy.wait_recv()
    for half, values in enumerate(put([(swap_in[k], behind[k]) for k in range(GROUP)], by_time)):
        turned[half * HALF : (half + 1) * HALF, :] = values.astype(BF16)
    kappa_cols = jnp.transpose(kappa[...])
    eye = iota((BLOCK, BLOCK), 0) == iota((BLOCK, BLOCK), 1)
    for b in range(NB_DEV):
        part = slice(b * BLOCK, (b + 1) * BLOCK)
        sdiag = jnp.sum(jnp.where(eye, diag[b].astype(F32), 0.0), axis=1, keepdims=True)
        kappa_col = kappa_cols[:, b : b + 1]
        base = scale_space * sdiag + 2.0 * scale_time + kappa_col
        step[part, :] = base
        local_diag[part, :] = jnp.broadcast_to(kappa_col, (BLOCK, COLS))
        start = RELAX * turned[part, :].astype(F32) / base
        fine[part, :] = start
        field[0, part, :] = start.astype(BF16)

    for e in range(EXCHANGES):

        @pl.when(jnp.logical_not(has_down))
        def _():
            field[e, NODES_DEV : NODES_DEV + HALO_ROWS, :] = jnp.zeros((HALO_ROWS, COLS), BF16)

        @pl.when(jnp.logical_not(has_up))
        def _():
            field[e, NODES_DEV + HALO_ROWS :, :] = jnp.zeros((HALO_ROWS, COLS), BF16)

    for there, later in ((has_left, time_low), (has_right, time_high)):

        @pl.when(jnp.logical_not(there))
        def _():
            later[...] = jnp.zeros_like(later)

    for copy in needs_copies:
        copy.wait()
    for i in range(HALO_B):
        for b in range(NB_DEV):
            for side, row in ((1, i), (0, HALO_B + i)):
                picks[side, i, b] = mark(needs_in[side, row : row + 1, :] == b)

    def pack(e, first, shift):
        packed = jnp.zeros((BLOCK, BLOCK), F32)
        for b in range(NB_DEV):
            edge = field[e, b * BLOCK : (b + 1) * BLOCK, first : first + BLOCK].astype(F32)
            moved = pltpu.roll(edge, (shift + b * THIN) % BLOCK, 1)
            packed = jnp.where(lanes // THIN == b, moved, packed)
        return packed.astype(BF16)

    def time_copies(e):
        return both_ways(
            send_right.at[e],
            send_left.at[e],
            time_low.at[e],
            time_high.at[e],
            pair(time_send_sem, e),
            pair(time_recv_sem, e),
        )

    def start_time(e):
        send_right[e] = pack(e, COLS - BLOCK, THIN)
        send_left[e] = pack(e, 0, 0)
        start_copies(time_copies(e))

    def space_copies(e):
        copies = []
        for which, sends, receives, src, offset, target in (
            (0, has_up, has_down, send_up, 0, up),
            (1, has_down, has_up, send_down, HALO_ROWS, down),
        ):
            copy = pltpu.make_async_remote_copy(
                src_ref=src.at[e],
                dst_ref=field.at[e, pl.ds(NODES_DEV + offset, HALO_ROWS)],
                send_sem=space_send_sem.at[e, which],
                recv_sem=space_recv_sem.at[e, which],
                device_id=(target, slab),
                device_id_type=MESH,
            )
            copies.append((sends, receives, copy))
        return copies

    def start_space(e):
        for i in range(HALO_B):
            part = slice(i * BLOCK, (i + 1) * BLOCK)
            for side, staged in ((1, send_up), (0, send_down)):
                chosen = picks[side, i, 0] * field[e, :BLOCK, :]
                for b in range(1, NB_DEV):
                    chosen = chosen + picks[side, i, b] * field[e, b * BLOCK : (b + 1) * BLOCK, :]
                staged[e, part, :] = chosen
        start_copies(space_copies(e))

    start_space(0)
    start_time(0)

    row_t, lane_t = iota((COLS, COLS), 0), iota((COLS, COLS), 1)
    inner = jnp.where(
        row_t == lane_t, 2.0, jnp.where(jnp.abs(row_t - lane_t) == THIN, -1.0, 0.0)
    ).astype(BF16)
    def own_product(e):
        product[...] = dot(comb[:, :NODES_DEV], field[e, :NODES_DEV, :])

    def both(e, part):
        space = product[part, :] + dot(comb[part, NODES_DEV:], field[e, NODES_DEV:, :])
        return space, dot(field[e, part, :], inner)

    def parts():
        for c in range(CHUNKS):
            yield c, slice(c * CHUNK, (c + 1) * CHUNK)

    def beside_term(e, b):
        low, high = time_low[e].astype(F32), time_high[e].astype(F32)
        first = pltpu.roll(low, (BLOCK - b * THIN) % BLOCK, 1)
        last = pltpu.roll(high, (BLOCK - THIN - b * THIN) % BLOCK, 1)
        return jnp.concatenate(
            [jnp.where(lanes < THIN, first, 0.0), jnp.where(lanes >= BLOCK - THIN, last, 0.0)], axis=1
        )

    def beside_terms(e, c):
        return jnp.concatenate([beside_term(e, c * 2), beside_term(e, c * 2 + 1)], axis=0)

    def sweep(e):
        for c, part in parts():
            space, time = both(e, part)
            applied = (
                scale_space * space
                + scale_time * (time - beside_terms(e, c))
                + local_diag[part, :] * field[e, part, :].astype(F32)
            )
            solved = fine[part, :] + step[part, :] * (turned[part, :].astype(F32) - applied)
            fine[part, :] = solved
            field[e + 1, part, :] = solved.astype(BF16)

    own_product(0)

    counted[...] = jnp.zeros_like(counted)
    for copy in coef_copies:
        copy.wait_recv()
    row_w = iota((BLOCK, cap), 0)

    def weigh(k):
        which = lax.rem(k, 2)
        digits = recv_obs[k, NCOV:, :].astype(F32)
        live = digits[2:3, :] > 0.5
        number = (digits[0:1, :] * 64.0 + digits[1:2, :]).astype(jnp.int32)
        node = jnp.where(live, number // T_DEV, -1)
        time = number % T_DEV
        rows = recv_obs[k, :NCOV, :]
        eta = jnp.zeros((1, cap), F32)
        for c in range(NODES_DEV // CHUNK):
            part = slice(c * CHUNK, (c + 1) * CHUNK)
            scores = dot(coef[which, part, :], rows)
            found = iota((CHUNK, cap), 0) + c * CHUNK == node
            eta = eta + jnp.sum(jnp.where(found, scores, 0.0), axis=0, keepdims=True)
            masks[part, :] = mark(found)
        weight = jnp.where(live, jnp.exp(eta), 0.0)
        pieces = [piece.astype(F32) for piece in split3(weight)]
        spread = jnp.zeros((BLOCK, cap), F32)
        for i, piece in enumerate(pieces):
            spread = jnp.where(row_w == time + i * T_DEV, piece, spread)
        counted[which] += lax.dot_general(
            masks[...], spread.astype(BF16), NT_DIMS, preferred_element_type=F32
        )

    weigh(0)
    weigh(1)

    def receive(k, carry):
        obs_copy(k, target_of(k)).wait_recv()
        weigh(k)
        return carry

    lax.fori_loop(2, peers, receive, 0)

    for which in range(2):
        packed = jnp.zeros((BLOCK, BLOCK), F32)
        for b in range(NB_DEV):
            held = counted[which, b * BLOCK : (b + 1) * BLOCK, :]
            held = held + pltpu.roll(held, BLOCK - T_DEV, 1) + pltpu.roll(held, BLOCK - 2 * T_DEV, 1)
            packed = jnp.where(lanes // T_DEV == b, pltpu.roll(held, b * T_DEV, 1), packed)
        sums_out[which] = jnp.transpose(packed)[:CELLS, :]
    for copy in sums_copies:
        copy.start()
    sums_in[0, place, :] = sums_out[0]
    for copy in sums_copies:
        copy.wait_recv()
    pieces = split3(jnp.transpose(sums_in[0] + sums_in[1]))
    for b in range(NB_DEV):
        part = slice(b * BLOCK, (b + 1) * BLOCK)
        cell_of = (high_wide // PROBES) * CELLS + b * T_DEV + (high_wide // THIN) % T_DEV
        repeat = mark(low_tall == cell_of)
        obs_diag = dot(pieces[0], repeat) + dot(pieces[1], repeat) + dot(pieces[2], repeat)
        local_diag[part, :] = local_diag[part, :] + obs_diag
        step[part, :] = RELAX / (step[part, :] + obs_diag)

    for e in range(ITERS):
        wait_arrivals(space_copies(e))
        wait_arrivals(time_copies(e))
        sweep(e)
        start_space(e + 1)
        start_time(e + 1)
        if e < ITERS - 1:
            own_product(e + 1)

    for k in range(1, GROUP):
        back_out[k] = take(field.at[ITERS, pl.ds(0, NODES_DEV)], by_time, lax.rem(turn + k, GROUP))
        back_copies[k - 1].start()
    own_product(ITERS)
    kept = take(field.at[ITERS, pl.ds(0, NODES_DEV)], by_time, turn)
    for _, part in parts():
        rest = fine[part, :] - field[ITERS, part, :].astype(F32)
        residual[part, :] = rest.astype(BF16)
    small = take(residual, by_time, turn)
    wait_arrivals(space_copies(ITERS))
    wait_arrivals(time_copies(ITERS))
    sums = [jnp.zeros((1, COLS), F32), jnp.zeros((1, COLS), F32)]
    for c, part in parts():
        values = turned[part, :].astype(F32)
        space, time = both(ITERS, part)
        for i, term in enumerate((space, time - beside_terms(ITERS, c))):
            sums[i] = sums[i] + jnp.sum(values * term, axis=0, keepdims=True)
    run_out[...] = jnp.where(sub8 == 0, sums[0], jnp.where(sub8 == 1, sums[1], 0.0))
    run_in[0] = run_out[...]
    run_copies = [
        group_copy(k, run_out, run_in.at[k], run_send_sem, run_recv_sem) for k in range(1, GROUP)
    ]
    for copy in run_copies:
        copy.start()
    for copy in run_copies:
        copy.wait_recv()
    total = jnp.zeros((8, COLS), F32)
    for k in range(GROUP):
        chosen = (lane_t // THIN) % GROUP == behind[k]
        moved = mark(chosen & (row_t == turn * PROBES + (lane_t // PROBES) * THIN + lane_t % THIN))
        for piece in split3(run_in[k]):
            total = total + dot(piece, moved)
    grads_out[...] = total
    grads_in[me] = grads_out[...]

    def grads_copy(k):
        target = lax.rem(me + k, peers)
        return pltpu.make_async_remote_copy(
            src_ref=grads_out,
            dst_ref=grads_in.at[me],
            send_sem=grads_send_sem.at[k],
            recv_sem=grads_recv_sem.at[k],
            device_id=(target, slab),
            device_id_type=MESH,
        )

    def grads_send(k, carry):
        grads_copy(k).start()
        return carry

    lax.fori_loop(1, peers, grads_send, 0)

    def finish(k, carry):
        grads_copy(k).wait()
        return carry

    lax.fori_loop(1, peers, finish, 0)

    def sent(i, carry):
        obs_copy(i, target_of(i)).wait_send()
        return carry

    lax.fori_loop(2, peers, sent, 0)
    for e in range(EXCHANGES):
        wait_departures(space_copies(e))
        wait_departures(time_copies(e))
    for copy in scales_copies + swap_copies + coef_copies + sums_copies + run_copies + back_copies:
        copy.wait_send()
    for copy in back_copies:
        copy.wait_recv()
    parted = [(kept, turn), (small, turn)] + [(back_in[k], behind[k]) for k in range(1, GROUP)]
    for half, values in enumerate(put(parted, by_probe)):
        sol_ref[half * HALF : (half + 1) * HALF, :] = values
    total = grads_in[0]
    for s in range(1, peers):
        total = total + grads_in[s]
    grads_ref[...] = total[0:2, :] / (NODES_DEV * peers)


def shards(
    probe_field,
    kappa,
    theta_space,
    theta_time,
    diag_blocks,
    off_blocks,
    block_cols,
    halo_needs,
    covariates,
    obs_owner,
    obs_cell,
    svc_coef,
):
    peers = lax.axis_size("space")
    slabs = lax.axis_size("tm")
    cap = 2 * OBS_DEV // peers
    vmem = pl.BlockSpec(memory_space=pltpu.VMEM)
    dma = pltpu.SemaphoreType.DMA
    return pl.pallas_call(
        functools.partial(kernel, peers, slabs, cap),
        out_shape=(
            jax.ShapeDtypeStruct((NODES_DEV, COLS), F32),
            jax.ShapeDtypeStruct((2, COLS), F32),
        ),
        in_specs=[pl.BlockSpec(memory_space=pltpu.HBM)] * 12,
        out_specs=(vmem, vmem),
        scratch_shapes=[
            pltpu.VMEM((NODES_DEV, COLS), BF16),
            pltpu.VMEM((NB_DEV, BLOCK), F32),
            pltpu.SMEM((T_DEV,), F32),
            pltpu.SMEM((T_DEV,), F32),
            pltpu.VMEM((NB_DEV, BLOCK, BLOCK), BF16),
            pltpu.VMEM((NB_DEV, NB_DEV, BLOCK, BLOCK), BF16),
            pltpu.SMEM((NB_DEV, NB_DEV), jnp.int32),
            pltpu.SMEM((2 * HALO_B,), jnp.int32),
            pltpu.VMEM((OBS_DEV, NCOV), BF16),
            pltpu.VMEM((OBS_DEV // BLOCK, BLOCK), jnp.int32),
            pltpu.VMEM((OBS_DEV // BLOCK, BLOCK), jnp.int32),
            pltpu.VMEM((2, NODES_DEV, NCOV), BF16),
            pltpu.VMEM((OBS_DEV, BLOCK), jnp.int32),
            pltpu.VMEM((ROWS, OBS_DEV), BF16),
            pltpu.VMEM((OBS_DEV, cap), BF16),
            pltpu.VMEM((peers, ROWS, cap), BF16),
            pltpu.VMEM((peers, ROWS, cap), BF16),
            pltpu.VMEM((NODES_DEV, cap), BF16),
            pltpu.VMEM((2, NODES_DEV, BLOCK), F32),
            pltpu.VMEM((NODES_DEV, WIDTH), BF16),
            pltpu.VMEM((EXCHANGES, WIDTH, COLS), BF16),
            pltpu.VMEM((EXCHANGES, BLOCK, BLOCK), BF16),
            pltpu.VMEM((EXCHANGES, BLOCK, BLOCK), BF16),
            pltpu.VMEM((EXCHANGES, HALO_ROWS, COLS), BF16),
            pltpu.VMEM((EXCHANGES, HALO_ROWS, COLS), BF16),
            pltpu.VMEM((EXCHANGES, BLOCK, BLOCK), BF16),
            pltpu.VMEM((EXCHANGES, BLOCK, BLOCK), BF16),
            pltpu.VMEM((NODES_DEV, COLS), F32),
            pltpu.VMEM((NODES_DEV, COLS), BF16),
            pltpu.VMEM((NODES_DEV, COLS), F32),
            pltpu.VMEM((NODES_DEV, COLS), BF16),
            pltpu.VMEM((GROUP, HALF, BLOCK), BF16),
            pltpu.VMEM((GROUP, HALF, BLOCK), BF16),
            pltpu.VMEM((GROUP, HALF, BLOCK), BF16),
            pltpu.VMEM((GROUP, HALF, BLOCK), BF16),
            pltpu.VMEM((8, COLS), F32),
            pltpu.VMEM((GROUP, 8, COLS), F32),
            pltpu.VMEM((2, CELLS, BLOCK), F32),
            pltpu.VMEM((2, GROUP * CELLS, BLOCK), F32),
            pltpu.VMEM((8, COLS), jnp.int32),
            pltpu.VMEM((2, 8, COLS), jnp.int32),
            pltpu.VMEM((2, HALO_B, NB_DEV, 1, COLS), BF16),
            pltpu.VMEM((NODES_DEV, COLS), F32),
            pltpu.VMEM((NODES_DEV, COLS), F32),
            pltpu.VMEM((8, COLS), F32),
            pltpu.VMEM((GROUP, 8, COLS), F32),
            pltpu.VMEM((8, COLS), F32),
            pltpu.VMEM((peers, 8, COLS), F32),
            dma((12,)),
            dma((peers,)),
            dma((peers,)),
            dma((2,)),
            dma((2,)),
            dma((EXCHANGES, 2)),
            dma((EXCHANGES, 2)),
            dma((EXCHANGES, 2)),
            dma((EXCHANGES, 2)),
            dma((GROUP,)),
            dma((GROUP,)),
            dma((GROUP,)),
            dma((GROUP,)),
            dma((GROUP,)),
            dma((GROUP,)),
            dma((2 * GROUP,)),
            dma((2 * GROUP,)),
            dma((GROUP,)),
            dma((GROUP,)),
            dma((2,)),
            dma((2,)),
            dma((peers,)),
            dma((peers,)),
        ],
        compiler_params=pltpu.CompilerParams(
            collective_id=0,
            has_side_effects=True,
            vmem_limit_bytes=60 * 1024 * 1024,
        ),
    )(
        probe_field,
        kappa.reshape(NB_DEV, BLOCK),
        theta_space,
        theta_time,
        diag_blocks,
        off_blocks,
        block_cols,
        halo_needs,
        covariates,
        obs_owner.reshape(OBS_DEV // BLOCK, BLOCK),
        obs_cell.reshape(OBS_DEV // BLOCK, BLOCK),
        svc_coef,
    )


def solution(mesh):
    return jax.shard_map(
        shards,
        mesh=mesh,
        in_specs=(
            P("space", "tm"),
            P("space"),
            P("tm"),
            P("tm"),
            P("space", None, None),
            P("space", None, None, None),
            P("space", None),
            P("space"),
            P(("space", "tm"), None),
            P(("space", "tm"), None),
            P(("space", "tm")),
            P("space", None),
        ),
        out_specs=(P("space", "tm"), P(None, "tm")),
        check_vma=False,
    )
```

```python
import functools

import jax
import jax.numpy as jnp
from jax import lax
from jax.experimental import pallas as pl
from jax.experimental.pallas import tpu as pltpu
from jax.sharding import PartitionSpec as P

NB_DEV = 8
BLOCK = 128
HALO_B = 2
T_DEV = 4
PROBES = 64
NCOV = 256
OBS_DEV = 2048
ITERS = 4
NODES_DEV = 1024
COLS = T_DEV * PROBES
WIDTH = (NB_DEV + 2 * HALO_B) * BLOCK
HALO_ROWS = HALO_B * BLOCK
ROWS = NCOV + 16
EXCHANGES = ITERS + 1
CHUNK = 256
CHUNKS = NODES_DEV // CHUNK
GROUP = 4
HALF = NODES_DEV // 2
CELLS = NB_DEV * T_DEV

RELAX = 0.6
MESH = pl.DeviceIdType.MESH
F32 = jnp.float32
BF16 = jnp.bfloat16
NT_DIMS = (((1,), (1,)), ((), ()))


def dot(a, b):
    return jnp.dot(a, b, preferred_element_type=F32)


def iota(shape, dim):
    return lax.broadcasted_iota(jnp.int32, shape, dim)


def mark(condition):
    return jnp.where(condition, 1.0, 0.0).astype(BF16)


def split3(values):
    first = jnp.clip(values, -3.38e38, 3.38e38).astype(BF16)
    rest = values - first.astype(F32)
    second = rest.astype(BF16)
    third = (rest - second.astype(F32)).astype(BF16)
    return first, second, third


def kernel(
    peers,
    slabs,
    cap,
    probe_hbm,
    kappa_hbm,
    theta_space_hbm,
    theta_time_hbm,
    diag_hbm,
    off_hbm,
    cols_hbm,
    needs_hbm,
    cov_hbm,
    owner_hbm,
    cell_hbm,
    coef_hbm,
    sol_ref,
    grads_ref,
    probe,
    kappa,
    theta_space,
    theta_time,
    diag,
    off,
    cols,
    needs,
    cov,
    owner,
    cell,
    coef,
    slots,
    covt,
    onehot,
    send_obs,
    recv_obs,
    masks,
    counted,
    comb,
    field,
    first_low,
    first_high,
    time_low,
    time_high,
    send_up,
    send_down,
    send_left,
    send_right,
    product,
    residual,
    edges_out,
    edges_in,
    cross_out,
    cross_in,
    local_diag,
    step,
    needs_out,
    needs_in,
    picks,
    sums_out,
    sums_in,
    grads_out,
    grads_in,
    load_sem,
    obs_send_sem,
    obs_recv_sem,
    needs_send_sem,
    needs_recv_sem,
    space_send_sem,
    space_recv_sem,
    time_send_sem,
    time_recv_sem,
    edges_send_sem,
    edges_recv_sem,
    cross_send_sem,
    cross_recv_sem,
    grads_send_sem,
    grads_recv_sem,
    coef_send_sem,
    coef_recv_sem,
    sums_send_sem,
    sums_recv_sem,
):
    me = lax.axis_index("space")
    slab = lax.axis_index("tm")
    left = lax.rem(slab + slabs - 1, slabs)
    right = lax.rem(slab + 1, slabs)
    down = lax.rem(me + peers - 1, peers)
    up = lax.rem(me + 1, peers)
    depth = lax.rem(me // 2, 2)
    spot = (me // 4) * 2 + lax.rem(me, 2)
    spots = peers // 2
    partner = me + 2 - 4 * depth
    turn = lax.rem(slab, GROUP)
    across = slab - turn + lax.rem(turn + GROUP - 1 + 2 * depth, GROUP)
    has_down, has_up = me > 0, me < peers - 1
    has_left, has_right = slab > 0, slab < slabs - 1

    pairs = (
        (owner_hbm, owner),
        (cov_hbm, cov),
        (cell_hbm, cell),
        (needs_hbm, needs),
        (probe_hbm, probe),
        (kappa_hbm, kappa),
        (theta_space_hbm, theta_space),
        (theta_time_hbm, theta_time),
        (diag_hbm, diag),
        (off_hbm, off),
        (cols_hbm, cols),
        (coef_hbm, coef.at[0]),
    )
    loads = [
        pltpu.make_async_copy(src, dst, load_sem.at[i]) for i, (src, dst) in enumerate(pairs)
    ]
    for load in loads:
        load.start()

    barrier = pltpu.get_barrier_semaphore()

    def greet(k, carry):
        pl.semaphore_signal(
            barrier, inc=1, device_id=(lax.rem(me + k, peers), slab), device_id_type=MESH
        )
        return carry

    lax.fori_loop(1, peers, greet, 0)
    for target in ((me, left), (me, right), (partner, across)):
        pl.semaphore_signal(barrier, inc=1, device_id=target, device_id_type=MESH)

    loads[0].wait()
    owner_cols = jnp.transpose(owner[...].astype(F32))
    lanes = iota((BLOCK, BLOCK), 1)
    below = mark(iota((BLOCK, BLOCK), 1) < iota((BLOCK, BLOCK), 0))
    seen = jnp.zeros((1, BLOCK), F32)
    for c in range(OBS_DEV // BLOCK):
        owner_col = owner_cols[:, c : c + 1].astype(jnp.int32)
        hit = owner_col == lanes
        hits = mark(hit)
        before = dot(below, hits) + seen
        rank = jnp.sum(jnp.where(hit, before, 0.0), axis=1, keepdims=True)
        seen = seen + jnp.sum(hits.astype(F32), axis=0, keepdims=True)
        slot = owner_col * cap + rank.astype(jnp.int32)
        slots[c * BLOCK : (c + 1) * BLOCK, :] = jnp.broadcast_to(slot, (BLOCK, BLOCK))

    loads[1].wait()
    loads[2].wait()
    sub = iota((16, BLOCK), 0)
    for c in range(OBS_DEV // BLOCK):
        part = slice(c * BLOCK, (c + 1) * BLOCK)
        covt[:NCOV, part] = jnp.transpose(cov[part, :])
        row = jnp.broadcast_to(cell[c : c + 1, :], (16, BLOCK))
        extra = jnp.where(
            sub == 0, row // 64, jnp.where(sub == 1, row % 64, jnp.where(sub == 2, 1, 0))
        )
        covt[NCOV:, part] = extra.astype(F32).astype(BF16)

    def compact(target):
        for c in range(OBS_DEV // BLOCK):
            part = slice(c * BLOCK, (c + 1) * BLOCK)
            place = slots[part, :] - target * cap
            for h in range(0, cap, BLOCK):
                onehot[part, h : h + BLOCK] = mark(place == lanes + h)
        return dot(covt[...], onehot[...]).astype(BF16)

    for i in (8, 9, 10):
        loads[i].wait()

    def combine(i, carry):
        b = i // NB_DEV
        rows = pl.ds(pl.multiple_of((i % NB_DEV) * 16, 16), 16)
        parts = [off[b, k, rows, :].astype(F32) for k in range(NB_DEV)]
        own = diag[b, rows, :].astype(F32)
        columns = [cols[b, k] for k in range(NB_DEV)]
        place = pl.ds(pl.multiple_of(i * 16, 16), 16)
        for m in range(WIDTH // BLOCK):
            total = jnp.zeros((16, BLOCK), F32)
            for k in range(NB_DEV):
                total = total + jnp.where(columns[k] == m, 1.0, 0.0) * parts[k]
            if m < NB_DEV:
                total = total + jnp.where(b == m, 1.0, 0.0) * own
            comb[place, m * BLOCK : (m + 1) * BLOCK] = total.astype(BF16)
        return carry

    lax.fori_loop(0, NODES_DEV // 16, combine, 0)

    pl.semaphore_wait(barrier, peers + 2)

    loads[3].wait()
    sub8 = iota((8, COLS), 0)
    listed = jnp.zeros((8, COLS), jnp.int32)
    for i in range(2 * HALO_B):
        listed = jnp.where(sub8 == i, needs[i], listed)
    needs_out[...] = listed

    def needs_copy(side, target):
        return pltpu.make_async_remote_copy(
            src_ref=needs_out,
            dst_ref=needs_in.at[side],
            send_sem=needs_send_sem.at[side],
            recv_sem=needs_recv_sem.at[side],
            device_id=(target, slab),
            device_id_type=MESH,
        )

    needs_copies = (needs_copy(0, up), needs_copy(1, down))
    for copy in needs_copies:
        copy.start()

    for i in range(4, 8):
        loads[i].wait()
    sub_e = iota((8, BLOCK), 0)
    ends = (theta_space[T_DEV - 1], theta_time[T_DEV - 1], theta_space[0], theta_time[0])
    scales = jnp.ones((8, BLOCK), F32)
    for i, value in enumerate(ends):
        scales = jnp.where(sub_e == i, value, scales)
    edges_out[...] = scales

    def beside(sends, receives, src, dst, send_sem, recv_sem, target):
        copy = pltpu.make_async_remote_copy(
            src_ref=src,
            dst_ref=dst,
            send_sem=send_sem,
            recv_sem=recv_sem,
            device_id=(me, target),
            device_id_type=MESH,
        )
        return sends, receives, copy

    def both_ways(src_right, src_left, dst_low, dst_high, send_sems, recv_sems):
        return (
            beside(has_right, has_left, src_right, dst_low, send_sems[0], recv_sems[0], right),
            beside(has_left, has_right, src_left, dst_high, send_sems[1], recv_sems[1], left),
        )

    def pair(sems, *index):
        return [sems.at[*index, which] for which in range(2)]

    edge_copies = both_ways(
        edges_out, edges_out, edges_in.at[0], edges_in.at[1], pair(edges_send_sem), pair(edges_recv_sem)
    )

    def start_copies(copies):
        for sends, _, copy in copies:
            pl.when(sends)(copy.start)

    def wait_arrivals(copies):
        for _, receives, copy in copies:
            pl.when(receives)(copy.wait_recv)

    def wait_departures(copies):
        for sends, _, copy in copies:
            pl.when(sends)(copy.wait_send)

    start_copies(edge_copies)

    loads[11].wait()
    coef_copies = []
    for i, target in enumerate((slab, across)):
        rows = pl.ds(i * HALF, HALF)
        coef_copies.append(
            pltpu.make_async_remote_copy(
                src_ref=coef.at[0, rows],
                dst_ref=coef.at[1, rows],
                send_sem=coef_send_sem.at[i],
                recv_sem=coef_recv_sem.at[i],
                device_id=(partner, target),
                device_id_type=MESH,
            )
        )
    for copy in coef_copies:
        copy.start()
    sums_copy = pltpu.make_async_remote_copy(
        src_ref=sums_out,
        dst_ref=sums_in.at[pl.ds(0, CELLS)],
        send_sem=sums_send_sem,
        recv_sem=sums_recv_sem,
        device_id=(partner, slab),
        device_id_type=MESH,
    )
    sums_in[CELLS:, :] = jnp.zeros((BLOCK - CELLS, BLOCK), F32)

    def obs_copy(k, target):
        return pltpu.make_async_remote_copy(
            src_ref=send_obs.at[k],
            dst_ref=recv_obs.at[k],
            send_sem=obs_send_sem.at[k],
            recv_sem=obs_recv_sem.at[k],
            device_id=(target, slab),
            device_id_type=MESH,
        )

    def place_of(i):
        other = lax.rem(spot + i // 2, spots)
        return (other // 2) * 4 + lax.rem(other, 2)

    def owner_of(i):
        return place_of(i) + 2 * lax.rem(depth + i, 2)

    def target_of(i):
        return place_of(i) + 2 * depth

    def send(i, carry):
        send_obs[i] = compact(owner_of(i))
        obs_copy(i, target_of(i)).start()
        return carry

    lax.fori_loop(2, peers, send, 0)
    for i in range(2):
        recv_obs[i] = compact(owner_of(i))

    col_time = iota((1, COLS), 1) // PROBES
    scale_space = jnp.zeros((1, COLS), F32)
    scale_time = jnp.zeros((1, COLS), F32)
    for t in range(T_DEV):
        scale_space = jnp.where(col_time == t, theta_space[t], scale_space)
        scale_time = jnp.where(col_time == t, theta_time[t], scale_time)
    kappa_cols = jnp.transpose(kappa[...])
    eye = iota((BLOCK, BLOCK), 0) == iota((BLOCK, BLOCK), 1)
    sdiag_cols = []
    for b in range(NB_DEV):
        part = slice(b * BLOCK, (b + 1) * BLOCK)
        sdiag = jnp.sum(jnp.where(eye, diag[b].astype(F32), 0.0), axis=1, keepdims=True)
        sdiag_cols.append(sdiag)
        kappa_col = kappa_cols[:, b : b + 1]
        base = scale_space * sdiag + 2.0 * scale_time + kappa_col
        step[part, :] = base
        local_diag[part, :] = jnp.broadcast_to(kappa_col, (BLOCK, COLS))
        start = RELAX * probe[part, :].astype(F32) / base
        sol_ref[part, :] = start
        field[0, part, :] = start.astype(BF16)

    for e in range(EXCHANGES):

        @pl.when(jnp.logical_not(has_down))
        def _():
            field[e, NODES_DEV : NODES_DEV + HALO_ROWS, :] = jnp.zeros((HALO_ROWS, COLS), BF16)

        @pl.when(jnp.logical_not(has_up))
        def _():
            field[e, NODES_DEV + HALO_ROWS :, :] = jnp.zeros((HALO_ROWS, COLS), BF16)

    for there, side, first, later in ((has_left, 0, first_low, time_low), (has_right, 1, first_high, time_high)):

        @pl.when(jnp.logical_not(there))
        def _():
            first[...] = jnp.zeros_like(first)
            later[...] = jnp.zeros_like(later)
            edges_in[side] = jnp.ones((8, BLOCK), F32)
            cross_in[side] = jnp.zeros((8, BLOCK), F32)

    for copy in needs_copies:
        copy.wait()
    for i in range(HALO_B):
        for b in range(NB_DEV):
            for side, row in ((1, i), (0, HALO_B + i)):
                picks[side, i, b] = mark(needs_in[side, row : row + 1, :] == b)

    lower_half = lanes < PROBES

    def pack_last(values):
        return jnp.where(
            lower_half, pltpu.roll(values[:BLOCK, BLOCK:], PROBES, 1), values[BLOCK:, BLOCK:]
        )

    def pack_first(values):
        return jnp.where(
            lower_half, values[:BLOCK, :BLOCK], pltpu.roll(values[BLOCK:, :BLOCK], PROBES, 1)
        )

    def time_copies(e, c):
        lows, highs = (first_low, first_high) if e == 0 else (time_low.at[e], time_high.at[e])
        return both_ways(
            send_right.at[e, c],
            send_left.at[e, c],
            lows.at[c],
            highs.at[c],
            pair(time_send_sem, e, c),
            pair(time_recv_sem, e, c),
        )

    def start_time(e, c, values):
        send_right[e, c] = pack_last(values).astype(BF16)
        send_left[e, c] = pack_first(values).astype(BF16)
        start_copies(time_copies(e, c))

    def space_copies(e):
        copies = []
        for which, sends, receives, src, offset, target in (
            (0, has_up, has_down, send_up, 0, up),
            (1, has_down, has_up, send_down, HALO_ROWS, down),
        ):
            copy = pltpu.make_async_remote_copy(
                src_ref=src.at[e],
                dst_ref=field.at[e, pl.ds(NODES_DEV + offset, HALO_ROWS)],
                send_sem=space_send_sem.at[e, which],
                recv_sem=space_recv_sem.at[e, which],
                device_id=(target, slab),
                device_id_type=MESH,
            )
            copies.append((sends, receives, copy))
        return copies

    def start_space(e):
        for i in range(HALO_B):
            part = slice(i * BLOCK, (i + 1) * BLOCK)
            for side, staged in ((1, send_up), (0, send_down)):
                chosen = picks[side, i, 0] * field[e, :BLOCK, :]
                for b in range(1, NB_DEV):
                    chosen = chosen + picks[side, i, b] * field[e, b * BLOCK : (b + 1) * BLOCK, :]
                staged[e, part, :] = chosen
        start_copies(space_copies(e))

    start_space(0)
    for c in range(CHUNKS):
        start_time(0, c, probe[c * CHUNK : (c + 1) * CHUNK, :].astype(F32))

    row_t, lane_t = iota((COLS, COLS), 0), iota((COLS, COLS), 1)
    inner = jnp.where(
        row_t == lane_t, 2.0, jnp.where(jnp.abs(row_t - lane_t) == PROBES, -1.0, 0.0)
    ).astype(BF16)
    def own_product(e):
        product[...] = dot(comb[:, :NODES_DEV], field[e, :NODES_DEV, :])

    def both(e, part):
        space = product[part, :] + dot(comb[part, NODES_DEV:], field[e, NODES_DEV:, :])
        return space, dot(field[e, part, :], inner)

    def parts():
        for c in range(CHUNKS):
            yield c, slice(c * CHUNK, (c + 1) * CHUNK)

    def inner_residual(e):
        for _, part in parts():
            space, time = both(e, part)
            applied = (
                scale_space * space
                + scale_time * time
                + local_diag[part, :] * field[e, part, :].astype(F32)
            )
            residual[part, :] = probe[part, :].astype(F32) - applied

    def update(e, c, part):
        low, high = time_low[e, c].astype(F32), time_high[e, c].astype(F32)
        first = scale_time[:, :BLOCK] * jnp.concatenate(
            [jnp.where(lower_half, low, 0.0), jnp.where(lower_half, pltpu.roll(low, PROBES, 1), 0.0)], axis=0
        )
        last = scale_time[:, BLOCK:] * jnp.concatenate(
            [jnp.where(lower_half, 0.0, pltpu.roll(high, PROBES, 1)), jnp.where(lower_half, 0.0, high)], axis=0
        )
        left_over = residual[part, :] + jnp.concatenate([first, last], axis=1)
        solved = sol_ref[part, :] + step[part, :] * left_over
        sol_ref[part, :] = solved
        field[e + 1, part, :] = solved.astype(BF16)
        return solved

    own_product(0)

    counted[...] = jnp.zeros_like(counted)
    for copy in coef_copies:
        copy.wait_recv()
    row_w = iota((BLOCK, cap), 0)

    def weigh(k):
        which = lax.rem(k, 2)
        digits = recv_obs[k, NCOV:, :].astype(F32)
        live = digits[2:3, :] > 0.5
        number = (digits[0:1, :] * 64.0 + digits[1:2, :]).astype(jnp.int32)
        node = jnp.where(live, number // T_DEV, -1)
        time = number % T_DEV
        rows = recv_obs[k, :NCOV, :]
        eta = jnp.zeros((1, cap), F32)
        for c in range(NODES_DEV // CHUNK):
            part = slice(c * CHUNK, (c + 1) * CHUNK)
            scores = dot(coef[which, part, :], rows)
            found = iota((CHUNK, cap), 0) + c * CHUNK == node
            eta = eta + jnp.sum(jnp.where(found, scores, 0.0), axis=0, keepdims=True)
            masks[part, :] = mark(found)
        weight = jnp.where(live, jnp.exp(eta), 0.0)
        pieces = [piece.astype(F32) for piece in split3(weight)]
        spread = jnp.zeros((BLOCK, cap), F32)
        for i, piece in enumerate(pieces):
            spread = jnp.where(row_w == time + i * T_DEV, piece, spread)
        counted[which] += lax.dot_general(
            masks[...], spread.astype(BF16), NT_DIMS, preferred_element_type=F32
        )

    weigh(0)
    weigh(1)

    def receive(k, carry):
        obs_copy(k, target_of(k)).wait_recv()
        weigh(k)
        return carry

    lax.fori_loop(2, peers, receive, 0)

    def pack_sums(which):
        packed = jnp.zeros((BLOCK, BLOCK), F32)
        for b in range(NB_DEV):
            held = counted[which, b * BLOCK : (b + 1) * BLOCK, :]
            held = held + pltpu.roll(held, BLOCK - T_DEV, 1) + pltpu.roll(held, BLOCK - 2 * T_DEV, 1)
            packed = jnp.where(lanes // T_DEV == b, pltpu.roll(held, b * T_DEV, 1), packed)
        return packed

    sums_out[...] = jnp.transpose(pack_sums(1))[:CELLS, :]
    sums_copy.start()
    own_sums = pack_sums(0)

    wait_arrivals(edge_copies)
    for c in range(CHUNKS):
        wait_arrivals(time_copies(0, c))
        lo, hi = 2 * c, 2 * c + 1
        sdiag = jnp.where(lower_half, sdiag_cols[lo], sdiag_cols[hi])
        nugget = jnp.where(lower_half, kappa_cols[:, lo : lo + 1], kappa_cols[:, hi : hi + 1])
        for side, row, first, later in ((0, 0, first_low, time_low), (1, 2, first_high, time_high)):
            base = edges_in[side, row : row + 1, :] * sdiag + 2.0 * edges_in[side, row + 1 : row + 2, :] + nugget
            later[0, c] = (RELAX * first[c].astype(F32) / base).astype(BF16)

    sums_copy.wait_recv()
    pieces = split3(own_sums + jnp.transpose(sums_in[...]))
    cell_row, cell_col = iota((BLOCK, COLS), 0), iota((BLOCK, COLS), 1) // PROBES
    for b in range(NB_DEV):
        part = slice(b * BLOCK, (b + 1) * BLOCK)
        repeat = mark(cell_row == b * T_DEV + cell_col)
        obs_diag = dot(pieces[0], repeat) + dot(pieces[1], repeat) + dot(pieces[2], repeat)
        local_diag[part, :] = local_diag[part, :] + obs_diag
        step[part, :] = RELAX / (step[part, :] + obs_diag)

    crossed = [jnp.zeros((1, BLOCK), F32), jnp.zeros((1, BLOCK), F32)]
    for e in range(ITERS):
        wait_arrivals(space_copies(e))
        inner_residual(e)
        for c, part in parts():
            if e > 0:
                wait_arrivals(time_copies(e, c))
            solved = update(e, c, part)
            if e < ITERS - 1:
                start_time(e + 1, c, solved)
            else:
                rounded = solved.astype(BF16).astype(F32)
                for i, packed, there in ((0, pack_last(rounded), first_high), (1, pack_first(rounded), first_low)):
                    terms = packed * there[c].astype(F32)
                    crossed[i] = crossed[i] + jnp.sum(terms, axis=0, keepdims=True)
        start_space(e + 1)
        if e < ITERS - 1:
            own_product(e + 1)

    for i in range(2):
        cross_out[i] = jnp.broadcast_to(crossed[i], (8, BLOCK))
    cross_copies = both_ways(
        cross_out.at[0],
        cross_out.at[1],
        cross_in.at[0],
        cross_in.at[1],
        pair(cross_send_sem),
        pair(cross_recv_sem),
    )
    start_copies(cross_copies)
    own_product(ITERS)
    wait_arrivals(space_copies(ITERS))
    sums = [jnp.zeros((1, COLS), F32), jnp.zeros((1, COLS), F32)]
    for _, part in parts():
        values = probe[part, :].astype(F32)
        for i, term in enumerate(both(ITERS, part)):
            sums[i] = sums[i] + jnp.sum(values * term, axis=0, keepdims=True)
    wait_arrivals(cross_copies)
    folded = [cross_in[i] + pltpu.roll(cross_in[i], PROBES, 1) for i in range(2)]
    low8 = iota((8, BLOCK), 1) < PROBES
    owed = jnp.concatenate([jnp.where(low8, folded[0], 0.0), jnp.where(low8, 0.0, folded[1])], axis=1)
    sums[1] = sums[1] - owed[0:1, :]
    grads_out[...] = jnp.where(sub8 == 0, sums[0], jnp.where(sub8 == 1, sums[1], 0.0))
    grads_in[me] = grads_out[...]

    def grads_copy(k):
        target = lax.rem(me + k, peers)
        return pltpu.make_async_remote_copy(
            src_ref=grads_out,
            dst_ref=grads_in.at[me],
            send_sem=grads_send_sem.at[k],
            recv_sem=grads_recv_sem.at[k],
            device_id=(target, slab),
            device_id_type=MESH,
        )

    def grads_send(k, carry):
        grads_copy(k).start()
        return carry

    lax.fori_loop(1, peers, grads_send, 0)

    def finish(k, carry):
        grads_copy(k).wait()
        return carry

    lax.fori_loop(1, peers, finish, 0)

    def sent(i, carry):
        obs_copy(i, target_of(i)).wait_send()
        return carry

    lax.fori_loop(2, peers, sent, 0)
    sums_copy.wait_send()
    for copy in coef_copies:
        copy.wait_send()
    wait_departures(edge_copies)
    wait_departures(cross_copies)
    for e in range(EXCHANGES):
        wait_departures(space_copies(e))
        if e < ITERS:
            for c in range(CHUNKS):
                wait_departures(time_copies(e, c))
    total = grads_in[0]
    for s in range(1, peers):
        total = total + grads_in[s]
    grads_ref[...] = total[0:2, :] / (NODES_DEV * peers)


def shards(
    probe_field,
    kappa,
    theta_space,
    theta_time,
    diag_blocks,
    off_blocks,
    block_cols,
    halo_needs,
    covariates,
    obs_owner,
    obs_cell,
    svc_coef,
):
    peers = lax.axis_size("space")
    slabs = lax.axis_size("tm")
    cap = 2 * OBS_DEV // peers
    vmem = pl.BlockSpec(memory_space=pltpu.VMEM)
    dma = pltpu.SemaphoreType.DMA
    return pl.pallas_call(
        functools.partial(kernel, peers, slabs, cap),
        out_shape=(
            jax.ShapeDtypeStruct((NODES_DEV, COLS), F32),
            jax.ShapeDtypeStruct((2, COLS), F32),
        ),
        in_specs=[pl.BlockSpec(memory_space=pltpu.HBM)] * 12,
        out_specs=(vmem, vmem),
        scratch_shapes=[
            pltpu.VMEM((NODES_DEV, COLS), BF16),
            pltpu.VMEM((NB_DEV, BLOCK), F32),
            pltpu.SMEM((T_DEV,), F32),
            pltpu.SMEM((T_DEV,), F32),
            pltpu.VMEM((NB_DEV, BLOCK, BLOCK), BF16),
            pltpu.VMEM((NB_DEV, NB_DEV, BLOCK, BLOCK), BF16),
            pltpu.SMEM((NB_DEV, NB_DEV), jnp.int32),
            pltpu.SMEM((2 * HALO_B,), jnp.int32),
            pltpu.VMEM((OBS_DEV, NCOV), BF16),
            pltpu.VMEM((OBS_DEV // BLOCK, BLOCK), jnp.int32),
            pltpu.VMEM((OBS_DEV // BLOCK, BLOCK), jnp.int32),
            pltpu.VMEM((2, NODES_DEV, NCOV), BF16),
            pltpu.VMEM((OBS_DEV, BLOCK), jnp.int32),
            pltpu.VMEM((ROWS, OBS_DEV), BF16),
            pltpu.VMEM((OBS_DEV, cap), BF16),
            pltpu.VMEM((peers, ROWS, cap), BF16),
            pltpu.VMEM((peers, ROWS, cap), BF16),
            pltpu.VMEM((NODES_DEV, cap), BF16),
            pltpu.VMEM((2, NODES_DEV, BLOCK), F32),
            pltpu.VMEM((NODES_DEV, WIDTH), BF16),
            pltpu.VMEM((EXCHANGES, WIDTH, COLS), BF16),
            pltpu.VMEM((CHUNKS, BLOCK, BLOCK), BF16),
            pltpu.VMEM((CHUNKS, BLOCK, BLOCK), BF16),
            pltpu.VMEM((ITERS, CHUNKS, BLOCK, BLOCK), BF16),
            pltpu.VMEM((ITERS, CHUNKS, BLOCK, BLOCK), BF16),
            pltpu.VMEM((EXCHANGES, HALO_ROWS, COLS), BF16),
            pltpu.VMEM((EXCHANGES, HALO_ROWS, COLS), BF16),
            pltpu.VMEM((ITERS, CHUNKS, BLOCK, BLOCK), BF16),
            pltpu.VMEM((ITERS, CHUNKS, BLOCK, BLOCK), BF16),
            pltpu.VMEM((NODES_DEV, COLS), F32),
            pltpu.VMEM((NODES_DEV, COLS), F32),
            pltpu.VMEM((8, BLOCK), F32),
            pltpu.VMEM((2, 8, BLOCK), F32),
            pltpu.VMEM((2, 8, BLOCK), F32),
            pltpu.VMEM((2, 8, BLOCK), F32),
            pltpu.VMEM((NODES_DEV, COLS), F32),
            pltpu.VMEM((NODES_DEV, COLS), F32),
            pltpu.VMEM((8, COLS), jnp.int32),
            pltpu.VMEM((2, 8, COLS), jnp.int32),
            pltpu.VMEM((2, HALO_B, NB_DEV, 1, COLS), BF16),
            pltpu.VMEM((CELLS, BLOCK), F32),
            pltpu.VMEM((BLOCK, BLOCK), F32),
            pltpu.VMEM((8, COLS), F32),
            pltpu.VMEM((peers, 8, COLS), F32),
            dma((12,)),
            dma((peers,)),
            dma((peers,)),
            dma((2,)),
            dma((2,)),
            dma((EXCHANGES, 2)),
            dma((EXCHANGES, 2)),
            dma((ITERS, CHUNKS, 2)),
            dma((ITERS, CHUNKS, 2)),
            dma((2,)),
            dma((2,)),
            dma((2,)),
            dma((2,)),
            dma((peers,)),
            dma((peers,)),
            dma((2,)),
            dma((2,)),
            dma,
            dma,
        ],
        compiler_params=pltpu.CompilerParams(
            collective_id=0,
            has_side_effects=True,
            vmem_limit_bytes=60 * 1024 * 1024,
        ),
    )(
        probe_field,
        kappa.reshape(NB_DEV, BLOCK),
        theta_space,
        theta_time,
        diag_blocks,
        off_blocks,
        block_cols,
        halo_needs,
        covariates,
        obs_owner.reshape(OBS_DEV // BLOCK, BLOCK),
        obs_cell.reshape(OBS_DEV // BLOCK, BLOCK),
        svc_coef,
    )


def solution(mesh):
    return jax.shard_map(
        shards,
        mesh=mesh,
        in_specs=(
            P("space", "tm"),
            P("space"),
            P("tm"),
            P("tm"),
            P("space", None, None),
            P("space", None, None, None),
            P("space", None),
            P("space"),
            P(("space", "tm"), None),
            P(("space", "tm"), None),
            P(("space", "tm")),
            P("space", None),
        ),
        out_specs=(P("space", "tm"), P(None, "tm")),
        check_vma=False,
    )
```

```python
import functools

import jax
import jax.numpy as jnp
from jax import lax
from jax.experimental import pallas as pl
from jax.experimental.pallas import tpu as pltpu
from jax.sharding import PartitionSpec as P

NB_DEV = 8
BLOCK = 128
HALO_B = 2
T_DEV = 4
PROBES = 64
NCOV = 256
OBS_DEV = 2048
ITERS = 4
NODES_DEV = 1024
COLS = T_DEV * PROBES
WIDTH = (NB_DEV + 2 * HALO_B) * BLOCK
HALO_ROWS = HALO_B * BLOCK
ROWS = NCOV + 16
EXCHANGES = ITERS + 1
CHUNK = 256
CHUNKS = NODES_DEV // CHUNK

RELAX = 0.6
MESH = pl.DeviceIdType.MESH
F32 = jnp.float32
BF16 = jnp.bfloat16
NT_DIMS = (((1,), (1,)), ((), ()))


def dot(a, b):
    return jnp.dot(a, b, preferred_element_type=F32)


def iota(shape, dim):
    return lax.broadcasted_iota(jnp.int32, shape, dim)


def mark(condition):
    return jnp.where(condition, 1.0, 0.0).astype(BF16)


def split3(values):
    first = jnp.clip(values, -3.38e38, 3.38e38).astype(BF16)
    rest = values - first.astype(F32)
    second = rest.astype(BF16)
    third = (rest - second.astype(F32)).astype(BF16)
    return first, second, third


def kernel(
    peers,
    slabs,
    cap,
    probe_hbm,
    kappa_hbm,
    theta_space_hbm,
    theta_time_hbm,
    diag_hbm,
    off_hbm,
    cols_hbm,
    needs_hbm,
    cov_hbm,
    owner_hbm,
    cell_hbm,
    coef_hbm,
    sol_ref,
    grads_ref,
    probe,
    kappa,
    theta_space,
    theta_time,
    diag,
    off,
    cols,
    needs,
    cov,
    owner,
    cell,
    coef,
    slots,
    covt,
    onehot,
    send_obs,
    recv_obs,
    masks,
    counted,
    comb,
    field,
    first_low,
    first_high,
    time_low,
    time_high,
    send_up,
    send_down,
    send_left,
    send_right,
    product,
    residual,
    edges_out,
    edges_in,
    cross_out,
    cross_in,
    local_diag,
    step,
    needs_out,
    needs_in,
    picks,
    grads_out,
    grads_in,
    load_sem,
    obs_send_sem,
    obs_recv_sem,
    needs_send_sem,
    needs_recv_sem,
    space_send_sem,
    space_recv_sem,
    time_send_sem,
    time_recv_sem,
    edges_send_sem,
    edges_recv_sem,
    cross_send_sem,
    cross_recv_sem,
    grads_send_sem,
    grads_recv_sem,
):
    me = lax.axis_index("space")
    slab = lax.axis_index("tm")
    left = lax.rem(slab + slabs - 1, slabs)
    right = lax.rem(slab + 1, slabs)
    down = lax.rem(me + peers - 1, peers)
    up = lax.rem(me + 1, peers)
    has_down, has_up = me > 0, me < peers - 1
    has_left, has_right = slab > 0, slab < slabs - 1

    pairs = (
        (owner_hbm, owner),
        (cov_hbm, cov),
        (cell_hbm, cell),
        (needs_hbm, needs),
        (probe_hbm, probe),
        (kappa_hbm, kappa),
        (theta_space_hbm, theta_space),
        (theta_time_hbm, theta_time),
        (diag_hbm, diag),
        (off_hbm, off),
        (cols_hbm, cols),
        (coef_hbm, coef),
    )
    loads = [
        pltpu.make_async_copy(src, dst, load_sem.at[i]) for i, (src, dst) in enumerate(pairs)
    ]
    for load in loads:
        load.start()

    barrier = pltpu.get_barrier_semaphore()

    def greet(k, carry):
        pl.semaphore_signal(
            barrier, inc=1, device_id=(lax.rem(me + k, peers), slab), device_id_type=MESH
        )
        return carry

    lax.fori_loop(1, peers, greet, 0)
    for other in (left, right):
        pl.semaphore_signal(barrier, inc=1, device_id=(me, other), device_id_type=MESH)

    loads[0].wait()
    owner_cols = jnp.transpose(owner[...].astype(F32))
    lanes = iota((BLOCK, BLOCK), 1)
    below = mark(iota((BLOCK, BLOCK), 1) < iota((BLOCK, BLOCK), 0))
    seen = jnp.zeros((1, BLOCK), F32)
    for c in range(OBS_DEV // BLOCK):
        owner_col = owner_cols[:, c : c + 1].astype(jnp.int32)
        hit = owner_col == lanes
        hits = mark(hit)
        before = dot(below, hits) + seen
        rank = jnp.sum(jnp.where(hit, before, 0.0), axis=1, keepdims=True)
        seen = seen + jnp.sum(hits.astype(F32), axis=0, keepdims=True)
        slot = owner_col * cap + rank.astype(jnp.int32)
        slots[c * BLOCK : (c + 1) * BLOCK, :] = jnp.broadcast_to(slot, (BLOCK, BLOCK))

    loads[1].wait()
    loads[2].wait()
    sub = iota((16, BLOCK), 0)
    for c in range(OBS_DEV // BLOCK):
        part = slice(c * BLOCK, (c + 1) * BLOCK)
        covt[:NCOV, part] = jnp.transpose(cov[part, :])
        row = jnp.broadcast_to(cell[c : c + 1, :], (16, BLOCK))
        extra = jnp.where(
            sub == 0, row // 64, jnp.where(sub == 1, row % 64, jnp.where(sub == 2, 1, 0))
        )
        covt[NCOV:, part] = extra.astype(F32).astype(BF16)

    def compact(target):
        for c in range(OBS_DEV // BLOCK):
            part = slice(c * BLOCK, (c + 1) * BLOCK)
            place = slots[part, :] - target * cap
            for h in range(0, cap, BLOCK):
                onehot[part, h : h + BLOCK] = mark(place == lanes + h)
        return dot(covt[...], onehot[...]).astype(BF16)

    for i in (8, 9, 10):
        loads[i].wait()

    def combine(i, carry):
        b = i // NB_DEV
        rows = pl.ds(pl.multiple_of((i % NB_DEV) * 16, 16), 16)
        parts = [off[b, k, rows, :].astype(F32) for k in range(NB_DEV)]
        own = diag[b, rows, :].astype(F32)
        columns = [cols[b, k] for k in range(NB_DEV)]
        place = pl.ds(pl.multiple_of(i * 16, 16), 16)
        for m in range(WIDTH // BLOCK):
            total = jnp.zeros((16, BLOCK), F32)
            for k in range(NB_DEV):
                total = total + jnp.where(columns[k] == m, 1.0, 0.0) * parts[k]
            if m < NB_DEV:
                total = total + jnp.where(b == m, 1.0, 0.0) * own
            comb[place, m * BLOCK : (m + 1) * BLOCK] = total.astype(BF16)
        return carry

    lax.fori_loop(0, NODES_DEV // 16, combine, 0)

    pl.semaphore_wait(barrier, peers + 1)

    loads[3].wait()
    sub8 = iota((8, COLS), 0)
    listed = jnp.zeros((8, COLS), jnp.int32)
    for i in range(2 * HALO_B):
        listed = jnp.where(sub8 == i, needs[i], listed)
    needs_out[...] = listed

    def needs_copy(side, target):
        return pltpu.make_async_remote_copy(
            src_ref=needs_out,
            dst_ref=needs_in.at[side],
            send_sem=needs_send_sem.at[side],
            recv_sem=needs_recv_sem.at[side],
            device_id=(target, slab),
            device_id_type=MESH,
        )

    needs_copies = (needs_copy(0, up), needs_copy(1, down))
    for copy in needs_copies:
        copy.start()

    for i in range(4, 8):
        loads[i].wait()
    sub_e = iota((8, BLOCK), 0)
    ends = (theta_space[T_DEV - 1], theta_time[T_DEV - 1], theta_space[0], theta_time[0])
    scales = jnp.ones((8, BLOCK), F32)
    for i, value in enumerate(ends):
        scales = jnp.where(sub_e == i, value, scales)
    edges_out[...] = scales

    def beside(sends, receives, src, dst, send_sem, recv_sem, target):
        copy = pltpu.make_async_remote_copy(
            src_ref=src,
            dst_ref=dst,
            send_sem=send_sem,
            recv_sem=recv_sem,
            device_id=(me, target),
            device_id_type=MESH,
        )
        return sends, receives, copy

    def both_ways(src_right, src_left, dst_low, dst_high, send_sems, recv_sems):
        return (
            beside(has_right, has_left, src_right, dst_low, send_sems[0], recv_sems[0], right),
            beside(has_left, has_right, src_left, dst_high, send_sems[1], recv_sems[1], left),
        )

    def pair(sems, *index):
        return [sems.at[*index, which] for which in range(2)]

    edge_copies = both_ways(
        edges_out, edges_out, edges_in.at[0], edges_in.at[1], pair(edges_send_sem), pair(edges_recv_sem)
    )

    def start_copies(copies):
        for sends, _, copy in copies:
            pl.when(sends)(copy.start)

    def wait_arrivals(copies):
        for _, receives, copy in copies:
            pl.when(receives)(copy.wait_recv)

    def wait_departures(copies):
        for sends, _, copy in copies:
            pl.when(sends)(copy.wait_send)

    start_copies(edge_copies)

    def obs_copy(k, target):
        return pltpu.make_async_remote_copy(
            src_ref=send_obs.at[k],
            dst_ref=recv_obs.at[k],
            send_sem=obs_send_sem.at[k],
            recv_sem=obs_recv_sem.at[k],
            device_id=(target, slab),
            device_id_type=MESH,
        )

    far = peers // 4

    def in_turn(j):
        kind = lax.rem(j, 3)
        return far * (2 - kind + 3 * (kind // 2)) + j // 3

    def send(k, carry):
        target = lax.rem(me + k, peers)
        send_obs[k] = compact(target)
        obs_copy(k, target).start()
        return carry

    lax.fori_loop(0, 3 * far, lambda j, carry: send(in_turn(j), carry), 0)
    lax.fori_loop(1, far, send, 0)
    recv_obs[0] = compact(me)

    col_time = iota((1, COLS), 1) // PROBES
    scale_space = jnp.zeros((1, COLS), F32)
    scale_time = jnp.zeros((1, COLS), F32)
    for t in range(T_DEV):
        scale_space = jnp.where(col_time == t, theta_space[t], scale_space)
        scale_time = jnp.where(col_time == t, theta_time[t], scale_time)
    kappa_cols = jnp.transpose(kappa[...])
    eye = iota((BLOCK, BLOCK), 0) == iota((BLOCK, BLOCK), 1)
    sdiag_cols = []
    for b in range(NB_DEV):
        part = slice(b * BLOCK, (b + 1) * BLOCK)
        sdiag = jnp.sum(jnp.where(eye, diag[b].astype(F32), 0.0), axis=1, keepdims=True)
        sdiag_cols.append(sdiag)
        kappa_col = kappa_cols[:, b : b + 1]
        base = scale_space * sdiag + 2.0 * scale_time + kappa_col
        step[part, :] = base
        local_diag[part, :] = jnp.broadcast_to(kappa_col, (BLOCK, COLS))
        start = probe[part, :].astype(F32) / base
        sol_ref[part, :] = start
        field[0, part, :] = (RELAX * start).astype(BF16)

    for e in range(EXCHANGES):

        @pl.when(jnp.logical_not(has_down))
        def _():
            field[e, NODES_DEV : NODES_DEV + HALO_ROWS, :] = jnp.zeros((HALO_ROWS, COLS), BF16)

        @pl.when(jnp.logical_not(has_up))
        def _():
            field[e, NODES_DEV + HALO_ROWS :, :] = jnp.zeros((HALO_ROWS, COLS), BF16)

    for there, side, first, later in ((has_left, 0, first_low, time_low), (has_right, 1, first_high, time_high)):

        @pl.when(jnp.logical_not(there))
        def _():
            first[...] = jnp.zeros_like(first)
            later[...] = jnp.zeros_like(later)
            edges_in[side] = jnp.ones((8, BLOCK), F32)
            cross_in[side] = jnp.zeros((8, BLOCK), F32)

    for copy in needs_copies:
        copy.wait()
    for i in range(HALO_B):
        for b in range(NB_DEV):
            for side, row in ((1, i), (0, HALO_B + i)):
                picks[side, i, b] = mark(needs_in[side, row : row + 1, :] == b)

    lower_half = lanes < PROBES

    def pack_last(values):
        return jnp.where(
            lower_half, pltpu.roll(values[:BLOCK, BLOCK:], PROBES, 1), values[BLOCK:, BLOCK:]
        )

    def pack_first(values):
        return jnp.where(
            lower_half, values[:BLOCK, :BLOCK], pltpu.roll(values[BLOCK:, :BLOCK], PROBES, 1)
        )

    def time_copies(e, c):
        lows, highs = (first_low, first_high) if e == 0 else (time_low.at[e], time_high.at[e])
        return both_ways(
            send_right.at[e, c],
            send_left.at[e, c],
            lows.at[c],
            highs.at[c],
            pair(time_send_sem, e, c),
            pair(time_recv_sem, e, c),
        )

    def start_time(e, c, values):
        send_right[e, c] = pack_last(values).astype(BF16)
        send_left[e, c] = pack_first(values).astype(BF16)
        start_copies(time_copies(e, c))

    def space_copies(e):
        copies = []
        for which, sends, receives, src, offset, target in (
            (0, has_up, has_down, send_up, 0, up),
            (1, has_down, has_up, send_down, HALO_ROWS, down),
        ):
            copy = pltpu.make_async_remote_copy(
                src_ref=src.at[e],
                dst_ref=field.at[e, pl.ds(NODES_DEV + offset, HALO_ROWS)],
                send_sem=space_send_sem.at[e, which],
                recv_sem=space_recv_sem.at[e, which],
                device_id=(target, slab),
                device_id_type=MESH,
            )
            copies.append((sends, receives, copy))
        return copies

    def start_space(e):
        for i in range(HALO_B):
            part = slice(i * BLOCK, (i + 1) * BLOCK)
            for side, staged in ((1, send_up), (0, send_down)):
                chosen = picks[side, i, 0] * field[e, :BLOCK, :]
                for b in range(1, NB_DEV):
                    chosen = chosen + picks[side, i, b] * field[e, b * BLOCK : (b + 1) * BLOCK, :]
                staged[e, part, :] = chosen
        start_copies(space_copies(e))

    start_space(0)
    for c in range(CHUNKS):
        start_time(0, c, probe[c * CHUNK : (c + 1) * CHUNK, :].astype(F32))

    row_t, lane_t = iota((COLS, COLS), 0), iota((COLS, COLS), 1)
    inner = jnp.where(
        row_t == lane_t, 2.0, jnp.where(jnp.abs(row_t - lane_t) == PROBES, -1.0, 0.0)
    ).astype(BF16)
    def own_product(e):
        product[...] = dot(comb[:, :NODES_DEV], field[e, :NODES_DEV, :])

    def both(e, part):
        space = product[part, :] + dot(comb[part, NODES_DEV:], field[e, NODES_DEV:, :])
        return space, dot(field[e, part, :], inner)

    def parts():
        for c in range(CHUNKS):
            yield c, slice(c * CHUNK, (c + 1) * CHUNK)

    def inner_residual(e):
        for _, part in parts():
            space, time = both(e, part)
            applied = (
                scale_space * space
                + scale_time * time
                + local_diag[part, :] * field[e, part, :].astype(F32)
            )
            residual[part, :] = probe[part, :].astype(F32) - applied

    def update(e, c, part):
        low, high = time_low[e, c].astype(F32), time_high[e, c].astype(F32)
        first = scale_time[:, :BLOCK] * jnp.concatenate(
            [jnp.where(lower_half, low, 0.0), jnp.where(lower_half, pltpu.roll(low, PROBES, 1), 0.0)], axis=0
        )
        last = scale_time[:, BLOCK:] * jnp.concatenate(
            [jnp.where(lower_half, 0.0, pltpu.roll(high, PROBES, 1)), jnp.where(lower_half, 0.0, high)], axis=0
        )
        left_over = residual[part, :] + jnp.concatenate([first, last], axis=1)
        scaled = sol_ref[part, :] + step[part, :] * left_over
        sol_ref[part, :] = scaled
        solved = RELAX * scaled
        field[e + 1, part, :] = solved.astype(BF16)
        return solved

    own_product(0)

    loads[11].wait()
    counted[...] = jnp.zeros((NODES_DEV, BLOCK), F32)
    row_w = iota((BLOCK, cap), 0)

    def weigh(k):
        digits = recv_obs[k, NCOV:, :].astype(F32)
        live = digits[2:3, :] > 0.5
        number = (digits[0:1, :] * 64.0 + digits[1:2, :]).astype(jnp.int32)
        node = jnp.where(live, number // T_DEV, -1)
        time = number % T_DEV
        rows = recv_obs[k, :NCOV, :]
        eta = jnp.zeros((1, cap), F32)
        for c in range(NODES_DEV // CHUNK):
            part = slice(c * CHUNK, (c + 1) * CHUNK)
            scores = dot(coef[part, :], rows)
            found = iota((CHUNK, cap), 0) + c * CHUNK == node
            eta = eta + jnp.sum(jnp.where(found, scores, 0.0), axis=0, keepdims=True)
            masks[part, :] = mark(found)
        weight = jnp.where(live, jnp.exp(eta), 0.0)
        pieces = [piece.astype(F32) for piece in split3(weight)]
        spread = jnp.zeros((BLOCK, cap), F32)
        for i, piece in enumerate(pieces):
            spread = jnp.where(row_w == time + i * T_DEV, piece, spread)
        counted[...] += lax.dot_general(
            masks[...], spread.astype(BF16), NT_DIMS, preferred_element_type=F32
        )

    weigh(0)

    def receive(k, carry):
        obs_copy(k, lax.rem(me + k, peers)).wait_recv()
        weigh(k)
        return carry

    lax.fori_loop(0, 3 * far, lambda j, carry: receive(in_turn(j), carry), 0)
    lax.fori_loop(1, far, receive, 0)

    spread_row, spread_col = iota((BLOCK, COLS), 0), iota((BLOCK, COLS), 1) // PROBES
    repeat = mark((spread_row < 3 * T_DEV) & (spread_row % T_DEV == spread_col))
    for _, part in parts():
        pieces = split3(counted[part, :])
        obs_diag = dot(pieces[0], repeat) + dot(pieces[1], repeat) + dot(pieces[2], repeat)
        local_diag[part, :] = local_diag[part, :] + obs_diag
        step[part, :] = 1.0 / (step[part, :] + obs_diag)

    wait_arrivals(edge_copies)
    for c in range(CHUNKS):
        wait_arrivals(time_copies(0, c))
        lo, hi = 2 * c, 2 * c + 1
        sdiag = jnp.where(lower_half, sdiag_cols[lo], sdiag_cols[hi])
        nugget = jnp.where(lower_half, kappa_cols[:, lo : lo + 1], kappa_cols[:, hi : hi + 1])
        for side, row, first, later in ((0, 0, first_low, time_low), (1, 2, first_high, time_high)):
            base = edges_in[side, row : row + 1, :] * sdiag + 2.0 * edges_in[side, row + 1 : row + 2, :] + nugget
            later[0, c] = (RELAX * (first[c].astype(F32) / base)).astype(BF16)

    crossed = [jnp.zeros((1, BLOCK), F32), jnp.zeros((1, BLOCK), F32)]
    for e in range(ITERS):
        wait_arrivals(space_copies(e))
        inner_residual(e)
        for c, part in parts():
            if e > 0:
                wait_arrivals(time_copies(e, c))
            solved = update(e, c, part)
            if e < ITERS - 1:
                start_time(e + 1, c, solved)
            else:
                rounded = solved.astype(BF16).astype(F32)
                for i, packed, there in ((0, pack_last(rounded), first_high), (1, pack_first(rounded), first_low)):
                    terms = packed * there[c].astype(F32)
                    crossed[i] = crossed[i] + jnp.sum(terms, axis=0, keepdims=True)
        start_space(e + 1)
        if e < ITERS - 1:
            own_product(e + 1)

    for i in range(2):
        cross_out[i] = jnp.broadcast_to(crossed[i], (8, BLOCK))
    cross_copies = both_ways(
        cross_out.at[0],
        cross_out.at[1],
        cross_in.at[0],
        cross_in.at[1],
        pair(cross_send_sem),
        pair(cross_recv_sem),
    )
    start_copies(cross_copies)
    own_product(ITERS)
    wait_arrivals(space_copies(ITERS))
    sums = [jnp.zeros((1, COLS), F32), jnp.zeros((1, COLS), F32)]
    for _, part in parts():
        values = probe[part, :].astype(F32)
        for i, term in enumerate(both(ITERS, part)):
            sums[i] = sums[i] + jnp.sum(values * term, axis=0, keepdims=True)
    wait_arrivals(cross_copies)
    folded = [cross_in[i] + pltpu.roll(cross_in[i], PROBES, 1) for i in range(2)]
    low8 = iota((8, BLOCK), 1) < PROBES
    owed = jnp.concatenate([jnp.where(low8, folded[0], 0.0), jnp.where(low8, 0.0, folded[1])], axis=1)
    sums[1] = sums[1] - owed[0:1, :]
    grads_out[...] = jnp.where(sub8 == 0, sums[0], jnp.where(sub8 == 1, sums[1], 0.0))
    grads_in[me] = grads_out[...]

    def grads_copy(k):
        target = lax.rem(me + k, peers)
        return pltpu.make_async_remote_copy(
            src_ref=grads_out,
            dst_ref=grads_in.at[me],
            send_sem=grads_send_sem.at[k],
            recv_sem=grads_recv_sem.at[k],
            device_id=(target, slab),
            device_id_type=MESH,
        )

    def grads_send(k, carry):
        grads_copy(k).start()
        return carry

    lax.fori_loop(1, peers, grads_send, 0)

    def finish(k, carry):
        grads_copy(k).wait()
        obs_copy(k, lax.rem(me + k, peers)).wait_send()
        return carry

    lax.fori_loop(1, peers, finish, 0)
    wait_departures(edge_copies)
    wait_departures(cross_copies)
    for e in range(EXCHANGES):
        wait_departures(space_copies(e))
        if e < ITERS:
            for c in range(CHUNKS):
                wait_departures(time_copies(e, c))
    total = grads_in[0]
    for s in range(1, peers):
        total = total + grads_in[s]
    grads_ref[...] = total[0:2, :]


def shards(
    probe_field,
    kappa,
    theta_space,
    theta_time,
    diag_blocks,
    off_blocks,
    block_cols,
    halo_needs,
    covariates,
    obs_owner,
    obs_cell,
    svc_coef,
):
    peers = lax.axis_size("space")
    slabs = lax.axis_size("tm")
    cap = 2 * OBS_DEV // peers
    vmem = pl.BlockSpec(memory_space=pltpu.VMEM)
    dma = pltpu.SemaphoreType.DMA
    scaled, totals = pl.pallas_call(
        functools.partial(kernel, peers, slabs, cap),
        out_shape=(
            jax.ShapeDtypeStruct((NODES_DEV, COLS), F32),
            jax.ShapeDtypeStruct((2, COLS), F32),
        ),
        in_specs=[pl.BlockSpec(memory_space=pltpu.HBM)] * 12,
        out_specs=(vmem, vmem),
        scratch_shapes=[
            pltpu.VMEM((NODES_DEV, COLS), BF16),
            pltpu.VMEM((NB_DEV, BLOCK), F32),
            pltpu.SMEM((T_DEV,), F32),
            pltpu.SMEM((T_DEV,), F32),
            pltpu.VMEM((NB_DEV, BLOCK, BLOCK), BF16),
            pltpu.VMEM((NB_DEV, NB_DEV, BLOCK, BLOCK), BF16),
            pltpu.SMEM((NB_DEV, NB_DEV), jnp.int32),
            pltpu.SMEM((2 * HALO_B,), jnp.int32),
            pltpu.VMEM((OBS_DEV, NCOV), BF16),
            pltpu.VMEM((OBS_DEV // BLOCK, BLOCK), jnp.int32),
            pltpu.VMEM((OBS_DEV // BLOCK, BLOCK), jnp.int32),
            pltpu.VMEM((NODES_DEV, NCOV), BF16),
            pltpu.VMEM((OBS_DEV, BLOCK), jnp.int32),
            pltpu.VMEM((ROWS, OBS_DEV), BF16),
            pltpu.VMEM((OBS_DEV, cap), BF16),
            pltpu.VMEM((peers, ROWS, cap), BF16),
            pltpu.VMEM((peers, ROWS, cap), BF16),
            pltpu.VMEM((NODES_DEV, cap), BF16),
            pltpu.VMEM((NODES_DEV, BLOCK), F32),
            pltpu.VMEM((NODES_DEV, WIDTH), BF16),
            pltpu.VMEM((EXCHANGES, WIDTH, COLS), BF16),
            pltpu.VMEM((CHUNKS, BLOCK, BLOCK), BF16),
            pltpu.VMEM((CHUNKS, BLOCK, BLOCK), BF16),
            pltpu.VMEM((ITERS, CHUNKS, BLOCK, BLOCK), BF16),
            pltpu.VMEM((ITERS, CHUNKS, BLOCK, BLOCK), BF16),
            pltpu.VMEM((EXCHANGES, HALO_ROWS, COLS), BF16),
            pltpu.VMEM((EXCHANGES, HALO_ROWS, COLS), BF16),
            pltpu.VMEM((ITERS, CHUNKS, BLOCK, BLOCK), BF16),
            pltpu.VMEM((ITERS, CHUNKS, BLOCK, BLOCK), BF16),
            pltpu.VMEM((NODES_DEV, COLS), F32),
            pltpu.VMEM((NODES_DEV, COLS), F32),
            pltpu.VMEM((8, BLOCK), F32),
            pltpu.VMEM((2, 8, BLOCK), F32),
            pltpu.VMEM((2, 8, BLOCK), F32),
            pltpu.VMEM((2, 8, BLOCK), F32),
            pltpu.VMEM((NODES_DEV, COLS), F32),
            pltpu.VMEM((NODES_DEV, COLS), F32),
            pltpu.VMEM((8, COLS), jnp.int32),
            pltpu.VMEM((2, 8, COLS), jnp.int32),
            pltpu.VMEM((2, HALO_B, NB_DEV, 1, COLS), BF16),
            pltpu.VMEM((8, COLS), F32),
            pltpu.VMEM((peers, 8, COLS), F32),
            dma((12,)),
            dma((peers,)),
            dma((peers,)),
            dma((2,)),
            dma((2,)),
            dma((EXCHANGES, 2)),
            dma((EXCHANGES, 2)),
            dma((ITERS, CHUNKS, 2)),
            dma((ITERS, CHUNKS, 2)),
            dma((2,)),
            dma((2,)),
            dma((2,)),
            dma((2,)),
            dma((peers,)),
            dma((peers,)),
        ],
        compiler_params=pltpu.CompilerParams(
            collective_id=0,
            has_side_effects=True,
            vmem_limit_bytes=60 * 1024 * 1024,
        ),
    )(
        probe_field,
        kappa.reshape(NB_DEV, BLOCK),
        theta_space,
        theta_time,
        diag_blocks,
        off_blocks,
        block_cols,
        halo_needs,
        covariates,
        obs_owner.reshape(OBS_DEV // BLOCK, BLOCK),
        obs_cell.reshape(OBS_DEV // BLOCK, BLOCK),
        svc_coef,
    )
    return RELAX * scaled, totals / (NODES_DEV * peers)


def solution(mesh):
    return jax.shard_map(
        shards,
        mesh=mesh,
        in_specs=(
            P("space", "tm"),
            P("space"),
            P("tm"),
            P("tm"),
            P("space", None, None),
            P("space", None, None, None),
            P("space", None),
            P("space"),
            P(("space", "tm"), None),
            P(("space", "tm"), None),
            P(("space", "tm")),
            P("space", None),
        ),
        out_specs=(P("space", "tm"), P(None, "tm")),
        check_vma=False,
    )
```

```python
import functools

import jax
import jax.numpy as jnp
from jax import lax
from jax.experimental import pallas as pl
from jax.experimental.pallas import tpu as pltpu
from jax.sharding import PartitionSpec as P

NB_DEV = 8
BLOCK = 128
HALO_B = 2
T_DEV = 4
PROBES = 64
NCOV = 256
OBS_DEV = 2048
ITERS = 4
NODES_DEV = 1024
COLS = T_DEV * PROBES
WIDTH = (NB_DEV + 2 * HALO_B) * BLOCK
HALO_ROWS = HALO_B * BLOCK
ROWS = NCOV + 16
EXCHANGES = ITERS + 1
CHUNK = 256
CHUNKS = NODES_DEV // CHUNK
GROUP = 4
HALF = NODES_DEV // 2
CELLS = NB_DEV * T_DEV

RELAX = 0.6
MESH = pl.DeviceIdType.MESH
F32 = jnp.float32
BF16 = jnp.bfloat16
NT_DIMS = (((1,), (1,)), ((), ()))


def dot(a, b):
    return jnp.dot(a, b, preferred_element_type=F32)


def iota(shape, dim):
    return lax.broadcasted_iota(jnp.int32, shape, dim)


def mark(condition):
    return jnp.where(condition, 1.0, 0.0).astype(BF16)


def split3(values):
    first = jnp.clip(values, -3.38e38, 3.38e38).astype(BF16)
    rest = values - first.astype(F32)
    second = rest.astype(BF16)
    third = (rest - second.astype(F32)).astype(BF16)
    return first, second, third


def kernel(
    peers,
    slabs,
    cap,
    probe_hbm,
    kappa_hbm,
    theta_space_hbm,
    theta_time_hbm,
    diag_hbm,
    off_hbm,
    cols_hbm,
    needs_hbm,
    cov_hbm,
    owner_hbm,
    cell_hbm,
    coef_hbm,
    sol_ref,
    grads_ref,
    probe,
    kappa,
    theta_space,
    theta_time,
    diag,
    off,
    cols,
    needs,
    cov,
    owner,
    cell,
    coef,
    slots,
    covt,
    onehot,
    send_obs,
    recv_obs,
    masks,
    counted,
    comb,
    field,
    first_low,
    first_high,
    time_low,
    time_high,
    send_up,
    send_down,
    send_left,
    send_right,
    product,
    residual,
    edges_out,
    edges_in,
    cross_out,
    cross_in,
    local_diag,
    step,
    needs_out,
    needs_in,
    picks,
    sums_out,
    sums_in,
    grads_out,
    grads_in,
    load_sem,
    obs_send_sem,
    obs_recv_sem,
    needs_send_sem,
    needs_recv_sem,
    space_send_sem,
    space_recv_sem,
    time_send_sem,
    time_recv_sem,
    edges_send_sem,
    edges_recv_sem,
    cross_send_sem,
    cross_recv_sem,
    grads_send_sem,
    grads_recv_sem,
    coef_send_sem,
    coef_recv_sem,
    sums_send_sem,
    sums_recv_sem,
):
    me = lax.axis_index("space")
    slab = lax.axis_index("tm")
    left = lax.rem(slab + slabs - 1, slabs)
    right = lax.rem(slab + 1, slabs)
    down = lax.rem(me + peers - 1, peers)
    up = lax.rem(me + 1, peers)
    depth = lax.rem(me // 2, 2)
    spot = (me // 4) * 2 + lax.rem(me, 2)
    spots = peers // 2
    partner = me + 2 - 4 * depth
    turn = lax.rem(slab, GROUP)
    across = slab - turn + lax.rem(turn + GROUP - 1 + 2 * depth, GROUP)
    has_down, has_up = me > 0, me < peers - 1
    has_left, has_right = slab > 0, slab < slabs - 1

    pairs = (
        (owner_hbm, owner),
        (cov_hbm, cov),
        (cell_hbm, cell),
        (needs_hbm, needs),
        (probe_hbm, probe),
        (kappa_hbm, kappa),
        (theta_space_hbm, theta_space),
        (theta_time_hbm, theta_time),
        (diag_hbm, diag),
        (off_hbm, off),
        (cols_hbm, cols),
        (coef_hbm, coef.at[0]),
    )
    loads = [
        pltpu.make_async_copy(src, dst, load_sem.at[i]) for i, (src, dst) in enumerate(pairs)
    ]
    for load in loads:
        load.start()

    barrier = pltpu.get_barrier_semaphore()

    def greet(k, carry):
        pl.semaphore_signal(
            barrier, inc=1, device_id=(lax.rem(me + k, peers), slab), device_id_type=MESH
        )
        return carry

    lax.fori_loop(1, peers, greet, 0)
    for target in ((me, left), (me, right), (partner, across)):
        pl.semaphore_signal(barrier, inc=1, device_id=target, device_id_type=MESH)

    loads[0].wait()
    owner_cols = jnp.transpose(owner[...].astype(F32))
    lanes = iota((BLOCK, BLOCK), 1)
    below = mark(iota((BLOCK, BLOCK), 1) < iota((BLOCK, BLOCK), 0))
    seen = jnp.zeros((1, BLOCK), F32)
    for c in range(OBS_DEV // BLOCK):
        owner_col = owner_cols[:, c : c + 1].astype(jnp.int32)
        hit = owner_col == lanes
        hits = mark(hit)
        before = dot(below, hits) + seen
        rank = jnp.sum(jnp.where(hit, before, 0.0), axis=1, keepdims=True)
        seen = seen + jnp.sum(hits.astype(F32), axis=0, keepdims=True)
        slot = owner_col * cap + rank.astype(jnp.int32)
        slots[c * BLOCK : (c + 1) * BLOCK, :] = jnp.broadcast_to(slot, (BLOCK, BLOCK))

    loads[1].wait()
    loads[2].wait()
    sub = iota((16, BLOCK), 0)
    for c in range(OBS_DEV // BLOCK):
        part = slice(c * BLOCK, (c + 1) * BLOCK)
        covt[:NCOV, part] = jnp.transpose(cov[part, :])
        row = jnp.broadcast_to(cell[c : c + 1, :], (16, BLOCK))
        extra = jnp.where(
            sub == 0, row // 64, jnp.where(sub == 1, row % 64, jnp.where(sub == 2, 1, 0))
        )
        covt[NCOV:, part] = extra.astype(F32).astype(BF16)

    def compact(target):
        for c in range(OBS_DEV // BLOCK):
            part = slice(c * BLOCK, (c + 1) * BLOCK)
            place = slots[part, :] - target * cap
            for h in range(0, cap, BLOCK):
                onehot[part, h : h + BLOCK] = mark(place == lanes + h)
        return dot(covt[...], onehot[...]).astype(BF16)

    pl.semaphore_wait(barrier, peers + 2)

    loads[3].wait()
    sub8 = iota((8, COLS), 0)
    listed = jnp.zeros((8, COLS), jnp.int32)
    for i in range(2 * HALO_B):
        listed = jnp.where(sub8 == i, needs[i], listed)
    needs_out[...] = listed

    def needs_copy(side, target):
        return pltpu.make_async_remote_copy(
            src_ref=needs_out,
            dst_ref=needs_in.at[side],
            send_sem=needs_send_sem.at[side],
            recv_sem=needs_recv_sem.at[side],
            device_id=(target, slab),
            device_id_type=MESH,
        )

    needs_copies = (needs_copy(0, up), needs_copy(1, down))
    for copy in needs_copies:
        copy.start()

    for i in range(4, 9):
        loads[i].wait()
    sub_e = iota((8, BLOCK), 0)
    ends = (theta_space[T_DEV - 1], theta_time[T_DEV - 1], theta_space[0], theta_time[0])
    scales = jnp.ones((8, BLOCK), F32)
    for i, value in enumerate(ends):
        scales = jnp.where(sub_e == i, value, scales)
    edges_out[...] = scales

    def beside(sends, receives, src, dst, send_sem, recv_sem, target):
        copy = pltpu.make_async_remote_copy(
            src_ref=src,
            dst_ref=dst,
            send_sem=send_sem,
            recv_sem=recv_sem,
            device_id=(me, target),
            device_id_type=MESH,
        )
        return sends, receives, copy

    def both_ways(src_right, src_left, dst_low, dst_high, send_sems, recv_sems):
        return (
            beside(has_right, has_left, src_right, dst_low, send_sems[0], recv_sems[0], right),
            beside(has_left, has_right, src_left, dst_high, send_sems[1], recv_sems[1], left),
        )

    def pair(sems, *index):
        return [sems.at[*index, which] for which in range(2)]

    edge_copies = both_ways(
        edges_out, edges_out, edges_in.at[0], edges_in.at[1], pair(edges_send_sem), pair(edges_recv_sem)
    )

    def start_copies(copies):
        for sends, _, copy in copies:
            pl.when(sends)(copy.start)

    def wait_arrivals(copies):
        for _, receives, copy in copies:
            pl.when(receives)(copy.wait_recv)

    def wait_departures(copies):
        for sends, _, copy in copies:
            pl.when(sends)(copy.wait_send)

    start_copies(edge_copies)

    loads[11].wait()
    coef_copies = []
    for i, target in enumerate((slab, across)):
        rows = pl.ds(i * HALF, HALF)
        coef_copies.append(
            pltpu.make_async_remote_copy(
                src_ref=coef.at[0, rows],
                dst_ref=coef.at[1, rows],
                send_sem=coef_send_sem.at[i],
                recv_sem=coef_recv_sem.at[i],
                device_id=(partner, target),
                device_id_type=MESH,
            )
        )
    for copy in coef_copies:
        copy.start()
    sums_copy = pltpu.make_async_remote_copy(
        src_ref=sums_out,
        dst_ref=sums_in.at[pl.ds(0, CELLS)],
        send_sem=sums_send_sem,
        recv_sem=sums_recv_sem,
        device_id=(partner, slab),
        device_id_type=MESH,
    )
    sums_in[CELLS:, :] = jnp.zeros((BLOCK - CELLS, BLOCK), F32)

    def obs_copy(k, target):
        return pltpu.make_async_remote_copy(
            src_ref=send_obs.at[k],
            dst_ref=recv_obs.at[k],
            send_sem=obs_send_sem.at[k],
            recv_sem=obs_recv_sem.at[k],
            device_id=(target, slab),
            device_id_type=MESH,
        )

    def place_of(i):
        other = lax.rem(spot + i // 2, spots)
        return (other // 2) * 4 + lax.rem(other, 2)

    def owner_of(i):
        return place_of(i) + 2 * lax.rem(depth + i, 2)

    def target_of(i):
        return place_of(i) + 2 * depth

    def send(i, carry):
        send_obs[i] = compact(owner_of(i))
        obs_copy(i, target_of(i)).start()
        return carry

    lax.fori_loop(2, peers, send, 0)
    for i in range(2):
        recv_obs[i] = compact(owner_of(i))

    col_time = iota((1, COLS), 1) // PROBES
    scale_space = jnp.zeros((1, COLS), F32)
    scale_time = jnp.zeros((1, COLS), F32)
    for t in range(T_DEV):
        scale_space = jnp.where(col_time == t, theta_space[t], scale_space)
        scale_time = jnp.where(col_time == t, theta_time[t], scale_time)
    kappa_cols = jnp.transpose(kappa[...])
    eye = iota((BLOCK, BLOCK), 0) == iota((BLOCK, BLOCK), 1)
    sdiag_cols = []
    for b in range(NB_DEV):
        part = slice(b * BLOCK, (b + 1) * BLOCK)
        sdiag = jnp.sum(jnp.where(eye, diag[b].astype(F32), 0.0), axis=1, keepdims=True)
        sdiag_cols.append(sdiag)
        kappa_col = kappa_cols[:, b : b + 1]
        base = scale_space * sdiag + 2.0 * scale_time + kappa_col
        step[part, :] = base
        local_diag[part, :] = jnp.broadcast_to(kappa_col, (BLOCK, COLS))
        start = RELAX * probe[part, :].astype(F32) / base
        sol_ref[part, :] = start
        field[0, part, :] = start.astype(BF16)

    for e in range(EXCHANGES):

        @pl.when(jnp.logical_not(has_down))
        def _():
            field[e, NODES_DEV : NODES_DEV + HALO_ROWS, :] = jnp.zeros((HALO_ROWS, COLS), BF16)

        @pl.when(jnp.logical_not(has_up))
        def _():
            field[e, NODES_DEV + HALO_ROWS :, :] = jnp.zeros((HALO_ROWS, COLS), BF16)

    for there, side, first, later in ((has_left, 0, first_low, time_low), (has_right, 1, first_high, time_high)):

        @pl.when(jnp.logical_not(there))
        def _():
            first[...] = jnp.zeros_like(first)
            later[...] = jnp.zeros_like(later)
            edges_in[side] = jnp.ones((8, BLOCK), F32)
            cross_in[side] = jnp.zeros((8, BLOCK), F32)

    for copy in needs_copies:
        copy.wait()
    for i in range(HALO_B):
        for b in range(NB_DEV):
            for side, row in ((1, i), (0, HALO_B + i)):
                picks[side, i, b] = mark(needs_in[side, row : row + 1, :] == b)

    lower_half = lanes < PROBES

    def pack_last(values):
        return jnp.where(
            lower_half, pltpu.roll(values[:BLOCK, BLOCK:], PROBES, 1), values[BLOCK:, BLOCK:]
        )

    def pack_first(values):
        return jnp.where(
            lower_half, values[:BLOCK, :BLOCK], pltpu.roll(values[BLOCK:, :BLOCK], PROBES, 1)
        )

    def time_copies(e, c):
        lows, highs = (first_low, first_high) if e == 0 else (time_low.at[e], time_high.at[e])
        return both_ways(
            send_right.at[e, c],
            send_left.at[e, c],
            lows.at[c],
            highs.at[c],
            pair(time_send_sem, e, c),
            pair(time_recv_sem, e, c),
        )

    def start_time(e, c, values):
        send_right[e, c] = pack_last(values).astype(BF16)
        send_left[e, c] = pack_first(values).astype(BF16)
        start_copies(time_copies(e, c))

    def space_copies(e):
        copies = []
        for which, sends, receives, src, offset, target in (
            (0, has_up, has_down, send_up, 0, up),
            (1, has_down, has_up, send_down, HALO_ROWS, down),
        ):
            copy = pltpu.make_async_remote_copy(
                src_ref=src.at[e],
                dst_ref=field.at[e, pl.ds(NODES_DEV + offset, HALO_ROWS)],
                send_sem=space_send_sem.at[e, which],
                recv_sem=space_recv_sem.at[e, which],
                device_id=(target, slab),
                device_id_type=MESH,
            )
            copies.append((sends, receives, copy))
        return copies

    def start_space(e):
        for i in range(HALO_B):
            part = slice(i * BLOCK, (i + 1) * BLOCK)
            for side, staged in ((1, send_up), (0, send_down)):
                chosen = picks[side, i, 0] * field[e, :BLOCK, :]
                for b in range(1, NB_DEV):
                    chosen = chosen + picks[side, i, b] * field[e, b * BLOCK : (b + 1) * BLOCK, :]
                staged[e, part, :] = chosen
        start_copies(space_copies(e))

    start_space(0)
    for c in range(CHUNKS):
        start_time(0, c, probe[c * CHUNK : (c + 1) * CHUNK, :].astype(F32))

    for i in (9, 10):
        loads[i].wait()

    def combine(i, carry):
        b = i // NB_DEV
        rows = pl.ds(pl.multiple_of((i % NB_DEV) * 16, 16), 16)
        parts = [off[b, k, rows, :].astype(F32) for k in range(NB_DEV)]
        own = diag[b, rows, :].astype(F32)
        columns = [cols[b, k] for k in range(NB_DEV)]
        place = pl.ds(pl.multiple_of(i * 16, 16), 16)
        for m in range(WIDTH // BLOCK):
            total = jnp.zeros((16, BLOCK), F32)
            for k in range(NB_DEV):
                total = total + jnp.where(columns[k] == m, 1.0, 0.0) * parts[k]
            if m < NB_DEV:
                total = total + jnp.where(b == m, 1.0, 0.0) * own
            comb[place, m * BLOCK : (m + 1) * BLOCK] = total.astype(BF16)
        return carry

    lax.fori_loop(0, NODES_DEV // 16, combine, 0)

    row_t, lane_t = iota((COLS, COLS), 0), iota((COLS, COLS), 1)
    inner = jnp.where(
        row_t == lane_t, 2.0, jnp.where(jnp.abs(row_t - lane_t) == PROBES, -1.0, 0.0)
    ).astype(BF16)
    def own_product(e):
        product[...] = dot(comb[:, :NODES_DEV], field[e, :NODES_DEV, :])

    def both(e, part):
        space = product[part, :] + dot(comb[part, NODES_DEV:], field[e, NODES_DEV:, :])
        return space, dot(field[e, part, :], inner)

    def parts():
        for c in range(CHUNKS):
            yield c, slice(c * CHUNK, (c + 1) * CHUNK)

    def inner_residual(e):
        for _, part in parts():
            space, time = both(e, part)
            applied = (
                scale_space * space
                + scale_time * time
                + local_diag[part, :] * field[e, part, :].astype(F32)
            )
            residual[part, :] = probe[part, :].astype(F32) - applied

    def update(e, c, part):
        low, high = time_low[e, c].astype(F32), time_high[e, c].astype(F32)
        first = scale_time[:, :BLOCK] * jnp.concatenate(
            [jnp.where(lower_half, low, 0.0), jnp.where(lower_half, pltpu.roll(low, PROBES, 1), 0.0)], axis=0
        )
        last = scale_time[:, BLOCK:] * jnp.concatenate(
            [jnp.where(lower_half, 0.0, pltpu.roll(high, PROBES, 1)), jnp.where(lower_half, 0.0, high)], axis=0
        )
        left_over = residual[part, :] + jnp.concatenate([first, last], axis=1)
        solved = sol_ref[part, :] + step[part, :] * left_over
        sol_ref[part, :] = solved
        field[e + 1, part, :] = solved.astype(BF16)
        return solved

    own_product(0)

    counted[...] = jnp.zeros_like(counted)
    for copy in coef_copies:
        copy.wait_recv()
    row_w = iota((BLOCK, cap), 0)

    def weigh(k):
        which = lax.rem(k, 2)
        digits = recv_obs[k, NCOV:, :].astype(F32)
        live = digits[2:3, :] > 0.5
        number = (digits[0:1, :] * 64.0 + digits[1:2, :]).astype(jnp.int32)
        node = jnp.where(live, number // T_DEV, -1)
        time = number % T_DEV
        rows = recv_obs[k, :NCOV, :]
        eta = jnp.zeros((1, cap), F32)
        for c in range(NODES_DEV // CHUNK):
            part = slice(c * CHUNK, (c + 1) * CHUNK)
            scores = dot(coef[which, part, :], rows)
            found = iota((CHUNK, cap), 0) + c * CHUNK == node
            eta = eta + jnp.sum(jnp.where(found, scores, 0.0), axis=0, keepdims=True)
            masks[part, :] = mark(found)
        weight = jnp.where(live, jnp.exp(eta), 0.0)
        pieces = [piece.astype(F32) for piece in split3(weight)]
        spread = jnp.zeros((BLOCK, cap), F32)
        for i, piece in enumerate(pieces):
            spread = jnp.where(row_w == time + i * T_DEV, piece, spread)
        counted[which] += lax.dot_general(
            masks[...], spread.astype(BF16), NT_DIMS, preferred_element_type=F32
        )

    weigh(0)
    weigh(1)

    def receive(k, carry):
        obs_copy(k, target_of(k)).wait_recv()
        weigh(k)
        return carry

    lax.fori_loop(2, peers, receive, 0)

    def pack_sums(which):
        packed = jnp.zeros((BLOCK, BLOCK), F32)
        for b in range(NB_DEV):
            held = counted[which, b * BLOCK : (b + 1) * BLOCK, :]
            held = held + pltpu.roll(held, BLOCK - T_DEV, 1) + pltpu.roll(held, BLOCK - 2 * T_DEV, 1)
            packed = jnp.where(lanes // T_DEV == b, pltpu.roll(held, b * T_DEV, 1), packed)
        return packed

    sums_out[...] = jnp.transpose(pack_sums(1))[:CELLS, :]
    sums_copy.start()
    own_sums = pack_sums(0)

    wait_arrivals(edge_copies)
    for c in range(CHUNKS):
        wait_arrivals(time_copies(0, c))
        lo, hi = 2 * c, 2 * c + 1
        sdiag = jnp.where(lower_half, sdiag_cols[lo], sdiag_cols[hi])
        nugget = jnp.where(lower_half, kappa_cols[:, lo : lo + 1], kappa_cols[:, hi : hi + 1])
        for side, row, first, later in ((0, 0, first_low, time_low), (1, 2, first_high, time_high)):
            base = edges_in[side, row : row + 1, :] * sdiag + 2.0 * edges_in[side, row + 1 : row + 2, :] + nugget
            later[0, c] = (RELAX * first[c].astype(F32) / base).astype(BF16)

    sums_copy.wait_recv()
    pieces = split3(own_sums + jnp.transpose(sums_in[...]))
    cell_row, cell_col = iota((BLOCK, COLS), 0), iota((BLOCK, COLS), 1) // PROBES
    for b in range(NB_DEV):
        part = slice(b * BLOCK, (b + 1) * BLOCK)
        repeat = mark(cell_row == b * T_DEV + cell_col)
        obs_diag = dot(pieces[0], repeat) + dot(pieces[1], repeat) + dot(pieces[2], repeat)
        local_diag[part, :] = local_diag[part, :] + obs_diag
        step[part, :] = RELAX / (step[part, :] + obs_diag)

    crossed = [jnp.zeros((1, BLOCK), F32), jnp.zeros((1, BLOCK), F32)]
    for e in range(ITERS):
        wait_arrivals(space_copies(e))
        inner_residual(e)
        for c, part in parts():
            if e > 0:
                wait_arrivals(time_copies(e, c))
            solved = update(e, c, part)
            if e < ITERS - 1:
                start_time(e + 1, c, solved)
            else:
                rounded = solved.astype(BF16).astype(F32)
                for i, packed, there in ((0, pack_last(rounded), first_high), (1, pack_first(rounded), first_low)):
                    terms = packed * there[c].astype(F32)
                    crossed[i] = crossed[i] + jnp.sum(terms, axis=0, keepdims=True)
        start_space(e + 1)
        if e < ITERS - 1:
            own_product(e + 1)

    for i in range(2):
        cross_out[i] = jnp.broadcast_to(crossed[i], (8, BLOCK))
    cross_copies = both_ways(
        cross_out.at[0],
        cross_out.at[1],
        cross_in.at[0],
        cross_in.at[1],
        pair(cross_send_sem),
        pair(cross_recv_sem),
    )
    start_copies(cross_copies)
    own_product(ITERS)
    wait_arrivals(space_copies(ITERS))
    sums = [jnp.zeros((1, COLS), F32), jnp.zeros((1, COLS), F32)]
    for _, part in parts():
        values = probe[part, :].astype(F32)
        for i, term in enumerate(both(ITERS, part)):
            sums[i] = sums[i] + jnp.sum(values * term, axis=0, keepdims=True)
    wait_arrivals(cross_copies)
    folded = [cross_in[i] + pltpu.roll(cross_in[i], PROBES, 1) for i in range(2)]
    low8 = iota((8, BLOCK), 1) < PROBES
    owed = jnp.concatenate([jnp.where(low8, folded[0], 0.0), jnp.where(low8, 0.0, folded[1])], axis=1)
    sums[1] = sums[1] - owed[0:1, :]
    grads_out[...] = jnp.where(sub8 == 0, sums[0], jnp.where(sub8 == 1, sums[1], 0.0))
    grads_in[me] = grads_out[...]

    def grads_copy(k):
        target = lax.rem(me + k, peers)
        return pltpu.make_async_remote_copy(
            src_ref=grads_out,
            dst_ref=grads_in.at[me],
            send_sem=grads_send_sem.at[k],
            recv_sem=grads_recv_sem.at[k],
            device_id=(target, slab),
            device_id_type=MESH,
        )

    def grads_send(k, carry):
        grads_copy(k).start()
        return carry

    lax.fori_loop(1, peers, grads_send, 0)

    def finish(k, carry):
        grads_copy(k).wait()
        return carry

    lax.fori_loop(1, peers, finish, 0)

    def sent(i, carry):
        obs_copy(i, target_of(i)).wait_send()
        return carry

    lax.fori_loop(2, peers, sent, 0)
    sums_copy.wait_send()
    for copy in coef_copies:
        copy.wait_send()
    wait_departures(edge_copies)
    wait_departures(cross_copies)
    for e in range(EXCHANGES):
        wait_departures(space_copies(e))
        if e < ITERS:
            for c in range(CHUNKS):
                wait_departures(time_copies(e, c))
    total = grads_in[0]
    for s in range(1, peers):
        total = total + grads_in[s]
    grads_ref[...] = total[0:2, :] / (NODES_DEV * peers)


def shards(
    probe_field,
    kappa,
    theta_space,
    theta_time,
    diag_blocks,
    off_blocks,
    block_cols,
    halo_needs,
    covariates,
    obs_owner,
    obs_cell,
    svc_coef,
):
    peers = lax.axis_size("space")
    slabs = lax.axis_size("tm")
    cap = 2 * OBS_DEV // peers
    vmem = pl.BlockSpec(memory_space=pltpu.VMEM)
    dma = pltpu.SemaphoreType.DMA
    return pl.pallas_call(
        functools.partial(kernel, peers, slabs, cap),
        out_shape=(
            jax.ShapeDtypeStruct((NODES_DEV, COLS), F32),
            jax.ShapeDtypeStruct((2, COLS), F32),
        ),
        in_specs=[pl.BlockSpec(memory_space=pltpu.HBM)] * 12,
        out_specs=(vmem, vmem),
        scratch_shapes=[
            pltpu.VMEM((NODES_DEV, COLS), BF16),
            pltpu.VMEM((NB_DEV, BLOCK), F32),
            pltpu.SMEM((T_DEV,), F32),
            pltpu.SMEM((T_DEV,), F32),
            pltpu.VMEM((NB_DEV, BLOCK, BLOCK), BF16),
            pltpu.VMEM((NB_DEV, NB_DEV, BLOCK, BLOCK), BF16),
            pltpu.SMEM((NB_DEV, NB_DEV), jnp.int32),
            pltpu.SMEM((2 * HALO_B,), jnp.int32),
            pltpu.VMEM((OBS_DEV, NCOV), BF16),
            pltpu.VMEM((OBS_DEV // BLOCK, BLOCK), jnp.int32),
            pltpu.VMEM((OBS_DEV // BLOCK, BLOCK), jnp.int32),
            pltpu.VMEM((2, NODES_DEV, NCOV), BF16),
            pltpu.VMEM((OBS_DEV, BLOCK), jnp.int32),
            pltpu.VMEM((ROWS, OBS_DEV), BF16),
            pltpu.VMEM((OBS_DEV, cap), BF16),
            pltpu.VMEM((peers, ROWS, cap), BF16),
            pltpu.VMEM((peers, ROWS, cap), BF16),
            pltpu.VMEM((NODES_DEV, cap), BF16),
            pltpu.VMEM((2, NODES_DEV, BLOCK), F32),
            pltpu.VMEM((NODES_DEV, WIDTH), BF16),
            pltpu.VMEM((EXCHANGES, WIDTH, COLS), BF16),
            pltpu.VMEM((CHUNKS, BLOCK, BLOCK), BF16),
            pltpu.VMEM((CHUNKS, BLOCK, BLOCK), BF16),
            pltpu.VMEM((ITERS, CHUNKS, BLOCK, BLOCK), BF16),
            pltpu.VMEM((ITERS, CHUNKS, BLOCK, BLOCK), BF16),
            pltpu.VMEM((EXCHANGES, HALO_ROWS, COLS), BF16),
            pltpu.VMEM((EXCHANGES, HALO_ROWS, COLS), BF16),
            pltpu.VMEM((ITERS, CHUNKS, BLOCK, BLOCK), BF16),
            pltpu.VMEM((ITERS, CHUNKS, BLOCK, BLOCK), BF16),
            pltpu.VMEM((NODES_DEV, COLS), F32),
            pltpu.VMEM((NODES_DEV, COLS), F32),
            pltpu.VMEM((8, BLOCK), F32),
            pltpu.VMEM((2, 8, BLOCK), F32),
            pltpu.VMEM((2, 8, BLOCK), F32),
            pltpu.VMEM((2, 8, BLOCK), F32),
            pltpu.VMEM((NODES_DEV, COLS), F32),
            pltpu.VMEM((NODES_DEV, COLS), F32),
            pltpu.VMEM((8, COLS), jnp.int32),
            pltpu.VMEM((2, 8, COLS), jnp.int32),
            pltpu.VMEM((2, HALO_B, NB_DEV, 1, COLS), BF16),
            pltpu.VMEM((CELLS, BLOCK), F32),
            pltpu.VMEM((BLOCK, BLOCK), F32),
            pltpu.VMEM((8, COLS), F32),
            pltpu.VMEM((peers, 8, COLS), F32),
            dma((12,)),
            dma((peers,)),
            dma((peers,)),
            dma((2,)),
            dma((2,)),
            dma((EXCHANGES, 2)),
            dma((EXCHANGES, 2)),
            dma((ITERS, CHUNKS, 2)),
            dma((ITERS, CHUNKS, 2)),
            dma((2,)),
            dma((2,)),
            dma((2,)),
            dma((2,)),
            dma((peers,)),
            dma((peers,)),
            dma((2,)),
            dma((2,)),
            dma,
            dma,
        ],
        compiler_params=pltpu.CompilerParams(
            collective_id=0,
            has_side_effects=True,
            vmem_limit_bytes=60 * 1024 * 1024,
        ),
    )(
        probe_field,
        kappa.reshape(NB_DEV, BLOCK),
        theta_space,
        theta_time,
        diag_blocks,
        off_blocks,
        block_cols,
        halo_needs,
        covariates,
        obs_owner.reshape(OBS_DEV // BLOCK, BLOCK),
        obs_cell.reshape(OBS_DEV // BLOCK, BLOCK),
        svc_coef,
    )


def solution(mesh):
    return jax.shard_map(
        shards,
        mesh=mesh,
        in_specs=(
            P("space", "tm"),
            P("space"),
            P("tm"),
            P("tm"),
            P("space", None, None),
            P("space", None, None, None),
            P("space", None),
            P("space"),
            P(("space", "tm"), None),
            P(("space", "tm"), None),
            P(("space", "tm")),
            P("space", None),
        ),
        out_specs=(P("space", "tm"), P(None, "tm")),
        check_vma=False,
    )
```
